128 devices in a mesh: seq: 16 (over x, z), tp: 4 (over y_lo, core), img: 2 (over y_hi).
Axes of the slice: x: 4, y: 4 (y_hi: 2, y_lo: 2; y = y_hi * 2 + y_lo), z: 4, core: 2. Of those that a mesh axis runs over, the one named last changes fastest.
Arguments:
- patches: bfloat16 [16, 1024, 1280], P('seq'), may hold values from -6 to 6
- patch_counts: int32 [16], P('seq'), may hold values from 64 to 1024, as said below
- image_offsets: int32 [16], P('seq'), may hold values from 0 to 8191, as said below
- vision_gain: float32 [1280], replicated, may hold values from 0.1 to 1.9
- vision_shift: float32 [1280], replicated, may hold values from -3 to 3
- vision_qkv: bfloat16 [1280, 3840], P(None, ('tp', 'img'))
- vision_qkv_bias: bfloat16 [3840], P(('tp', 'img')), may hold values from -3 to 3
- vision_proj: bfloat16 [1280, 1280], P(('tp', 'img')), may hold values from -0.15625 to 0.15625
- vision_proj_bias: float32 [1280], replicated, may hold values from -3 to 3
- merge_gain: float32 [1280], replicated, may hold values from 0.1 to 1.9
- merge_shift: float32 [1280], replicated, may hold values from -3 to 3
- merge_weight: bfloat16 [5120, 8192], P(None, ('tp', 'img')), may hold values from -0.078125 to 0.078125
- merge_bias: bfloat16 [8192], P(('tp', 'img')), may hold values from -3 to 3
- text_embed: bfloat16 [8192, 8192], P(('seq', 'img'), 'tp'), may hold values from -6 to 6
- norm_gain: bfloat16 [8192], replicated, may hold values from 0.099609375 to 1.8984375
- qkv_weight: bfloat16 [8192, 5120], P(('seq', 'img'), 'tp')
- qkv_bias: bfloat16 [5120], P('tp'), may hold values from -3 to 3
Outputs:
- attention_out: bfloat16 [8192, 4096], P(('seq', 'img'), 'tp')
The draws below stay inside these ranges and needn't reach their ends.
Inputs may be any that keep to these rules, and one draw needn't show every extreme that they name: `patch_counts`: each a multiple of 4; one image in every draw has all 1024 slots filled. The merged tokens of image s take the positions image_offsets[s] to image_offsets[s] + patch_counts[s] / 4 - 1, all within s * 512 to (s + 1) * 512 - 1.
All inputs are finite; a program needn't handle non-finite values.
Results may differ from the reference program's by a relative error of at most 0.0065.
Values may be sent and summed in bfloat16 or wider, within the bound.
A program may use at most 128 MiB of HBM per device.

```python
import jax
import jax.numpy as jnp
from jax import lax

D = 8192
HEADS = 32
KV = 4
HEAD = 128
VW = 1280
VHEADS = 16
PATCH_CAP = 1024
TOK_DEV = 256
GROUP = 8
VHEAD = 80
VCAP = 256
IMAGES = 16
SECTION = 512
TOKENS = 8192


def layout_draw(key):
    first_key, second_key, third_key, fourth_key = jax.random.split(key, 4)
    quarter = PATCH_CAP // 4
    octave = jax.random.randint(first_key, (IMAGES,), 0, 4)
    base_size = jnp.right_shift(jnp.full((IMAGES,), quarter, jnp.int32), octave.astype(jnp.int32))
    merged = base_size - jax.random.randint(second_key, (IMAGES,), 0, 1 + base_size // 2)
    largest = jax.random.randint(third_key, (), 0, IMAGES)
    merged = jnp.where(jnp.arange(IMAGES, dtype=jnp.int32) == largest, quarter, merged).astype(jnp.int32)
    free_room = SECTION - merged
    slack_rows = jax.random.randint(fourth_key, (IMAGES,), 0, free_room + 1)
    offsets = jnp.arange(IMAGES, dtype=jnp.int32) * SECTION + slack_rows.astype(jnp.int32)
    return ((4 * merged).astype(jnp.int32), offsets.astype(jnp.int32))


def draw_patch_counts(key, part):
    shared = layout_draw(key)
    return shared[0]


def draw_image_offsets(key, part):
    shared = layout_draw(key)
    return shared[1]


def draw_vision_qkv(key, part):
    key = jax.random.fold_in(key, 3)
    weight_key = jax.random.fold_in(key, 0)
    weights = jax.random.normal(weight_key, (VW, VHEADS, 3, VHEAD), jnp.float32) * VW ** (-0.5)
    return weights.reshape(VW, 3 * VW).astype(jnp.bfloat16)


def draw_qkv_weight(key, part):
    key = jax.random.fold_in(key, 5)
    weight_key = jax.random.fold_in(key, 0)
    weights = jax.random.normal(weight_key, (D, KV, GROUP + 2, HEAD), jnp.float32) * D ** (-0.5)
    return weights.reshape(D, KV * (GROUP + 2) * HEAD).astype(jnp.bfloat16)


def block_levels(own_key, extent, cuts, low, high):
    level, own = 1.0, jax.random.fold_in(own_key, 6)
    for position, parts in cuts:
        heights = jnp.exp(jax.random.uniform(jax.random.fold_in(own, position), (parts,), jnp.float32, low / len(cuts), high / len(cuts)))
        level = level * jnp.repeat(heights, extent[position] // parts).reshape([-1 if axis == position else 1 for axis in range(len(extent))])
    return level


def scatter_about(stream_key, shape, scale, limit, pieces=(), kind=jnp.bfloat16):
    entries = scale * jax.random.normal(stream_key, shape, jnp.float32)
    if pieces:
        entries = entries * block_levels(stream_key, shape, pieces, -0.22, 0.18)
    return jnp.clip(entries, -limit, limit).astype(kind)


def setup_inputs(seed: int = 0) -> dict:
    key_list = jax.random.split(jax.random.key(seed), 18)
    return {
        "patches": scatter_about(key_list[0], (IMAGES, PATCH_CAP, VW), 1.0, 6.0, ((0, 16),)),
        "patch_counts": draw_patch_counts(jax.random.fold_in(key_list[17], 71), 0),
        "image_offsets": draw_image_offsets(jax.random.fold_in(key_list[17], 71), 0),
        "vision_gain": jnp.clip(1.0 + 0.18 * jax.random.normal(key_list[3], (VW,), jnp.float32), 0.1, 1.9),
        "vision_shift": scatter_about(key_list[4], (VW,), 0.5, 3.0, (), jnp.float32),
        "vision_qkv": draw_vision_qkv(jax.random.fold_in(key_list[17], 71), 0),
        "vision_qkv_bias": scatter_about(key_list[6], (3 * VW,), 0.5, 3.0, ((0, 8),)),
        "vision_proj": scatter_about(key_list[7], (VW, VW), VW ** -0.5, 0.15625, ((0, 8),)),
        "vision_proj_bias": scatter_about(key_list[8], (VW,), 0.5, 3.0, (), jnp.float32),
        "merge_gain": jnp.clip(1.0 + 0.18 * jax.random.normal(key_list[9], (VW,), jnp.float32), 0.1, 1.9),
        "merge_shift": scatter_about(key_list[10], (VW,), 0.5, 3.0, (), jnp.float32),
        "merge_weight": scatter_about(key_list[11], (4 * VW, D), (4 * VW) ** -0.5, 0.078125, ((1, 8),)),
        "merge_bias": scatter_about(key_list[12], (D,), 0.5, 3.0, ((0, 8),)),
        "text_embed": scatter_about(key_list[13], (TOKENS, D), 1.0, 6.0, ((0, 32), (1, 4))),
        "norm_gain": jnp.clip(1.0 + 0.18 * jax.random.normal(key_list[14], (D,), jnp.float32), 0.099609375, 1.8984375).astype(jnp.bfloat16),
        "qkv_weight": draw_qkv_weight(jax.random.fold_in(key_list[17], 71), 0),
        "qkv_bias": scatter_about(key_list[16], (KV * (GROUP + 2) * HEAD,), 0.5, 3.0, ((0, 4),)),
    }


EPSILON = 1e-06
THETA = 1000000.0
MASKED = -1e+30

def layer_norm(source, scaling, shifting):
    average = lax.optimization_barrier(jnp.mean(source, axis=-1, keepdims=True))
    centred = source - average
    spread = lax.optimization_barrier(jnp.mean(centred * centred, axis=-1, keepdims=True))
    return centred * lax.rsqrt(spread + EPSILON) * scaling.astype(jnp.float32) + shifting.astype(jnp.float32)

def rotary(inputs, positions, head_width):
    halfway = head_width // 2
    frequency = jnp.power(jnp.float32(THETA), -(jnp.arange(halfway, dtype=jnp.float32) * 2.0) / head_width)
    angles = positions.astype(jnp.float32)[:, None] * frequency[None, :]
    angles = angles.reshape((angles.shape[0],) + (1,) * (inputs.ndim - 2) + (halfway,))
    cosine = jnp.cos(angles)
    sine_value = jnp.sin(angles)
    leading = inputs[..., :halfway]
    trailing = inputs[..., halfway:]
    return jnp.concatenate([leading * cosine - trailing * sine_value, trailing * cosine + leading * sine_value], axis=-1)

def vision_image(pixels, count, vision_gain, vision_shift, vision_qkv, vision_qkv_bias, vision_proj, vision_proj_bias, merge_gain, merge_shift, merge_weight, merge_bias):
    source = pixels.astype(jnp.float32)
    normed = layer_norm(source, vision_gain, vision_shift).astype(jnp.bfloat16)
    mixed = jnp.dot(normed, vision_qkv, preferred_element_type=jnp.float32) + vision_qkv_bias.astype(jnp.float32)
    mixed = lax.optimization_barrier(mixed.astype(jnp.bfloat16))
    mixed = mixed.reshape(PATCH_CAP, VHEADS, 3, VHEAD).astype(jnp.float32)
    scores = jnp.einsum('qhe,khe->hqk', mixed[:, :, 0], mixed[:, :, 1]) * VHEAD ** (-0.5)
    valid = jnp.arange(PATCH_CAP, dtype=jnp.int32) < count
    scores = jnp.where(valid[None, None, :], scores, MASKED)
    top_score = lax.optimization_barrier(jnp.max(scores, axis=-1, keepdims=True))
    raw = jnp.where(valid[None, None, :], jnp.exp(scores - top_score), 0.0)
    totals = lax.optimization_barrier(jnp.sum(raw, axis=-1))
    rounded = lax.optimization_barrier(raw.astype(jnp.bfloat16)).astype(jnp.float32)
    context = jnp.einsum('hqk,khe->qhe', rounded, mixed[:, :, 2]) / jnp.transpose(totals)[:, :, None]
    context = context.astype(jnp.bfloat16).reshape(PATCH_CAP, VW)
    resid = jnp.dot(context, vision_proj, preferred_element_type=jnp.float32) + vision_proj_bias.astype(jnp.float32) + source
    merge_in = layer_norm(resid, merge_gain, merge_shift).astype(jnp.bfloat16).reshape(VCAP, 4 * VW)
    merged = jnp.dot(merge_in, merge_weight, preferred_element_type=jnp.float32) + merge_bias.astype(jnp.float32)
    return merged.astype(jnp.bfloat16)

def reference(patches, patch_counts, image_offsets, vision_gain, vision_shift, vision_qkv, vision_qkv_bias, vision_proj, vision_proj_bias, merge_gain, merge_shift, merge_weight, merge_bias, text_embed, norm_gain, qkv_weight, qkv_bias):

    def one_image(items):
        return vision_image(items[0], items[1], vision_gain, vision_shift, vision_qkv, vision_qkv_bias, vision_proj, vision_proj_bias, merge_gain, merge_shift, merge_weight, merge_bias)
    vision_tokens = lax.map(one_image, (patches, patch_counts))
    sections = text_embed.reshape(IMAGES, SECTION, D)

    def place(items):
        section, tokens, count, offset, number = items
        start_row = number * SECTION
        padded = jnp.pad(tokens, ((SECTION, SECTION), (0, 0)))
        where_at = jnp.clip(start_row - offset + SECTION, 0, VCAP + SECTION)
        placed = lax.dynamic_slice_in_dim(padded, where_at, SECTION, 0)
        spots = start_row + jnp.arange(SECTION, dtype=jnp.int32)
        inside = (spots >= offset) & (spots < offset + count // 4)
        return jnp.where(inside[:, None], placed, section)
    numbers = jnp.arange(IMAGES, dtype=jnp.int32)
    hidden = lax.map(place, (sections, vision_tokens, patch_counts, image_offsets, numbers)).reshape(TOKENS, D)
    wide = hidden.astype(jnp.float32)
    normed = wide * lax.rsqrt(lax.optimization_barrier(jnp.mean(wide * wide, axis=-1, keepdims=True)) + EPSILON) * norm_gain.astype(jnp.float32)
    normed = normed.astype(jnp.bfloat16)
    projected = jnp.dot(normed, qkv_weight, preferred_element_type=jnp.float32) + qkv_bias.astype(jnp.float32)
    projected = projected.reshape(TOKENS, KV, GROUP + 2, HEAD)
    positions = jnp.arange(TOKENS, dtype=jnp.int32)
    queries = rotary(projected[:, :, :GROUP], positions, HEAD).astype(jnp.bfloat16)
    keys = rotary(projected[:, :, GROUP], positions, HEAD).astype(jnp.bfloat16)
    values = projected[:, :, GROUP + 1].astype(jnp.bfloat16)
    blocks = TOKENS // TOK_DEV

    def group_attend(items):
        group_queries, group_keys, group_values = items
        key_wide = group_keys.astype(jnp.float32)
        value_wide = group_values.astype(jnp.float32)

        def block_attend(number):
            rows = lax.dynamic_slice_in_dim(group_queries, number * TOK_DEV, TOK_DEV, 0).astype(jnp.float32)
            scores = jnp.einsum('qae,ke->aqk', rows, key_wide) * HEAD ** (-0.5)
            query_pos = number * TOK_DEV + jnp.arange(TOK_DEV, dtype=jnp.int32)
            allowed = positions[None, :] <= query_pos[:, None]
            scores = jnp.where(allowed[None], scores, MASKED)
            top_score = lax.optimization_barrier(jnp.max(scores, axis=-1, keepdims=True))
            raw = jnp.where(allowed[None], jnp.exp(scores - top_score), 0.0)
            totals = lax.optimization_barrier(jnp.sum(raw, axis=-1))
            rounded = lax.optimization_barrier(raw.astype(jnp.bfloat16)).astype(jnp.float32)
            context = jnp.einsum('aqk,ke->qae', rounded, value_wide)
            return context / jnp.transpose(totals)[:, :, None]
        outputs = lax.map(block_attend, jnp.arange(blocks, dtype=jnp.int32))
        return outputs.reshape(TOKENS, GROUP, HEAD)
    attended = lax.map(group_attend, (jnp.transpose(queries, (1, 0, 2, 3)), jnp.transpose(keys, (1, 0, 2)), jnp.transpose(values, (1, 0, 2))))
    return jnp.transpose(attended, (1, 0, 2, 3)).reshape(TOKENS, HEADS * HEAD).astype(jnp.bfloat16)
```

```python
import functools

import jax
import jax.numpy as jnp
from jax import lax
from jax.experimental import pallas as pl
from jax.experimental.pallas import tpu as pltpu
from jax.sharding import PartitionSpec as P

HEAD = 128
VW = 1280
PATCH_CAP = 1024
GROUP = 8
VHEAD = 80
SECTION = 512
HALF = 256
OWN_HEADS = 4

EPSILON = 1e-06
THETA = 1000000.0
MASKED = -1e30
LOG2E = 1.4426950408889634
MESH = pl.DeviceIdType.MESH


def layer_norm(source, scaling, shifting):
    average = jnp.mean(source, axis=-1, keepdims=True)
    centred = source - average
    spread = jnp.mean(centred * centred, axis=-1, keepdims=True)
    return centred * lax.rsqrt(spread + EPSILON) * scaling + shifting


def rotary(inputs, positions, head_width):
    halfway = head_width // 2
    frequency = jnp.power(
        jnp.float32(THETA), -(jnp.arange(halfway, dtype=jnp.float32) * 2.0) / head_width
    )
    angles = positions.astype(jnp.float32)[:, None] * frequency[None, :]
    angles = angles.reshape((angles.shape[0],) + (1,) * (inputs.ndim - 2) + (halfway,))
    cosine = jnp.cos(angles)
    sine_value = jnp.sin(angles)
    leading = inputs[..., :halfway]
    trailing = inputs[..., halfway:]
    return jnp.concatenate(
        [leading * cosine - trailing * sine_value, trailing * cosine + leading * sine_value],
        axis=-1,
    )


def attend_kernel(x_ref, out_ref, buf, ext, other, top, acc, send, recv):
    seq = lax.axis_index("seq")
    img = lax.axis_index("img")
    x = seq // 4
    z = seq % 4
    partner = {"img": 1 - img}

    def along_x(d):
        return {"seq": ((x + d) % 4) * 4 + z}

    def along_z(d):
        return {"seq": x * 4 + (z + d) % 4}

    peers = [partner] + [along_x(d) for d in (1, 2, 3)] + [along_z(d) for d in (1, 2, 3)]
    barrier = pltpu.get_barrier_semaphore()
    for peer in peers:
        pl.semaphore_signal(barrier, inc=1, device_id=peer, device_id_type=MESH)
    pl.semaphore_wait(barrier, len(peers))

    def copy(src, dst, number, peer):
        return pltpu.make_async_remote_copy(
            src_ref=src,
            dst_ref=dst,
            send_sem=send.at[number],
            recv_sem=recv.at[number],
            device_id=peer,
            device_id_type=MESH,
        )

    buf[img, x, z] = x_ref[:, OWN_HEADS * HEAD :]
    own = buf.at[img, x, z]
    swap = copy(own, own, 0, partner)
    swap.start()
    swap.wait()
    first, second = pl.ds(0, HALF), pl.ds(HALF, HALF)
    part_a = buf.at[:, x, z, first]
    part_b = buf.at[:, x, z, second]
    one = [copy(part_a, part_a, d, along_x(d)) for d in (1, 2, 3)]
    two = [copy(part_b, part_b, 3 + d, along_z(d)) for d in (1, 2, 3)]
    for c in one + two:
        c.start()
    for c in one:
        c.wait()
    part_c = buf.at[:, :, z, first]
    three = [copy(part_c, part_c, 6 + d, along_z(d)) for d in (1, 2, 3)]
    for c in three:
        c.start()
    for c in two:
        c.wait()
    part_d = buf.at[:, x, :, second]
    four = [copy(part_d, part_d, 9 + d, along_x(d)) for d in (1, 2, 3)]
    for c in four:
        c.start()

    top[...] = jnp.full_like(top, MASKED)
    acc[...] = jnp.zeros_like(acc)
    ones = jnp.ones((SECTION, HEAD), jnp.bfloat16)

    def block(half, rows, head, keys, values, mask):
        query = x_ref[rows, head * HEAD : (head + 1) * HEAD]
        scores = lax.dot_general(
            query, keys, (((1,), (1,)), ((), ())), preferred_element_type=jnp.float32
        )
        scores = scores * (HEAD ** (-0.5) * LOG2E)
        if mask is not None:
            scores = jnp.where(mask, scores, MASKED)
        old = top[half, head]
        new = jnp.maximum(old, jnp.max(scores, axis=-1, keepdims=True))
        factor = jnp.exp2(old - new)
        weights = jnp.exp2(scores - new[:, :1]).astype(jnp.bfloat16)
        product = jnp.dot(weights, values, preferred_element_type=jnp.float32)
        top[half, head] = new
        acc[half, head] = acc[half, head] * jnp.concatenate([factor, factor], axis=1) + product

    def diagonal(half):
        rows = pl.ds(half * HALF, HALF)
        keys = buf[0, x, z]
        values = jnp.concatenate([buf[1, x, z], ones], axis=1)
        row = lax.broadcasted_iota(jnp.int32, (HALF, SECTION), 0) + half * HALF
        col = lax.broadcasted_iota(jnp.int32, (HALF, SECTION), 1)
        mask = col <= row
        for head in range(OWN_HEADS):
            block(half, rows, head, keys, values, mask)

    def earlier(half, number):
        rows = pl.ds(half * HALF, HALF)
        keys = buf[0, number // 4, number % 4]
        values = jnp.concatenate([buf[1, number // 4, number % 4], ones], axis=1)
        for head in range(OWN_HEADS):
            block(half, rows, head, keys, values, None)

    def finish(half):
        parts = []
        for head in range(OWN_HEADS):
            total = acc[half, head]
            parts.append((total[:, :HEAD] / total[:, HEAD:]).astype(jnp.bfloat16))
        return jnp.concatenate(parts, axis=1)

    lax.fori_loop(0, 2, lambda half, c: (diagonal(half), c)[1], 0)
    for c in three + four:
        c.wait()

    def run(half):
        lax.fori_loop(0, seq, lambda number, c: (earlier(half, number), c)[1], 0)

    run(1 - img)
    other[...] = finish(1 - img)
    columns = pl.ds(pl.multiple_of(img * (OWN_HEADS * HEAD), OWN_HEADS * HEAD), OWN_HEADS * HEAD)
    back = copy(other, out_ref.at[:, columns], 13, partner)
    back.start()
    run(img)
    out_ref[:, columns] = finish(img)
    back.wait()


def attend(rows):
    return pl.pallas_call(
        attend_kernel,
        out_shape=jax.ShapeDtypeStruct((HALF, 2 * OWN_HEADS * HEAD), jnp.bfloat16),
        in_specs=[pl.BlockSpec(memory_space=pltpu.VMEM)],
        out_specs=pl.BlockSpec(memory_space=pltpu.VMEM),
        scratch_shapes=[
            pltpu.VMEM((2, 4, 4, SECTION, HEAD), jnp.bfloat16),
            pltpu.VMEM((8, HEAD), jnp.bfloat16),
            pltpu.VMEM((HALF, OWN_HEADS * HEAD), jnp.bfloat16),
            pltpu.VMEM((2, OWN_HEADS, HALF, HEAD), jnp.float32),
            pltpu.VMEM((2, OWN_HEADS, HALF, 2 * HEAD), jnp.float32),
            pltpu.SemaphoreType.DMA((14,)),
            pltpu.SemaphoreType.DMA((14,)),
        ],
        compiler_params=pltpu.CompilerParams(
            collective_id=0, has_side_effects=True, vmem_limit_bytes=40 * 1024 * 1024
        ),
    )(rows)


def vision(patches, count, vision_gain, vision_shift, vision_qkv, vision_qkv_bias, vision_proj,
           vision_proj_bias, merge_gain, merge_shift, merge_weight, merge_bias):
    source = patches[0].astype(jnp.float32)
    normed_patches = layer_norm(source, vision_gain, vision_shift).astype(jnp.bfloat16)
    local_heads = vision_qkv.shape[1] // (3 * VHEAD)
    mixed = jnp.dot(
        normed_patches, vision_qkv, preferred_element_type=jnp.float32
    ) + vision_qkv_bias.astype(jnp.float32)
    mixed = mixed.astype(jnp.bfloat16).reshape(PATCH_CAP, local_heads, 3, VHEAD)
    scores = jnp.einsum(
        "qhe,khe->hqk", mixed[:, :, 0], mixed[:, :, 1], preferred_element_type=jnp.float32
    )
    scores = scores * VHEAD ** (-0.5)
    valid = jnp.arange(PATCH_CAP, dtype=jnp.int32) < count
    scores = jnp.where(valid[None, None, :], scores, MASKED)
    top_score = jnp.max(scores, axis=-1, keepdims=True)
    raw = jnp.where(valid[None, None, :], jnp.exp(scores - top_score), 0.0)
    totals = jnp.sum(raw, axis=-1)
    context = jnp.einsum(
        "hqk,khe->qhe", raw.astype(jnp.bfloat16), mixed[:, :, 2], preferred_element_type=jnp.float32
    )
    context = (context / jnp.transpose(totals)[:, :, None]).astype(jnp.bfloat16)
    context = context.reshape(PATCH_CAP, local_heads * VHEAD)
    partial_proj = jnp.dot(context, vision_proj, preferred_element_type=jnp.float32)
    summed = lax.psum(partial_proj, ("tp", "img"))
    resid = summed + vision_proj_bias + source
    merge_rows = layer_norm(resid, merge_gain, merge_shift).astype(jnp.bfloat16)
    merge_in = merge_rows.reshape(PATCH_CAP // 4, 4 * VW)
    token_part = jnp.dot(
        merge_in, merge_weight, preferred_element_type=jnp.float32
    ) + merge_bias.astype(jnp.float32)
    return lax.all_gather(token_part.astype(jnp.bfloat16), ("tp", "img"), axis=1, tiled=True)


def on_device(
    patches, patch_counts, image_offsets, vision_gain, vision_shift, vision_qkv, vision_qkv_bias,
    vision_proj, vision_proj_bias, merge_gain, merge_shift, merge_weight, merge_bias, text_embed,
    norm_gain, qkv_weight, qkv_bias,
):
    count = patch_counts[0]
    offset = image_offsets[0]
    img = lax.axis_index("img")
    wide_q = OWN_HEADS * HEAD

    def halves(array):
        first = jnp.concatenate([array[:, :wide_q], array[:, 2 * wide_q : 2 * wide_q + HEAD]], axis=1)
        second = jnp.concatenate([array[:, wide_q : 2 * wide_q], array[:, 2 * wide_q + HEAD :]], axis=1)
        return jnp.stack([first, second])

    shared = lax.all_to_all(halves(qkv_weight), "img", 0, 0)
    weight = lax.all_gather(shared.reshape(-1, shared.shape[-1]), "seq", axis=0, tiled=True)
    bias = halves(qkv_bias[None])[img, 0]
    text = lax.all_gather(lax.all_gather(text_embed, "img", axis=0, tiled=True), "tp", axis=1, tiled=True)
    tokens = vision(
        patches, count, vision_gain, vision_shift, vision_qkv, vision_qkv_bias, vision_proj,
        vision_proj_bias, merge_gain, merge_shift, merge_weight, merge_bias,
    )
    my_start = lax.axis_index("seq") * SECTION
    padded = jnp.pad(tokens, ((SECTION, SECTION), (0, 0)))
    where_at = jnp.clip(my_start - offset + SECTION, 0, PATCH_CAP // 4 + SECTION)
    placed = lax.dynamic_slice_in_dim(padded, where_at, SECTION, 0)
    positions = my_start + jnp.arange(SECTION, dtype=jnp.int32)
    inside = (positions >= offset) & (positions < offset + count // 4)
    hidden = jnp.where(inside[:, None], placed, text)
    wide = hidden.astype(jnp.float32)
    normed = (
        wide
        * lax.rsqrt(jnp.mean(wide * wide, axis=-1, keepdims=True) + EPSILON)
        * norm_gain.astype(jnp.float32)
    ).astype(jnp.bfloat16)
    projected = jnp.dot(normed, weight, preferred_element_type=jnp.float32) + bias.astype(jnp.float32)
    heads = projected.reshape(SECTION, OWN_HEADS + 1, HEAD)
    turned = rotary(heads, positions, HEAD)
    last = jnp.where(img == 0, turned[:, OWN_HEADS:], heads[:, OWN_HEADS:])
    rows = jnp.concatenate([turned[:, :OWN_HEADS], last], axis=1).astype(jnp.bfloat16)
    return attend(rows.reshape(SECTION, (OWN_HEADS + 1) * HEAD))


def solution(mesh):
    placed = (
        P("seq", None, None),
        P("seq"),
        P("seq"),
        P(),
        P(),
        P(None, ("tp", "img")),
        P(("tp", "img")),
        P(("tp", "img"), None),
        P(),
        P(),
        P(),
        P(None, ("tp", "img")),
        P(("tp", "img")),
        P(("seq", "img"), "tp"),
        P(),
        P(("seq", "img"), "tp"),
        P("tp"),
    )
    return jax.shard_map(
        on_device, mesh=mesh, in_specs=placed, out_specs=P(("seq", "img"), "tp"), check_vma=False
    )
```

```python
import functools

import jax
import jax.numpy as jnp
from jax import lax
from jax.experimental import pallas as pl
from jax.experimental.pallas import tpu as pltpu
from jax.sharding import PartitionSpec as P

HEAD = 128
VW = 1280
PATCH_CAP = 1024
GROUP = 8
VHEAD = 80
SECTION = 512
HALF = 256
OWN_HEADS = 4

EPSILON = 1e-06
THETA = 1000000.0
MASKED = -1e30
LOG2E = 1.4426950408889634
MESH = pl.DeviceIdType.MESH


def rotary(inputs, positions, head_width):
    halfway = head_width // 2
    frequency = jnp.power(
        jnp.float32(THETA), -(jnp.arange(halfway, dtype=jnp.float32) * 2.0) / head_width
    )
    angles = positions.astype(jnp.float32)[:, None] * frequency[None, :]
    angles = angles.reshape((angles.shape[0],) + (1,) * (inputs.ndim - 2) + (halfway,))
    cosine = jnp.cos(angles)
    sine_value = jnp.sin(angles)
    leading = inputs[..., :halfway]
    trailing = inputs[..., halfway:]
    return jnp.concatenate(
        [leading * cosine - trailing * sine_value, trailing * cosine + leading * sine_value],
        axis=-1,
    )


def attend_kernel(x_ref, out_ref, buf, ext, other, top, acc, send, recv):
    seq = lax.axis_index("seq")
    img = lax.axis_index("img")
    x = seq // 4
    z = seq % 4
    partner = {"img": 1 - img}

    def along_x(d):
        return {"seq": ((x + d) % 4) * 4 + z}

    def along_z(d):
        return {"seq": x * 4 + (z + d) % 4}

    peers = [partner] + [along_x(d) for d in (1, 2, 3)] + [along_z(d) for d in (1, 2, 3)]
    barrier = pltpu.get_barrier_semaphore()
    for peer in peers:
        pl.semaphore_signal(barrier, inc=1, device_id=peer, device_id_type=MESH)
    pl.semaphore_wait(barrier, len(peers))

    def copy(src, dst, number, peer):
        return pltpu.make_async_remote_copy(
            src_ref=src,
            dst_ref=dst,
            send_sem=send.at[number],
            recv_sem=recv.at[number],
            device_id=peer,
            device_id_type=MESH,
        )

    buf[img, x, z] = x_ref[:, OWN_HEADS * HEAD :]
    own = buf.at[img, x, z]
    swap = copy(own, own, 0, partner)
    swap.start()
    swap.wait()
    first, second = pl.ds(0, HALF), pl.ds(HALF, HALF)
    part_a = buf.at[:, x, z, first]
    part_b = buf.at[:, x, z, second]
    one = [copy(part_a, part_a, d, along_x(d)) for d in (1, 2, 3)]
    two = [copy(part_b, part_b, 3 + d, along_z(d)) for d in (1, 2, 3)]
    for c in one + two:
        c.start()
    for c in one:
        c.wait()
    part_c = buf.at[:, :, z, first]
    three = [copy(part_c, part_c, 6 + d, along_z(d)) for d in (1, 2, 3)]
    for c in three:
        c.start()
    for c in two:
        c.wait()
    part_d = buf.at[:, x, :, second]
    four = [copy(part_d, part_d, 9 + d, along_x(d)) for d in (1, 2, 3)]
    for c in four:
        c.start()

    top[...] = jnp.full_like(top, MASKED)
    acc[...] = jnp.zeros_like(acc)
    ones = jnp.ones((SECTION, HEAD), jnp.bfloat16)

    def block(half, rows, head, keys, values, mask):
        query = x_ref[rows, head * HEAD : (head + 1) * HEAD]
        scores = lax.dot_general(
            query, keys, (((1,), (1,)), ((), ())), preferred_element_type=jnp.float32
        )
        scores = scores * (HEAD ** (-0.5) * LOG2E)
        if mask is not None:
            scores = jnp.where(mask, scores, MASKED)
        old = top[half, head]
        new = jnp.maximum(old, jnp.max(scores, axis=-1, keepdims=True))
        factor = jnp.exp2(old - new)
        weights = jnp.exp2(scores - new[:, :1]).astype(jnp.bfloat16)
        product = jnp.dot(weights, values, preferred_element_type=jnp.float32)
        top[half, head] = new
        acc[half, head] = acc[half, head] * jnp.concatenate([factor, factor], axis=1) + product

    def diagonal(half):
        rows = pl.ds(half * HALF, HALF)
        keys = buf[0, x, z]
        values = jnp.concatenate([buf[1, x, z], ones], axis=1)
        row = lax.broadcasted_iota(jnp.int32, (HALF, SECTION), 0) + half * HALF
        col = lax.broadcasted_iota(jnp.int32, (HALF, SECTION), 1)
        mask = col <= row
        for head in range(OWN_HEADS):
            block(half, rows, head, keys, values, mask)

    def earlier(half, number):
        rows = pl.ds(half * HALF, HALF)
        keys = buf[0, number // 4, number % 4]
        values = jnp.concatenate([buf[1, number // 4, number % 4], ones], axis=1)
        for head in range(OWN_HEADS):
            block(half, rows, head, keys, values, None)

    def finish(half):
        parts = []
        for head in range(OWN_HEADS):
            total = acc[half, head]
            parts.append((total[:, :HEAD] / total[:, HEAD:]).astype(jnp.bfloat16))
        return jnp.concatenate(parts, axis=1)

    lax.fori_loop(0, 2, lambda half, c: (diagonal(half), c)[1], 0)
    for c in three + four:
        c.wait()

    def run(half):
        lax.fori_loop(0, seq, lambda number, c: (earlier(half, number), c)[1], 0)

    run(1 - img)
    other[...] = finish(1 - img)
    columns = pl.ds(pl.multiple_of(img * (OWN_HEADS * HEAD), OWN_HEADS * HEAD), OWN_HEADS * HEAD)
    back = copy(other, out_ref.at[:, columns], 13, partner)
    back.start()
    run(img)
    out_ref[:, columns] = finish(img)
    back.wait()


def attend(rows):
    return pl.pallas_call(
        attend_kernel,
        out_shape=jax.ShapeDtypeStruct((HALF, 2 * OWN_HEADS * HEAD), jnp.bfloat16),
        in_specs=[pl.BlockSpec(memory_space=pltpu.VMEM)],
        out_specs=pl.BlockSpec(memory_space=pltpu.VMEM),
        scratch_shapes=[
            pltpu.VMEM((2, 4, 4, SECTION, HEAD), jnp.bfloat16),
            pltpu.VMEM((8, HEAD), jnp.bfloat16),
            pltpu.VMEM((HALF, OWN_HEADS * HEAD), jnp.bfloat16),
            pltpu.VMEM((2, OWN_HEADS, HALF, HEAD), jnp.float32),
            pltpu.VMEM((2, OWN_HEADS, HALF, 2 * HEAD), jnp.float32),
            pltpu.SemaphoreType.DMA((14,)),
            pltpu.SemaphoreType.DMA((14,)),
        ],
        compiler_params=pltpu.CompilerParams(
            collective_id=0, has_side_effects=True, vmem_limit_bytes=40 * 1024 * 1024
        ),
    )(rows)


def ring_gather(copy, base, block, part, here, ahead, behind):
    before, after = (here + 3) % 4, (here + 1) % 4
    send_up = copy(block(here), block(here), base, ahead)
    send_down = copy(block(here), block(here), base + 1, behind)
    pass_up = copy(part(before, 0), part(before, 0), base + 2, ahead)
    pass_down = copy(part(after, 1), part(after, 1), base + 3, behind)

    def start():
        send_up.start()
        send_down.start()

    def turn():
        send_up.wait_recv()
        pass_up.start()
        send_down.wait_recv()
        pass_down.start()

    def done():
        pass_up.wait_recv()
        pass_down.wait_recv()
        for c in (send_up, send_down, pass_up, pass_down):
            c.wait_send()

    return start, turn, done


def column_gather(copy, base, slot, part, y, core, device):
    before, after, far = (y + 3) % 4, (y + 1) % 4, (y + 2) % 4
    ahead, behind, sibling = device(after, core), device(before, core), device(y, 1 - core)
    own = slot(y, core)
    share = copy(own, own, base, sibling)
    send_up = copy(own, own, base + 1, ahead)
    send_down = copy(own, own, base + 2, behind)
    low, high = part(before, core, 0), part(after, core, 1)
    pass_up = copy(low, low, base + 3, ahead)
    pass_down = copy(high, high, base + 4, behind)
    left, right = slot(before, core), slot(after, core)
    give_left = copy(left, left, base + 5, sibling)
    give_right = copy(right, right, base + 6, sibling)
    far_low, far_high = part(far, core, 0), part(far, core, 1)
    give_low = copy(far_low, far_low, base + 7, sibling)
    give_high = copy(far_high, far_high, base + 8, sibling)

    def start():
        send_up.start()
        send_down.start()
        share.start()

    def turn():
        send_up.wait_recv()
        pass_up.start()
        give_left.start()
        send_down.wait_recv()
        pass_down.start()
        give_right.start()

    def last():
        pass_up.wait_recv()
        give_low.start()
        pass_down.wait_recv()
        give_high.start()

    def done():
        for c in (share, give_left, give_right, give_low, give_high):
            c.wait_recv()
        for c in (share, send_up, send_down, pass_up, pass_down, give_left, give_right, give_low, give_high):
            c.wait_send()

    return start, turn, last, done


def vision_kernel(
    count_ref, patches_ref, gain_ref, shift_ref, qkv_ref, qkv_bias_ref, proj_ref, proj_bias_ref,
    merge_gain_ref, merge_shift_ref, merge_ref, merge_bias_ref, text_ref, norm_gain_ref, half_ref,
    text_out, vision_out,
    mixed, ctx, ctx_in, proj_all, merge_w, lines, merge_in, tok, weight, text, squares,
    send, recv, ctx_send, ctx_recv, local,
):
    seq = lax.axis_index("seq")
    tp = lax.axis_index("tp")
    img = lax.axis_index("img")
    x, z = seq // 4, seq % 4
    core, y = tp % 2, img * 2 + tp // 2
    me = tp * 2 + img

    def device(y_at, core_at):
        return {"tp": 2 * (y_at % 2) + core_at, "img": y_at // 2}

    def order(y_at, core_at):
        return (2 * (y_at % 2) + core_at) * 2 + y_at // 2

    def along_x(d):
        return {"seq": ((x + d) % 4) * 4 + z}

    def along_z(d):
        return {"seq": x * 4 + (z + d) % 4}

    def member(index):
        return {"tp": index // 2, "img": index % 2}

    peers = [member((me + d) % 8) for d in range(1, 8)]
    peers += [along_x(1), along_x(3), along_z(1), along_z(3)]
    barrier = pltpu.get_barrier_semaphore()
    for peer in peers:
        pl.semaphore_signal(barrier, inc=1, device_id=peer, device_id_type=MESH)
    load_merge = pltpu.make_async_copy(merge_ref, merge_w, local.at[0])
    load_merge.start()
    load_half = pltpu.make_async_copy(half_ref.at[img], weight.at[x, z, img], local.at[1])
    load_half.start()
    load_text = pltpu.make_async_copy(text_ref, text.at[tp, img], local.at[2])
    load_text.start()
    proj_all[:, 2 * VHEAD :, :] = jnp.zeros((8, 256 - 2 * VHEAD, VW), jnp.bfloat16)
    proj_all[me, : 2 * VHEAD, :] = proj_ref[...]
    pl.semaphore_wait(barrier, len(peers))

    def copy(src, dst, number, peer):
        return pltpu.make_async_remote_copy(
            src_ref=src,
            dst_ref=dst,
            send_sem=send.at[number],
            recv_sem=recv.at[number],
            device_id=peer,
            device_id_type=MESH,
        )

    proj_gather = column_gather(
        copy, 0,
        lambda a, b: proj_all.at[order(a, b), pl.ds(0, 160)],
        lambda a, b, h: proj_all.at[order(a, b), pl.ds(80 * h, 80)],
        y, core, device,
    )
    merge_gather = column_gather(
        copy, 9,
        lambda a, b: merge_in.at[:, pl.ds(order(a, b) * 32, 32)],
        lambda a, b, h: merge_in.at[pl.ds(2 * h, 2), pl.ds(order(a, b) * 32, 32)],
        y, core, device,
    )
    token_gather = column_gather(
        copy, 18,
        lambda a, b: tok.at[order(a, b)],
        lambda a, b, h: tok.at[order(a, b), pl.ds(128 * h, 128)],
        y, core, device,
    )
    text_gather = column_gather(
        copy, 27,
        lambda a, b: text.at[2 * (a % 2) + b, a // 2],
        lambda a, b, h: text.at[2 * (a % 2) + b, a // 2, pl.ds(128 * h, 128)],
        y, core, device,
    )
    swap_src = half_ref.at[1 - img]
    swap = copy(swap_src, weight.at[x, z, img], 36, {"img": 1 - img})
    theirs = 1 - img
    one_x = ring_gather(
        copy, 37,
        lambda a: weight.at[a, z, img],
        lambda a, h: weight.at[a, z, img, pl.ds(128 * h, 128)],
        x, along_x(1), along_x(3),
    )
    one_z = ring_gather(
        copy, 41,
        lambda a: weight.at[x, a, theirs],
        lambda a, h: weight.at[x, a, theirs, pl.ds(128 * h, 128)],
        z, along_z(1), along_z(3),
    )
    two_z = ring_gather(
        copy, 45,
        lambda a: weight.at[:, a, img],
        lambda a, h: weight.at[:, a, img, pl.ds(128 * h, 128)],
        z, along_z(1), along_z(3),
    )
    two_x = ring_gather(
        copy, 49,
        lambda a: weight.at[a, :, theirs],
        lambda a, h: weight.at[a, :, theirs, pl.ds(128 * h, 128)],
        x, along_x(1), along_x(3),
    )

    proj_gather[0]()
    swap.start()
    load_half.wait()
    one_x[0]()

    def norm(source, gain, shift):
        average = jnp.mean(source, axis=-1, keepdims=True)
        centred = source - average
        spread = jnp.mean(centred * centred, axis=-1, keepdims=True)
        return centred * lax.rsqrt(spread + EPSILON) * gain + shift

    def mix(number, carry):
        rows = pl.ds(number * 256, 256)
        normed = norm(patches_ref[rows, :].astype(jnp.float32), gain_ref[...], shift_ref[...])
        product = jnp.dot(normed.astype(jnp.bfloat16), qkv_ref[...], preferred_element_type=jnp.float32)
        mixed[rows, :] = (product + qkv_bias_ref[...]).astype(jnp.bfloat16)
        return carry

    lax.fori_loop(0, 4, mix, 0)
    proj_gather[1]()
    swap.wait()
    one_z[0]()
    one_x[1]()
    valid = lax.broadcasted_iota(jnp.int32, (256, PATCH_CAP), 1) < count_ref[0]
    lane = lax.broadcasted_iota(jnp.int32, (256, HEAD), 1)

    def look(number):
        rows = pl.ds(number * 256, 256)
        parts = []
        for head in range(2):
            query = mixed[rows, 384 * head : 384 * head + 128]
            keys = mixed[:, 384 * head + 128 : 384 * head + 256]
            values = mixed[:, 384 * head + 256 : 384 * head + 384]
            scores = lax.dot_general(
                query, keys, (((1,), (1,)), ((), ())), preferred_element_type=jnp.float32
            )
            scores = jnp.where(valid, scores * (VHEAD ** (-0.5) * LOG2E), MASKED)
            best = jnp.max(scores, axis=-1, keepdims=True)
            weights = jnp.exp2(scores - best).astype(jnp.bfloat16)
            product = jnp.dot(weights, values, preferred_element_type=jnp.float32)
            parts.append(product / product[:, VHEAD : VHEAD + 1])
        turned = pltpu.roll(parts[1], VHEAD, 1)
        ctx[rows, :HEAD] = jnp.where(lane < VHEAD, parts[0], turned).astype(jnp.bfloat16)
        ctx[rows, HEAD:] = jnp.where(lane < 2 * VHEAD - HEAD, turned, 0.0).astype(jnp.bfloat16)

    def ctx_copy(number, target):
        return pltpu.make_async_remote_copy(
            src_ref=ctx.at[pl.ds(target * 128, 128)],
            dst_ref=ctx_in.at[me],
            send_sem=ctx_send.at[number],
            recv_sem=ctx_recv.at[me],
            device_id=member(target),
            device_id_type=MESH,
        )

    pair = me // 2
    def look_step(number, carry):
        target = (pair + 1 + number) % 4
        look(target)
        ctx_copy(2 * number, 2 * target).start()
        ctx_copy(2 * number + 1, 2 * target + 1).start()
        return carry

    lax.fori_loop(0, 3, look_step, 0)
    look(pair)
    ctx_copy(6, 2 * pair + 1 - img).start()
    ctx_in[me] = ctx[pl.ds(me * 128, 128), :]
    one_z[1]()
    one_x[2]()
    two_z[0]()
    proj_gather[2]()
    proj_gather[3]()
    one_z[2]()
    two_x[0]()

    def arrived(number, carry):
        source = (me + 1 + number) % 8
        pltpu.make_async_remote_copy(
            src_ref=ctx.at[pl.ds(0, 128)],
            dst_ref=ctx_in.at[source],
            send_sem=ctx_send.at[number],
            recv_sem=ctx_recv.at[source],
            device_id=member(source),
            device_id_type=MESH,
        ).wait()
        return carry

    lax.fori_loop(0, 7, arrived, 0)
    resid = patches_ref[pl.ds(me * 128, 128), :].astype(jnp.float32) + proj_bias_ref[...]
    for number in range(8):
        resid = resid + jnp.dot(ctx_in[number], proj_all[number], preferred_element_type=jnp.float32)
    settled = norm(resid, merge_gain_ref[...], merge_shift_ref[...])
    for tile in range(VW // HEAD):
        lines[tile] = settled[:, tile * HEAD : (tile + 1) * HEAD]
    for number in range(4):
        picked = [lines[tile, pl.ds(number, 32, stride=4), :] for tile in range(VW // HEAD)]
        merge_in[number, pl.ds(me * 32, 32), :] = jnp.concatenate(picked, axis=1).astype(jnp.bfloat16)
    merge_gather[0]()
    load_text.wait()
    merge_gather[1]()
    merge_gather[2]()
    load_merge.wait()
    merge_gather[3]()

    def merge(number, carry):
        columns = pl.ds(pl.multiple_of(number * 256, 256), 256)
        total = merge_bias_ref[:, columns]
        for part in range(4):
            total = total + jnp.dot(
                merge_in[part], merge_w[pl.ds(part * VW, VW), columns], preferred_element_type=jnp.float32
            )
        tok[me, :, columns] = total.astype(jnp.bfloat16)
        return carry

    lax.fori_loop(0, 4, merge, 0)
    token_gather[0]()
    text_gather[0]()
    two_z[1]()
    two_x[1]()
    token_gather[1]()
    text_gather[1]()
    token_gather[2]()
    text_gather[2]()
    two_z[2]()
    two_x[2]()
    token_gather[3]()

    def weigh(rows, wide, chunk, first):
        scaled = (wide * norm_gain_ref[chunk]).astype(jnp.bfloat16)
        folded = jnp.zeros((256, HEAD), jnp.float32)
        for number in range(8):
            piece = wide[:, number * HEAD : (number + 1) * HEAD]
            folded = folded + piece * piece
        w = weight[chunk // 2, pl.ds((chunk % 2) * 2, 2)].reshape(1024, 5 * HEAD)
        return jnp.dot(scaled, w, preferred_element_type=jnp.float32), folded

    def vision_step(chunk, carry):
        product, folded = weigh(None, tok[chunk].astype(jnp.float32), chunk, None)
        vision_out[...] += product
        squares[0] += folded
        return carry

    def text_step(chunk, carry):
        for half in range(2):
            columns = pl.ds(pl.multiple_of((chunk % 2) * 1024, 1024), 1024)
            wide = text[chunk // 2, half, :, columns].astype(jnp.float32)
            product, folded = weigh(None, wide, chunk, None)
            text_out[half] += product
            squares[1 + half] += folded
        return carry

    squares[...] = jnp.zeros_like(squares)
    vision_out[...] = jnp.zeros_like(vision_out)
    text_out[...] = jnp.zeros_like(text_out)
    lax.fori_loop(0, 8, vision_step, 0)
    text_gather[3]()
    lax.fori_loop(0, 8, text_step, 0)

    def scale(number):
        mean = jnp.sum(squares[number], axis=-1, keepdims=True) * (1.0 / 8192)
        return lax.rsqrt(mean + EPSILON)

    vision_out[...] = vision_out[...] * scale(0)
    text_out[0] = text_out[0] * scale(1)
    text_out[1] = text_out[1] * scale(2)


def encode(count, patches, gain, shift, qkv, qkv_bias, proj, proj_bias, merge_gain, merge_shift,
           merge_weight, merge_bias, text, norm_gain, half):
    vmem = pl.BlockSpec(memory_space=pltpu.VMEM)
    hbm = pl.BlockSpec(memory_space=pl.ANY)
    smem = pl.BlockSpec(memory_space=pltpu.SMEM)
    bf16, f32 = jnp.bfloat16, jnp.float32
    return pl.pallas_call(
        vision_kernel,
        out_shape=(
            jax.ShapeDtypeStruct((2, 256, 5 * HEAD), f32),
            jax.ShapeDtypeStruct((256, 5 * HEAD), f32),
        ),
        in_specs=[smem] + [vmem] * 9 + [hbm] + [vmem] + [hbm] + [vmem] + [hbm],
        out_specs=(vmem, vmem),
        scratch_shapes=[
            pltpu.VMEM((PATCH_CAP, 6 * HEAD), bf16),
            pltpu.VMEM((PATCH_CAP, 2 * HEAD), bf16),
            pltpu.VMEM((8, 128, 2 * HEAD), bf16),
            pltpu.VMEM((8, 256, VW), bf16),
            pltpu.VMEM((4 * VW, 1024), bf16),
            pltpu.VMEM((VW // HEAD, 128, HEAD), f32),
            pltpu.VMEM((4, 256, VW), bf16),
            pltpu.VMEM((8, 256, 1024), bf16),
            pltpu.VMEM((4, 4, 2, 256, 5 * HEAD), bf16),
            pltpu.VMEM((4, 2, 256, 2048), bf16),
            pltpu.VMEM((3, 256, HEAD), f32),
            pltpu.SemaphoreType.DMA((53,)),
            pltpu.SemaphoreType.DMA((53,)),
            pltpu.SemaphoreType.DMA((7,)),
            pltpu.SemaphoreType.DMA((8,)),
            pltpu.SemaphoreType.DMA((3,)),
        ],
        compiler_params=pltpu.CompilerParams(
            collective_id=1, has_side_effects=True, vmem_limit_bytes=62 * 1024 * 1024
        ),
    )(count, patches, gain, shift, qkv, qkv_bias, proj, proj_bias, merge_gain, merge_shift,
      merge_weight, merge_bias, text, norm_gain, half)


def on_device(
    patches, patch_counts, image_offsets, vision_gain, vision_shift, vision_qkv, vision_qkv_bias,
    vision_proj, vision_proj_bias, merge_gain, merge_shift, merge_weight, merge_bias, text_embed,
    norm_gain, qkv_weight, qkv_bias,
):
    count = patch_counts[0]
    offset = image_offsets[0]
    img = lax.axis_index("img")
    wide_q = OWN_HEADS * HEAD
    f32 = jnp.float32

    def halves(array):
        first = jnp.concatenate([array[:, :wide_q], array[:, 2 * wide_q : 2 * wide_q + HEAD]], axis=1)
        second = jnp.concatenate([array[:, wide_q : 2 * wide_q], array[:, 2 * wide_q + HEAD :]], axis=1)
        return jnp.stack([first, second])

    spare = ((0, 0), (0, 0), (0, HEAD - VHEAD))
    wide_qkv = jnp.pad(vision_qkv.reshape(VW, 6, VHEAD), spare).reshape(VW, 6 * HEAD)
    wide_bias = jnp.pad(vision_qkv_bias.astype(f32).reshape(1, 6, VHEAD), spare)
    wide_bias = wide_bias.at[:, 2::3, VHEAD].set(1.0).reshape(1, 6 * HEAD)
    from_text, from_vision = encode(
        patch_counts, patches[0], vision_gain[None], vision_shift[None], wide_qkv, wide_bias,
        vision_proj, vision_proj_bias[None], merge_gain[None], merge_shift[None], merge_weight,
        merge_bias.astype(f32)[None], text_embed, norm_gain.astype(f32).reshape(8, 1, 1024),
        halves(qkv_weight),
    )
    from_text = from_text.reshape(SECTION, 5 * HEAD)
    bias = halves(qkv_bias[None])[img, 0]
    my_start = lax.axis_index("seq") * SECTION
    padded = jnp.pad(from_vision, ((SECTION, SECTION), (0, 0)))
    where_at = jnp.clip(my_start - offset + SECTION, 0, PATCH_CAP // 4 + SECTION)
    placed = lax.dynamic_slice_in_dim(padded, where_at, SECTION, 0)
    positions = my_start + jnp.arange(SECTION, dtype=jnp.int32)
    inside = (positions >= offset) & (positions < offset + count // 4)
    projected = jnp.where(inside[:, None], placed, from_text) + bias.astype(f32)
    heads = projected.reshape(SECTION, OWN_HEADS + 1, HEAD)
    turned = rotary(heads, positions, HEAD)
    last = jnp.where(img == 0, turned[:, OWN_HEADS:], heads[:, OWN_HEADS:])
    rows = jnp.concatenate([turned[:, :OWN_HEADS], last], axis=1).astype(jnp.bfloat16)
    return attend(rows.reshape(SECTION, (OWN_HEADS + 1) * HEAD))


def solution(mesh):
    placed = (
        P("seq", None, None),
        P("seq"),
        P("seq"),
        P(),
        P(),
        P(None, ("tp", "img")),
        P(("tp", "img")),
        P(("tp", "img"), None),
        P(),
        P(),
        P(),
        P(None, ("tp", "img")),
        P(("tp", "img")),
        P(("seq", "img"), "tp"),
        P(),
        P(("seq", "img"), "tp"),
        P("tp"),
    )
    return jax.shard_map(
        on_device, mesh=mesh, in_specs=placed, out_specs=P(("seq", "img"), "tp"), check_vma=False
    )
```

```python
import functools

import jax
import jax.numpy as jnp
from jax import lax
from jax.experimental import pallas as pl
from jax.experimental.pallas import tpu as pltpu
from jax.sharding import PartitionSpec as P

HEAD = 128
VW = 1280
PATCH_CAP = 1024
GROUP = 8
VHEAD = 80
SECTION = 512
HALF = 256
OWN_HEADS = 4

EPSILON = 1e-06
THETA = 1000000.0
MASKED = -1e30
LOG2E = 1.4426950408889634
MESH = pl.DeviceIdType.MESH


def rotary(inputs, positions, head_width):
    halfway = head_width // 2
    frequency = jnp.power(
        jnp.float32(THETA), -(jnp.arange(halfway, dtype=jnp.float32) * 2.0) / head_width
    )
    angles = positions.astype(jnp.float32)[:, None] * frequency[None, :]
    angles = angles.reshape((angles.shape[0],) + (1,) * (inputs.ndim - 2) + (halfway,))
    cosine = jnp.cos(angles)
    sine_value = jnp.sin(angles)
    leading = inputs[..., :halfway]
    trailing = inputs[..., halfway:]
    return jnp.concatenate(
        [leading * cosine - trailing * sine_value, trailing * cosine + leading * sine_value],
        axis=-1,
    )


def ring_gather(copy, base, block, part, here, ahead, behind):
    before, after = (here + 3) % 4, (here + 1) % 4
    send_up = copy(block(here), block(here), base, ahead)
    send_down = copy(block(here), block(here), base + 1, behind)
    pass_up = copy(part(before, 0), part(before, 0), base + 2, ahead)
    pass_down = copy(part(after, 1), part(after, 1), base + 3, behind)

    def start():
        send_up.start()
        send_down.start()

    def turn():
        send_up.wait_recv()
        pass_up.start()
        send_down.wait_recv()
        pass_down.start()

    def done():
        pass_up.wait_recv()
        pass_down.wait_recv()
        for c in (send_up, send_down, pass_up, pass_down):
            c.wait_send()

    return start, turn, done


def grid_gather(copy, base, block, part, first, second, ahead, behind):
    before, after, far = (first + 3) % 4, (first + 1) % 4, (first + 2) % 4
    low, high = (second + 3) % 4, (second + 1) % 4

    def whole(number, a, way):
        return copy(block(a, second), block(a, second), base + number, way)

    def half(number, a, b, h, way):
        return copy(part(a, b, h), part(a, b, h), base + number, way)

    up, down = whole(0, first, ahead[0]), whole(1, first, behind[0])
    pass_up = half(2, before, second, 0, ahead[0])
    pass_down = half(3, after, second, 1, behind[0])
    columns = (first, before, after, far)
    over = [(whole(4 + 2 * n, a, ahead[1]), whole(5 + 2 * n, a, behind[1])) for n, a in enumerate(columns)]
    on = [
        (half(12 + 2 * n, a, low, 0, ahead[1]), half(13 + 2 * n, a, high, 1, behind[1]))
        for n, a in enumerate(columns)
    ]

    def spread(n):
        over[n][0].start()
        over[n][1].start()

    def relay(n):
        over[n][0].wait_recv()
        on[n][0].start()
        over[n][1].wait_recv()
        on[n][1].start()

    def begin():
        up.start()
        down.start()
        spread(0)

    def turn():
        up.wait_recv()
        pass_up.start()
        spread(1)
        down.wait_recv()
        pass_down.start()
        spread(2)

    def near():
        relay(0)

    def turned():
        pass_up.wait_recv()
        pass_down.wait_recv()
        spread(3)

    def middle():
        relay(1)
        relay(2)

    def last():
        relay(3)

    def done():
        for c in on:
            c[0].wait_recv()
            c[1].wait_recv()
        for c in [(up, down), (pass_up, pass_down)] + over + on:
            c[0].wait_send()
            c[1].wait_send()

    return begin, turn, near, turned, middle, last, done


def attend_kernel(x_ref, out_ref, buf, guest, query, away, home, top, acc, send, recv):
    seq = lax.axis_index("seq")
    img = lax.axis_index("img")
    x = seq // 4
    z = seq % 4
    partner = {"img": 1 - img}
    mirror = 15 - seq

    def along_x(d):
        return {"seq": ((x + d) % 4) * 4 + z}

    def along_z(d):
        return {"seq": x * 4 + (z + d) % 4}

    peers = [partner, along_x(1), along_x(3), along_z(1), along_z(3)]
    peers += [{"seq": mirror}, {"seq": mirror, "img": 1 - img}]
    barrier = pltpu.get_barrier_semaphore()
    for peer in peers:
        pl.semaphore_signal(barrier, inc=1, device_id=peer, device_id_type=MESH)

    def remote(src, dst, out, into, peer):
        return pltpu.make_async_remote_copy(
            src_ref=src,
            dst_ref=dst,
            send_sem=send.at[out],
            recv_sem=recv.at[into],
            device_id=peer,
            device_id_type=MESH,
        )

    def copy(src, dst, number, peer):
        return remote(src, dst, number, number, peer)

    two = 2 * HEAD
    own_rows = x_ref[:, OWN_HEADS * HEAD :].astype(jnp.float32)
    flipped = [own_rows[n * HEAD : (n + 1) * HEAD].T for n in range(SECTION // HEAD)]
    buf[img, x, z] = jnp.where(img == 0, jnp.concatenate(flipped, axis=0), own_rows).astype(jnp.bfloat16)
    pl.semaphore_wait(barrier, len(peers))
    swap = copy(buf.at[img, x, z], buf.at[img, x, z], 0, partner)
    swap.start()
    lend = copy(x_ref.at[:, pl.ds(two, two)], guest, 1, {"seq": mirror})
    lend.start()
    first, second = pl.ds(0, HALF), pl.ds(HALF, HALF)
    ways = (along_x(1), along_z(1)), (along_x(3), along_z(3))
    gather_one = grid_gather(
        copy, 2,
        lambda a, b: buf.at[:, a, b, first],
        lambda a, b, h: buf.at[h, a, b, first],
        x, z, ways[0], ways[1],
    )
    gather_two = grid_gather(
        copy, 22,
        lambda a, b: buf.at[:, b, a, second],
        lambda a, b, h: buf.at[h, b, a, second],
        z, x, ways[0][::-1], ways[1][::-1],
    )
    top[...] = jnp.full_like(top, MASKED)
    acc[...] = jnp.zeros_like(acc)
    for head in range(2):
        query[pl.ds(head * SECTION, SECTION), :] = x_ref[:, head * HEAD : (head + 1) * HEAD]
    rows_all = 2 * SECTION
    ones = jnp.ones((SECTION, HEAD), jnp.bfloat16)
    tiles = SECTION // HEAD

    def block(group, number, masked):
        rows = pl.ds(group * rows_all, rows_all)
        a, b = number // 4, number % 4
        keys = jnp.concatenate([buf[0, a, b, n * HEAD : (n + 1) * HEAD] for n in range(tiles)], axis=1)
        values = jnp.concatenate([buf[1, a, b], ones], axis=1)
        scores = jnp.dot(query[rows, :], keys, preferred_element_type=jnp.float32)
        scores = scores * (HEAD ** (-0.5) * LOG2E)
        if masked:
            row = lax.broadcasted_iota(jnp.int32, (rows_all, SECTION), 0) % SECTION
            col = lax.broadcasted_iota(jnp.int32, (rows_all, SECTION), 1)
            scores = jnp.where(col <= row, scores, MASKED)
        old = top[rows, :]
        new = jnp.maximum(old, jnp.max(scores, axis=-1, keepdims=True))
        factor = jnp.exp2(old - new)
        weights = [jnp.exp2(scores[:, n * HEAD : (n + 1) * HEAD] - new) for n in range(tiles)]
        weights = jnp.concatenate(weights, axis=1).astype(jnp.bfloat16)
        product = jnp.dot(weights, values, preferred_element_type=jnp.float32)
        top[rows, :] = new
        acc[rows, :] = acc[rows, :] * jnp.concatenate([factor, factor], axis=1) + product

    def run(group, count):
        lax.fori_loop(0, count, lambda number, c: (block(group, number, False), c)[1], 0)

    def finish(group):
        parts = []
        for head in range(2):
            total = acc[pl.ds(group * rows_all + head * SECTION, SECTION), :]
            parts.append((total[:, :HEAD] / total[:, HEAD:]).astype(jnp.bfloat16))
        return jnp.concatenate(parts, axis=1)

    swap.wait()
    gather_one[0]()
    gather_two[0]()
    block(0, seq, True)
    for step in range(1, 7):
        gather_one[step]()
        gather_two[step]()
    lend.wait()
    for head in range(2):
        query[pl.ds(rows_all + head * SECTION, SECTION), :] = guest[:, head * HEAD : (head + 1) * HEAD]
    block(1, mirror, True)
    run(1, mirror)
    away[...] = finish(1)
    to_mirror = [
        remote(
            away.at[pl.ds(HALF * n, HALF)],
            out_ref.at[:, pl.ds(pl.multiple_of(img * 2 * two + two, two), two)],
            42 + n, 42 + img, {"seq": mirror, "img": n},
        )
        for n in range(2)
    ]
    for c in to_mirror:
        c.start()
    run(0, seq)
    home[...] = finish(0)
    columns = pl.ds(pl.multiple_of(img * 2 * two, two), two)
    back = copy(home.at[pl.ds(pl.multiple_of((1 - img) * HALF, HALF), HALF)], out_ref.at[:, columns], 44, partner)
    back.start()
    out_ref[:, columns] = home[pl.ds(pl.multiple_of(img * HALF, HALF), HALF), :]
    for n in range(2):
        to_mirror[n].wait_send()
        remote(
            away.at[pl.ds(HALF * n, HALF)],
            out_ref.at[:, pl.ds(n * 2 * two + two, two)],
            42 + n, 42 + n, {"seq": mirror, "img": n},
        ).wait_recv()
    back.wait()


def attend(rows):
    return pl.pallas_call(
        attend_kernel,
        out_shape=jax.ShapeDtypeStruct((HALF, 2 * OWN_HEADS * HEAD), jnp.bfloat16),
        in_specs=[pl.BlockSpec(memory_space=pltpu.VMEM)],
        out_specs=pl.BlockSpec(memory_space=pltpu.VMEM),
        scratch_shapes=[
            pltpu.VMEM((2, 4, 4, SECTION, HEAD), jnp.bfloat16),
            pltpu.VMEM((SECTION, 2 * HEAD), jnp.bfloat16),
            pltpu.VMEM((4 * SECTION, HEAD), jnp.bfloat16),
            pltpu.VMEM((SECTION, 2 * HEAD), jnp.bfloat16),
            pltpu.VMEM((SECTION, 2 * HEAD), jnp.bfloat16),
            pltpu.VMEM((4 * SECTION, HEAD), jnp.float32),
            pltpu.VMEM((4 * SECTION, 2 * HEAD), jnp.float32),
            pltpu.SemaphoreType.DMA((45,)),
            pltpu.SemaphoreType.DMA((45,)),
        ],
        compiler_params=pltpu.CompilerParams(
            collective_id=0, has_side_effects=True, vmem_limit_bytes=40 * 1024 * 1024
        ),
    )(rows)


def column_gather(copy, base, slot, part, y, core, device):
    before, after, far = (y + 3) % 4, (y + 1) % 4, (y + 2) % 4
    ahead, behind, sibling = device(after, core), device(before, core), device(y, 1 - core)
    own = slot(y, core)
    share = copy(own, own, base, sibling)
    send_up = copy(own, own, base + 1, ahead)
    send_down = copy(own, own, base + 2, behind)
    low, high = part(before, core, 0), part(after, core, 1)
    pass_up = copy(low, low, base + 3, ahead)
    pass_down = copy(high, high, base + 4, behind)
    left, right = slot(before, core), slot(after, core)
    give_left = copy(left, left, base + 5, sibling)
    give_right = copy(right, right, base + 6, sibling)
    far_low, far_high = part(far, core, 0), part(far, core, 1)
    give_low = copy(far_low, far_low, base + 7, sibling)
    give_high = copy(far_high, far_high, base + 8, sibling)

    def start():
        send_up.start()
        send_down.start()
        share.start()

    def turn():
        send_up.wait_recv()
        pass_up.start()
        give_left.start()
        send_down.wait_recv()
        pass_down.start()
        give_right.start()

    def last():
        pass_up.wait_recv()
        give_low.start()
        pass_down.wait_recv()
        give_high.start()

    def done():
        for c in (share, give_left, give_right, give_low, give_high):
            c.wait_recv()
        for c in (share, send_up, send_down, pass_up, pass_down, give_left, give_right, give_low, give_high):
            c.wait_send()

    return start, turn, last, done


def vision_kernel(
    count_ref, patches_ref, gain_ref, shift_ref, qkv_ref, qkv_bias_ref, proj_ref, proj_bias_ref,
    merge_gain_ref, merge_shift_ref, merge_ref, merge_bias_ref, text_ref, norm_gain_ref, half_ref,
    text_out, vision_out,
    mixed, ctx, ctx_in, proj_all, merge_w, lines, merge_in, tok, weight, text, squares,
    send, recv, ctx_send, ctx_recv, local,
):
    seq = lax.axis_index("seq")
    tp = lax.axis_index("tp")
    img = lax.axis_index("img")
    x, z = seq // 4, seq % 4
    core, y = tp % 2, img * 2 + tp // 2
    me = tp * 2 + img

    def device(y_at, core_at):
        return {"tp": 2 * (y_at % 2) + core_at, "img": y_at // 2}

    def order(y_at, core_at):
        return (2 * (y_at % 2) + core_at) * 2 + y_at // 2

    def along_x(d):
        return {"seq": ((x + d) % 4) * 4 + z}

    def along_z(d):
        return {"seq": x * 4 + (z + d) % 4}

    def member(index):
        return {"tp": index // 2, "img": index % 2}

    peers = [member((me + d) % 8) for d in range(1, 8)]
    peers += [along_x(1), along_x(3), along_z(1), along_z(3)]
    barrier = pltpu.get_barrier_semaphore()
    for peer in peers:
        pl.semaphore_signal(barrier, inc=1, device_id=peer, device_id_type=MESH)
    load_merge = pltpu.make_async_copy(merge_ref, merge_w, local.at[0])
    load_merge.start()
    load_half = pltpu.make_async_copy(half_ref.at[img], weight.at[x, z, img], local.at[1])
    load_half.start()
    load_text = pltpu.make_async_copy(text_ref, text.at[tp, img], local.at[2])
    load_text.start()
    proj_all[:, 2 * VHEAD :, :] = jnp.zeros((8, 256 - 2 * VHEAD, VW), jnp.bfloat16)
    proj_all[me, : 2 * VHEAD, :] = proj_ref[...]
    pl.semaphore_wait(barrier, len(peers))

    def copy(src, dst, number, peer):
        return pltpu.make_async_remote_copy(
            src_ref=src,
            dst_ref=dst,
            send_sem=send.at[number],
            recv_sem=recv.at[number],
            device_id=peer,
            device_id_type=MESH,
        )

    proj_gather = column_gather(
        copy, 0,
        lambda a, b: proj_all.at[order(a, b), pl.ds(0, 160)],
        lambda a, b, h: proj_all.at[order(a, b), pl.ds(80 * h, 80)],
        y, core, device,
    )
    merge_gather = column_gather(
        copy, 9,
        lambda a, b: merge_in.at[:, pl.ds(order(a, b) * 32, 32)],
        lambda a, b, h: merge_in.at[pl.ds(2 * h, 2), pl.ds(order(a, b) * 32, 32)],
        y, core, device,
    )
    token_gather = column_gather(
        copy, 18,
        lambda a, b: tok.at[order(a, b)],
        lambda a, b, h: tok.at[order(a, b), pl.ds(128 * h, 128)],
        y, core, device,
    )
    text_gather = column_gather(
        copy, 27,
        lambda a, b: text.at[2 * (a % 2) + b, a // 2],
        lambda a, b, h: text.at[2 * (a % 2) + b, a // 2, pl.ds(128 * h, 128)],
        y, core, device,
    )
    swap_src = half_ref.at[1 - img]
    swap = copy(swap_src, weight.at[x, z, img], 36, {"img": 1 - img})
    theirs = 1 - img
    one_x = ring_gather(
        copy, 37,
        lambda a: weight.at[a, z, img],
        lambda a, h: weight.at[a, z, img, pl.ds(128 * h, 128)],
        x, along_x(1), along_x(3),
    )
    one_z = ring_gather(
        copy, 41,
        lambda a: weight.at[x, a, theirs],
        lambda a, h: weight.at[x, a, theirs, pl.ds(128 * h, 128)],
        z, along_z(1), along_z(3),
    )
    two_z = ring_gather(
        copy, 45,
        lambda a: weight.at[:, a, img],
        lambda a, h: weight.at[:, a, img, pl.ds(128 * h, 128)],
        z, along_z(1), along_z(3),
    )
    two_x = ring_gather(
        copy, 49,
        lambda a: weight.at[a, :, theirs],
        lambda a, h: weight.at[a, :, theirs, pl.ds(128 * h, 128)],
        x, along_x(1), along_x(3),
    )

    proj_gather[0]()
    swap.start()
    load_half.wait()
    one_x[0]()

    def norm(source, gain, shift):
        average = jnp.mean(source, axis=-1, keepdims=True)
        centred = source - average
        spread = jnp.mean(centred * centred, axis=-1, keepdims=True)
        return centred * lax.rsqrt(spread + EPSILON) * gain + shift

    def mix(number, carry):
        rows = pl.ds(number * 256, 256)
        normed = norm(patches_ref[rows, :].astype(jnp.float32), gain_ref[...], shift_ref[...])
        product = jnp.dot(normed.astype(jnp.bfloat16), qkv_ref[...], preferred_element_type=jnp.float32)
        mixed[rows, :] = (product + qkv_bias_ref[...]).astype(jnp.bfloat16)
        return carry

    lax.fori_loop(0, 4, mix, 0)
    proj_gather[1]()
    swap.wait()
    one_z[0]()
    one_x[1]()
    valid = lax.broadcasted_iota(jnp.int32, (256, PATCH_CAP), 1) < count_ref[0]
    lane = lax.broadcasted_iota(jnp.int32, (256, HEAD), 1)

    def look(number):
        rows = pl.ds(number * 256, 256)
        parts = []
        for head in range(2):
            query = mixed[rows, 384 * head : 384 * head + 128]
            keys = mixed[:, 384 * head + 128 : 384 * head + 256]
            values = mixed[:, 384 * head + 256 : 384 * head + 384]
            scores = lax.dot_general(
                query, keys, (((1,), (1,)), ((), ())), preferred_element_type=jnp.float32
            )
            scores = jnp.where(valid, scores * (VHEAD ** (-0.5) * LOG2E), MASKED)
            best = jnp.max(scores, axis=-1, keepdims=True)
            weights = jnp.exp2(scores - best).astype(jnp.bfloat16)
            product = jnp.dot(weights, values, preferred_element_type=jnp.float32)
            parts.append(product / product[:, VHEAD : VHEAD + 1])
        turned = pltpu.roll(parts[1], VHEAD, 1)
        ctx[rows, :HEAD] = jnp.where(lane < VHEAD, parts[0], turned).astype(jnp.bfloat16)
        ctx[rows, HEAD:] = jnp.where(lane < 2 * VHEAD - HEAD, turned, 0.0).astype(jnp.bfloat16)

    def ctx_copy(number, target):
        return pltpu.make_async_remote_copy(
            src_ref=ctx.at[pl.ds(target * 128, 128)],
            dst_ref=ctx_in.at[me],
            send_sem=ctx_send.at[number],
            recv_sem=ctx_recv.at[me],
            device_id=member(target),
            device_id_type=MESH,
        )

    pair = me // 2
    def look_step(number, carry):
        target = (pair + 1 + number) % 4
        look(target)
        ctx_copy(2 * number, 2 * target).start()
        ctx_copy(2 * number + 1, 2 * target + 1).start()
        return carry

    lax.fori_loop(0, 3, look_step, 0)
    look(pair)
    ctx_copy(6, 2 * pair + 1 - img).start()
    ctx_in[me] = ctx[pl.ds(me * 128, 128), :]
    one_z[1]()
    one_x[2]()
    two_z[0]()
    proj_gather[2]()
    proj_gather[3]()
    one_z[2]()
    two_x[0]()

    def arrived(number, carry):
        source = (me + 1 + number) % 8
        pltpu.make_async_remote_copy(
            src_ref=ctx.at[pl.ds(0, 128)],
            dst_ref=ctx_in.at[source],
            send_sem=ctx_send.at[number],
            recv_sem=ctx_recv.at[source],
            device_id=member(source),
            device_id_type=MESH,
        ).wait()
        return carry

    lax.fori_loop(0, 7, arrived, 0)
    resid = patches_ref[pl.ds(me * 128, 128), :].astype(jnp.float32) + proj_bias_ref[...]
    for number in range(8):
        resid = resid + jnp.dot(ctx_in[number], proj_all[number], preferred_element_type=jnp.float32)
    settled = norm(resid, merge_gain_ref[...], merge_shift_ref[...])
    for tile in range(VW // HEAD):
        lines[tile] = settled[:, tile * HEAD : (tile + 1) * HEAD]
    for number in range(4):
        picked = [lines[tile, pl.ds(number, 32, stride=4), :] for tile in range(VW // HEAD)]
        merge_in[number, pl.ds(me * 32, 32), :] = jnp.concatenate(picked, axis=1).astype(jnp.bfloat16)
    merge_gather[0]()
    load_text.wait()
    merge_gather[1]()
    merge_gather[2]()
    load_merge.wait()
    merge_gather[3]()

    def merge(number, carry):
        columns = pl.ds(pl.multiple_of(number * 256, 256), 256)
        total = merge_bias_ref[:, columns]
        for part in range(4):
            total = total + jnp.dot(
                merge_in[part], merge_w[pl.ds(part * VW, VW), columns], preferred_element_type=jnp.float32
            )
        tok[me, :, columns] = total.astype(jnp.bfloat16)
        return carry

    lax.fori_loop(0, 4, merge, 0)
    token_gather[0]()
    text_gather[0]()
    two_z[1]()
    two_x[1]()
    token_gather[1]()
    text_gather[1]()
    token_gather[2]()
    text_gather[2]()
    two_z[2]()
    two_x[2]()
    token_gather[3]()

    def weigh(rows, wide, chunk, first):
        scaled = (wide * norm_gain_ref[chunk]).astype(jnp.bfloat16)
        folded = jnp.zeros((256, HEAD), jnp.float32)
        for number in range(8):
            piece = wide[:, number * HEAD : (number + 1) * HEAD]
            folded = folded + piece * piece
        w = weight[chunk // 2, pl.ds((chunk % 2) * 2, 2)].reshape(1024, 5 * HEAD)
        return jnp.dot(scaled, w, preferred_element_type=jnp.float32), folded

    def vision_step(chunk, carry):
        product, folded = weigh(None, tok[chunk].astype(jnp.float32), chunk, None)
        vision_out[...] += product
        squares[0] += folded
        return carry

    def text_step(chunk, carry):
        for half in range(2):
            columns = pl.ds(pl.multiple_of((chunk % 2) * 1024, 1024), 1024)
            wide = text[chunk // 2, half, :, columns].astype(jnp.float32)
            product, folded = weigh(None, wide, chunk, None)
            text_out[half] += product
            squares[1 + half] += folded
        return carry

    squares[...] = jnp.zeros_like(squares)
    vision_out[...] = jnp.zeros_like(vision_out)
    text_out[...] = jnp.zeros_like(text_out)
    lax.fori_loop(0, 8, vision_step, 0)
    text_gather[3]()
    lax.fori_loop(0, 8, text_step, 0)

    def scale(number):
        mean = jnp.sum(squares[number], axis=-1, keepdims=True) * (1.0 / 8192)
        return lax.rsqrt(mean + EPSILON)

    vision_out[...] = vision_out[...] * scale(0)
    text_out[0] = text_out[0] * scale(1)
    text_out[1] = text_out[1] * scale(2)


def encode(count, patches, gain, shift, qkv, qkv_bias, proj, proj_bias, merge_gain, merge_shift,
           merge_weight, merge_bias, text, norm_gain, half):
    vmem = pl.BlockSpec(memory_space=pltpu.VMEM)
    hbm = pl.BlockSpec(memory_space=pl.ANY)
    smem = pl.BlockSpec(memory_space=pltpu.SMEM)
    bf16, f32 = jnp.bfloat16, jnp.float32
    return pl.pallas_call(
        vision_kernel,
        out_shape=(
            jax.ShapeDtypeStruct((2, 256, 5 * HEAD), f32),
            jax.ShapeDtypeStruct((256, 5 * HEAD), f32),
        ),
        in_specs=[smem] + [vmem] * 9 + [hbm] + [vmem] + [hbm] + [vmem] + [hbm],
        out_specs=(vmem, vmem),
        scratch_shapes=[
            pltpu.VMEM((PATCH_CAP, 6 * HEAD), bf16),
            pltpu.VMEM((PATCH_CAP, 2 * HEAD), bf16),
            pltpu.VMEM((8, 128, 2 * HEAD), bf16),
            pltpu.VMEM((8, 256, VW), bf16),
            pltpu.VMEM((4 * VW, 1024), bf16),
            pltpu.VMEM((VW // HEAD, 128, HEAD), f32),
            pltpu.VMEM((4, 256, VW), bf16),
            pltpu.VMEM((8, 256, 1024), bf16),
            pltpu.VMEM((4, 4, 2, 256, 5 * HEAD), bf16),
            pltpu.VMEM((4, 2, 256, 2048), bf16),
            pltpu.VMEM((3, 256, HEAD), f32),
            pltpu.SemaphoreType.DMA((53,)),
            pltpu.SemaphoreType.DMA((53,)),
            pltpu.SemaphoreType.DMA((7,)),
            pltpu.SemaphoreType.DMA((8,)),
            pltpu.SemaphoreType.DMA((3,)),
        ],
        compiler_params=pltpu.CompilerParams(
            collective_id=1, has_side_effects=True, vmem_limit_bytes=62 * 1024 * 1024
        ),
    )(count, patches, gain, shift, qkv, qkv_bias, proj, proj_bias, merge_gain, merge_shift,
      merge_weight, merge_bias, text, norm_gain, half)


def on_device(
    patches, patch_counts, image_offsets, vision_gain, vision_shift, vision_qkv, vision_qkv_bias,
    vision_proj, vision_proj_bias, merge_gain, merge_shift, merge_weight, merge_bias, text_embed,
    norm_gain, qkv_weight, qkv_bias,
):
    count = patch_counts[0]
    offset = image_offsets[0]
    img = lax.axis_index("img")
    wide_q = OWN_HEADS * HEAD
    f32 = jnp.float32

    def halves(array):
        first = jnp.concatenate([array[:, :wide_q], array[:, 2 * wide_q : 2 * wide_q + HEAD]], axis=1)
        second = jnp.concatenate([array[:, wide_q : 2 * wide_q], array[:, 2 * wide_q + HEAD :]], axis=1)
        return jnp.stack([first, second])

    spare = ((0, 0), (0, 0), (0, HEAD - VHEAD))
    wide_qkv = jnp.pad(vision_qkv.reshape(VW, 6, VHEAD), spare).reshape(VW, 6 * HEAD)
    wide_bias = jnp.pad(vision_qkv_bias.astype(f32).reshape(1, 6, VHEAD), spare)
    wide_bias = wide_bias.at[:, 2::3, VHEAD].set(1.0).reshape(1, 6 * HEAD)
    from_text, from_vision = encode(
        patch_counts, patches[0], vision_gain[None], vision_shift[None], wide_qkv, wide_bias,
        vision_proj, vision_proj_bias[None], merge_gain[None], merge_shift[None], merge_weight,
        merge_bias.astype(f32)[None], text_embed, norm_gain.astype(f32).reshape(8, 1, 1024),
        halves(qkv_weight),
    )
    from_text = from_text.reshape(SECTION, 5 * HEAD)
    bias = halves(qkv_bias[None])[img, 0]
    my_start = lax.axis_index("seq") * SECTION
    padded = jnp.pad(from_vision, ((SECTION, SECTION), (0, 0)))
    where_at = jnp.clip(my_start - offset + SECTION, 0, PATCH_CAP // 4 + SECTION)
    placed = lax.dynamic_slice_in_dim(padded, where_at, SECTION, 0)
    positions = my_start + jnp.arange(SECTION, dtype=jnp.int32)
    inside = (positions >= offset) & (positions < offset + count // 4)
    projected = jnp.where(inside[:, None], placed, from_text) + bias.astype(f32)
    heads = projected.reshape(SECTION, OWN_HEADS + 1, HEAD)
    turned = rotary(heads, positions, HEAD)
    last = jnp.where(img == 0, turned[:, OWN_HEADS:], heads[:, OWN_HEADS:])
    rows = jnp.concatenate([turned[:, :OWN_HEADS], last], axis=1).astype(jnp.bfloat16)
    return attend(rows.reshape(SECTION, (OWN_HEADS + 1) * HEAD))


def solution(mesh):
    placed = (
        P("seq", None, None),
        P("seq"),
        P("seq"),
        P(),
        P(),
        P(None, ("tp", "img")),
        P(("tp", "img")),
        P(("tp", "img"), None),
        P(),
        P(),
        P(),
        P(None, ("tp", "img")),
        P(("tp", "img")),
        P(("seq", "img"), "tp"),
        P(),
        P(("seq", "img"), "tp"),
        P("tp"),
    )
    return jax.shard_map(
        on_device, mesh=mesh, in_specs=placed, out_specs=P(("seq", "img"), "tp"), check_vma=False
    )
```

```python
import functools

import jax
import jax.numpy as jnp
from jax import lax
from jax.experimental import pallas as pl
from jax.experimental.pallas import tpu as pltpu
from jax.sharding import PartitionSpec as P

HEAD = 128
VW = 1280
PATCH_CAP = 1024
GROUP = 8
VHEAD = 80
SECTION = 512
HALF = 256
OWN_HEADS = 4

EPSILON = 1e-06
THETA = 1000000.0
MASKED = -1e30
LOG2E = 1.4426950408889634
MESH = pl.DeviceIdType.MESH


def rotation(positions):
    halfway = HEAD // 2
    frequency = jnp.power(jnp.float32(THETA), -(jnp.arange(halfway, dtype=jnp.float32) * 2.0) / HEAD)
    angles = positions.astype(jnp.float32)[:, None] * frequency[None, :]
    return jnp.cos(angles), jnp.sin(angles)


def grid_gather(copy, base, block, part, first, second, ahead, behind):
    before, after, far = (first + 3) % 4, (first + 1) % 4, (first + 2) % 4
    low, high = (second + 3) % 4, (second + 1) % 4

    def whole(number, a, way):
        return copy(block(a, second), block(a, second), base + number, way)

    def half(number, a, b, h, way):
        return copy(part(a, b, h), part(a, b, h), base + number, way)

    up, down = whole(0, first, ahead[0]), whole(1, first, behind[0])
    pass_up = half(2, before, second, 0, ahead[0])
    pass_down = half(3, after, second, 1, behind[0])
    columns = (first, before, after, far)
    over = [(whole(4 + 2 * n, a, ahead[1]), whole(5 + 2 * n, a, behind[1])) for n, a in enumerate(columns)]
    on = [
        (half(12 + 2 * n, a, low, 0, ahead[1]), half(13 + 2 * n, a, high, 1, behind[1]))
        for n, a in enumerate(columns)
    ]

    def spread(n):
        over[n][0].start()
        over[n][1].start()

    def relay(n):
        over[n][0].wait_recv()
        on[n][0].start()
        over[n][1].wait_recv()
        on[n][1].start()

    def begin():
        up.start()
        down.start()
        spread(0)

    def turn():
        up.wait_recv()
        pass_up.start()
        spread(1)
        down.wait_recv()
        pass_down.start()
        spread(2)

    def near():
        relay(0)

    def turned():
        pass_up.wait_recv()
        pass_down.wait_recv()
        spread(3)

    def middle():
        relay(1)
        relay(2)

    def last():
        relay(3)

    def done():
        for c in on:
            c[0].wait_recv()
            c[1].wait_recv()
        for c in [(up, down), (pass_up, pass_down)] + over + on:
            c[0].wait_send()
            c[1].wait_send()

    return begin, turn, near, turned, middle, last, done


def attend_kernel(x_ref, out_ref, buf, guest, query, away, home, top, acc, send, recv):
    seq = lax.axis_index("seq")
    img = lax.axis_index("img")
    x = seq // 4
    z = seq % 4
    partner = {"img": 1 - img}
    mirror = 15 - seq

    def along_x(d):
        return {"seq": ((x + d) % 4) * 4 + z}

    def along_z(d):
        return {"seq": x * 4 + (z + d) % 4}

    peers = [partner, along_x(1), along_x(3), along_z(1), along_z(3)]
    peers += [{"seq": mirror}, {"seq": mirror, "img": 1 - img}]
    barrier = pltpu.get_barrier_semaphore()
    for peer in peers:
        pl.semaphore_signal(barrier, inc=1, device_id=peer, device_id_type=MESH)

    def remote(src, dst, out, into, peer):
        return pltpu.make_async_remote_copy(
            src_ref=src,
            dst_ref=dst,
            send_sem=send.at[out],
            recv_sem=recv.at[into],
            device_id=peer,
            device_id_type=MESH,
        )

    def copy(src, dst, number, peer):
        return remote(src, dst, number, number, peer)

    two = 2 * HEAD
    own_rows = x_ref[:, OWN_HEADS * HEAD :].astype(jnp.float32)
    flipped = [own_rows[n * HEAD : (n + 1) * HEAD].T for n in range(SECTION // HEAD)]
    buf[img, x, z] = jnp.where(img == 0, jnp.concatenate(flipped, axis=0), own_rows).astype(jnp.bfloat16)
    pl.semaphore_wait(barrier, len(peers))
    swap = copy(buf.at[img, x, z], buf.at[img, x, z], 0, partner)
    swap.start()
    lend = copy(x_ref.at[:, pl.ds(two, two)], guest, 1, {"seq": mirror})
    lend.start()
    first, second = pl.ds(0, HALF), pl.ds(HALF, HALF)
    ways = (along_x(1), along_z(1)), (along_x(3), along_z(3))
    gather_one = grid_gather(
        copy, 2,
        lambda a, b: buf.at[:, a, b, first],
        lambda a, b, h: buf.at[h, a, b, first],
        x, z, ways[0], ways[1],
    )
    gather_two = grid_gather(
        copy, 22,
        lambda a, b: buf.at[:, b, a, second],
        lambda a, b, h: buf.at[h, b, a, second],
        z, x, ways[0][::-1], ways[1][::-1],
    )
    top[...] = jnp.full_like(top, MASKED)
    acc[...] = jnp.zeros_like(acc)
    for head in range(2):
        query[pl.ds(head * SECTION, SECTION), :] = x_ref[:, head * HEAD : (head + 1) * HEAD]
    rows_all = 2 * SECTION
    ones = jnp.ones((SECTION, HEAD), jnp.bfloat16)
    tiles = SECTION // HEAD

    def block(group, number, masked):
        rows = pl.ds(group * rows_all, rows_all)
        a, b = number // 4, number % 4
        keys = jnp.concatenate([buf[0, a, b, n * HEAD : (n + 1) * HEAD] for n in range(tiles)], axis=1)
        values = jnp.concatenate([buf[1, a, b], ones], axis=1)
        scores = jnp.dot(query[rows, :], keys, preferred_element_type=jnp.float32)
        scores = scores * (HEAD ** (-0.5) * LOG2E)
        if masked:
            row = lax.broadcasted_iota(jnp.int32, (rows_all, SECTION), 0) % SECTION
            col = lax.broadcasted_iota(jnp.int32, (rows_all, SECTION), 1)
            scores = jnp.where(col <= row, scores, MASKED)
        old = top[rows, :]
        new = jnp.maximum(old, jnp.max(scores, axis=-1, keepdims=True))
        factor = jnp.exp2(old - new)
        weights = [jnp.exp2(scores[:, n * HEAD : (n + 1) * HEAD] - new) for n in range(tiles)]
        weights = jnp.concatenate(weights, axis=1).astype(jnp.bfloat16)
        product = jnp.dot(weights, values, preferred_element_type=jnp.float32)
        top[rows, :] = new
        acc[rows, :] = acc[rows, :] * jnp.concatenate([factor, factor], axis=1) + product

    def run(group, count):
        lax.fori_loop(0, count, lambda number, c: (block(group, number, False), c)[1], 0)

    def finish(group):
        parts = []
        for head in range(2):
            total = acc[pl.ds(group * rows_all + head * SECTION, SECTION), :]
            parts.append((total[:, :HEAD] / total[:, HEAD:]).astype(jnp.bfloat16))
        return jnp.concatenate(parts, axis=1)

    swap.wait()
    gather_one[0]()
    gather_two[0]()
    block(0, seq, True)
    for step in range(1, 7):
        gather_one[step]()
        gather_two[step]()
    lend.wait()
    for head in range(2):
        query[pl.ds(rows_all + head * SECTION, SECTION), :] = guest[:, head * HEAD : (head + 1) * HEAD]
    block(1, mirror, True)
    run(1, mirror)
    away[...] = finish(1)
    to_mirror = [
        remote(
            away.at[pl.ds(HALF * n, HALF)],
            out_ref.at[:, pl.ds(pl.multiple_of(img * 2 * two + two, two), two)],
            42 + n, 42 + img, {"seq": mirror, "img": n},
        )
        for n in range(2)
    ]
    for c in to_mirror:
        c.start()
    run(0, seq)
    home[...] = finish(0)
    columns = pl.ds(pl.multiple_of(img * 2 * two, two), two)
    back = copy(home.at[pl.ds(pl.multiple_of((1 - img) * HALF, HALF), HALF)], out_ref.at[:, columns], 44, partner)
    back.start()
    out_ref[:, columns] = home[pl.ds(pl.multiple_of(img * HALF, HALF), HALF), :]
    for n in range(2):
        to_mirror[n].wait_send()
        remote(
            away.at[pl.ds(HALF * n, HALF)],
            out_ref.at[:, pl.ds(n * 2 * two + two, two)],
            42 + n, 42 + n, {"seq": mirror, "img": n},
        ).wait_recv()
    back.wait()


def attend(rows):
    return pl.pallas_call(
        attend_kernel,
        out_shape=jax.ShapeDtypeStruct((HALF, 2 * OWN_HEADS * HEAD), jnp.bfloat16),
        in_specs=[pl.BlockSpec(memory_space=pltpu.VMEM)],
        out_specs=pl.BlockSpec(memory_space=pltpu.VMEM),
        scratch_shapes=[
            pltpu.VMEM((2, 4, 4, SECTION, HEAD), jnp.bfloat16),
            pltpu.VMEM((SECTION, 2 * HEAD), jnp.bfloat16),
            pltpu.VMEM((4 * SECTION, HEAD), jnp.bfloat16),
            pltpu.VMEM((SECTION, 2 * HEAD), jnp.bfloat16),
            pltpu.VMEM((SECTION, 2 * HEAD), jnp.bfloat16),
            pltpu.VMEM((4 * SECTION, HEAD), jnp.float32),
            pltpu.VMEM((4 * SECTION, 2 * HEAD), jnp.float32),
            pltpu.SemaphoreType.DMA((45,)),
            pltpu.SemaphoreType.DMA((45,)),
        ],
        compiler_params=pltpu.CompilerParams(
            collective_id=0, has_side_effects=True, vmem_limit_bytes=40 * 1024 * 1024
        ),
    )(rows)


def column_gather(copy, base, slot, part, y, core, device):
    before, after, far = (y + 3) % 4, (y + 1) % 4, (y + 2) % 4
    ahead, behind, sibling = device(after, core), device(before, core), device(y, 1 - core)
    own = slot(y, core)
    share = copy(own, own, base, sibling)
    send_up = copy(own, own, base + 1, ahead)
    send_down = copy(own, own, base + 2, behind)
    low, high = part(before, core, 0), part(after, core, 1)
    pass_up = copy(low, low, base + 3, ahead)
    pass_down = copy(high, high, base + 4, behind)
    left, right = slot(before, core), slot(after, core)
    give_left = copy(left, left, base + 5, sibling)
    give_right = copy(right, right, base + 6, sibling)
    far_low, far_high = part(far, core, 0), part(far, core, 1)
    give_low = copy(far_low, far_low, base + 7, sibling)
    give_high = copy(far_high, far_high, base + 8, sibling)

    def start():
        send_up.start()
        send_down.start()
        share.start()

    def turn():
        send_up.wait_recv()
        pass_up.start()
        give_left.start()
        send_down.wait_recv()
        pass_down.start()
        give_right.start()

    def last():
        pass_up.wait_recv()
        give_low.start()
        pass_down.wait_recv()
        give_high.start()

    def done():
        for c in (share, give_left, give_right, give_low, give_high):
            c.wait_recv()
        for c in (share, send_up, send_down, pass_up, pass_down, give_left, give_right, give_low, give_high):
            c.wait_send()

    return start, turn, last, done


def vision_kernel(
    count_ref, start_ref, patches_ref, rows_ref, turn_ref, qkv_ref, proj_ref, merge_ref, text_ref, part_ref,
    rows_out,
    wide, mixed, flipped, ctx, ctx_in, proj_all, merge_w, lines, merge_in, weight, text, hidden, total, squares,
    send, recv, ctx_send, ctx_recv, local,
):
    seq = lax.axis_index("seq")
    tp = lax.axis_index("tp")
    img = lax.axis_index("img")
    x, z = seq // 4, seq % 4
    core, y = tp % 2, img * 2 + tp // 2
    me = tp * 2 + img
    gain, shift, proj_bias, merge_gain, merge_shift = [rows_ref[n : n + 1, :] for n in range(5)]

    def device(y_at, core_at):
        return {"tp": 2 * (y_at % 2) + core_at, "img": y_at // 2}

    def order(y_at, core_at):
        return (2 * (y_at % 2) + core_at) * 2 + y_at // 2

    def along_x(d):
        return {"seq": ((x + d) % 4) * 4 + z}

    def along_z(d):
        return {"seq": x * 4 + (z + d) % 4}

    def member(index):
        return {"tp": index // 2, "img": index % 2}

    peers = [member((me + d) % 8) for d in range(1, 8)]
    peers += [along_x(1), along_x(3), along_z(1), along_z(3)]
    barrier = pltpu.get_barrier_semaphore()
    for peer in peers:
        pl.semaphore_signal(barrier, inc=1, device_id=peer, device_id_type=MESH)
    load_merge = pltpu.make_async_copy(merge_ref, merge_w, local.at[0])
    load_merge.start()
    kept = [(img * 512, 0, 512), (1024 + img * HEAD, 512, HEAD)]
    given = [((1 - img) * 512, 0, 512), (1024 + (1 - img) * HEAD, 512, HEAD)]

    mine = pl.ds(pl.multiple_of(img * 1024, 1024), 1024)
    yours = pl.ds(pl.multiple_of((1 - img) * 1024, 1024), 1024)

    def columns_of(start, size):
        return part_ref.at[:, pl.ds(pl.multiple_of(start, HEAD), size)]

    load_half = [
        pltpu.make_async_copy(columns_of(at, size), weight.at[x, z, img, :, pl.ds(to, size)], local.at[1 + n])
        for n, (at, to, size) in enumerate(kept)
    ]
    for c in load_half:
        c.start()
    load_text = pltpu.make_async_copy(text_ref.at[:, mine], text.at[img], local.at[3])
    load_text.start()
    proj_all[:, 2 * VHEAD :, :] = jnp.zeros((8, 256 - 2 * VHEAD, VW), jnp.bfloat16)
    proj_all[me, : 2 * VHEAD, :] = proj_ref[...]
    pl.semaphore_wait(barrier, len(peers))

    def copy(src, dst, number, peer):
        return pltpu.make_async_remote_copy(
            src_ref=src,
            dst_ref=dst,
            send_sem=send.at[number],
            recv_sem=recv.at[number],
            device_id=peer,
            device_id_type=MESH,
        )

    proj_gather = column_gather(
        copy, 0,
        lambda a, b: proj_all.at[order(a, b), pl.ds(0, 160)],
        lambda a, b, h: proj_all.at[order(a, b), pl.ds(80 * h, 80)],
        y, core, device,
    )
    merge_gather = column_gather(
        copy, 9,
        lambda a, b: merge_in.at[:, pl.ds(order(a, b) * 32, 32)],
        lambda a, b, h: merge_in.at[pl.ds(2 * h, 2), pl.ds(order(a, b) * 32, 32)],
        y, core, device,
    )
    hidden_gather = [
        column_gather(
            copy, 18 + 9 * n,
            lambda a, b, n=n: hidden.at[order(a, b), n],
            lambda a, b, h, n=n: hidden.at[order(a, b), n, pl.ds(256 * h, 256)],
            y, core, device,
        )
        for n in range(4)
    ]
    text_swap = [
        copy(text_ref.at[pl.ds(128 * n, 128), yours], text.at[img, pl.ds(128 * n, 128)], 54 + n, {"img": 1 - img})
        for n in range(2)
    ]
    swap = [
        copy(columns_of(at, size), weight.at[x, z, img, :, pl.ds(to, size)], 56 + n, {"img": 1 - img})
        for n, (at, to, size) in enumerate(given)
    ]
    theirs = 1 - img
    ways = (along_x(1), along_z(1)), (along_x(3), along_z(3))
    weight_one = grid_gather(
        copy, 58,
        lambda a, b: weight.at[a, b, img],
        lambda a, b, h: weight.at[a, b, img, pl.ds(128 * h, 128)],
        x, z, ways[0], ways[1],
    )
    weight_two = grid_gather(
        copy, 78,
        lambda a, b: weight.at[b, a, theirs],
        lambda a, b, h: weight.at[b, a, theirs, pl.ds(128 * h, 128)],
        z, x, ways[0][::-1], ways[1][::-1],
    )

    proj_gather[0]()
    for c in load_half:
        c.wait()
    weight_one[0]()
    for c in swap:
        c.start()

    def norm(source, scaling, shifting):
        average = jnp.mean(source, axis=-1, keepdims=True)
        centred = source - average
        spread = jnp.mean(centred * centred, axis=-1, keepdims=True)
        return centred * lax.rsqrt(spread + EPSILON) * scaling + shifting

    old = lax.broadcasted_iota(jnp.int32, (6 * VHEAD, 6 * HEAD), 0)
    new = lax.broadcasted_iota(jnp.int32, (6 * VHEAD, 6 * HEAD), 1)
    place = ((old // VHEAD == new // HEAD) & (old % VHEAD == new % HEAD)).astype(jnp.float32).astype(jnp.bfloat16)
    wide[...] = jnp.dot(qkv_ref[...], place, preferred_element_type=jnp.float32).astype(jnp.bfloat16)
    bias = jnp.dot(
        rows_ref[5:6, : 6 * VHEAD].astype(jnp.bfloat16), place, preferred_element_type=jnp.float32
    )
    column = lax.broadcasted_iota(jnp.int32, (1, 6 * HEAD), 1)
    bias = bias + ((column % HEAD == VHEAD) & ((column // HEAD) % 3 == 2)).astype(jnp.float32)

    def mix(number, carry):
        rows = pl.ds(pl.multiple_of(number * 512, 512), 512)
        normed = norm(patches_ref[rows, :].astype(jnp.float32), gain, shift)
        product = jnp.dot(normed.astype(jnp.bfloat16), wide[...], preferred_element_type=jnp.float32) + bias
        mixed[rows, :] = product.astype(jnp.bfloat16)
        for head in range(2):
            keys = product[:, 384 * head + 128 : 384 * head + 256].T
            flipped[head, :, rows] = keys.astype(jnp.bfloat16)
        return carry

    lax.fori_loop(0, 2, mix, 0)
    for c in swap:
        c.wait()
    weight_two[0]()
    weight_one[1]()
    valid = lax.broadcasted_iota(jnp.int32, (512, PATCH_CAP), 1) < count_ref[0]
    lane = lax.broadcasted_iota(jnp.int32, (512, HEAD), 1)

    def look(number):
        rows = pl.ds(pl.multiple_of(number * 512, 512), 512)
        parts = []
        for head in range(2):
            query = mixed[rows, 384 * head : 384 * head + 128]
            values = mixed[:, 384 * head + 256 : 384 * head + 384]
            scores = jnp.dot(query, flipped[head], preferred_element_type=jnp.float32)
            scores = jnp.where(valid, scores * (VHEAD ** (-0.5) * LOG2E), MASKED)
            best = jnp.max(scores, axis=-1, keepdims=True) + jnp.zeros((512, HEAD), jnp.float32)
            weights = [jnp.exp2(scores[:, n * HEAD : (n + 1) * HEAD] - best) for n in range(8)]
            weights = jnp.concatenate(weights, axis=1).astype(jnp.bfloat16)
            product = jnp.dot(weights, values, preferred_element_type=jnp.float32)
            parts.append(product / product[:, VHEAD : VHEAD + 1])
        turned = pltpu.roll(parts[1], VHEAD, 1)
        ctx[rows, :HEAD] = jnp.where(lane < VHEAD, parts[0], turned).astype(jnp.bfloat16)
        ctx[rows, HEAD:] = jnp.where(lane < 2 * VHEAD - HEAD, turned, 0.0).astype(jnp.bfloat16)

    def ctx_copy(number, target):
        return pltpu.make_async_remote_copy(
            src_ref=ctx.at[pl.ds(pl.multiple_of(target * 128, 128), 128)],
            dst_ref=ctx_in.at[me],
            send_sem=ctx_send.at[number],
            recv_sem=ctx_recv.at[me],
            device_id=member(target),
            device_id_type=MESH,
        )

    side = me // 4
    look(1 - side)
    for n in range(4):
        ctx_copy(n, (1 - side) * 4 + n).start()
    proj_gather[1]()
    look(side)
    for n in range(3):
        ctx_copy(4 + n, side * 4 + (me + 1 + n) % 4).start()
    ctx_in[me] = ctx[pl.ds(pl.multiple_of(me * 128, 128), 128), :]
    proj_gather[2]()
    text_swap[0].start()
    weight_two[1]()
    weight_one[2]()
    weight_two[2]()

    def arrived(number, carry):
        source = (me + 1 + number) % 8
        pltpu.make_async_remote_copy(
            src_ref=ctx.at[pl.ds(0, 128)],
            dst_ref=ctx_in.at[source],
            send_sem=ctx_send.at[number],
            recv_sem=ctx_recv.at[source],
            device_id=member(source),
            device_id_type=MESH,
        ).wait()
        return carry

    lax.fori_loop(0, 7, arrived, 0)
    proj_gather[3]()
    resid = patches_ref[pl.ds(me * 128, 128), :].astype(jnp.float32) + proj_bias
    for number in range(8):
        resid = resid + jnp.dot(ctx_in[number], proj_all[number], preferred_element_type=jnp.float32)
    settled = norm(resid, merge_gain, merge_shift)
    for tile in range(VW // HEAD):
        lines[tile] = settled[:, tile * HEAD : (tile + 1) * HEAD]
    for number in range(4):
        picked = [lines[tile, pl.ds(number, 32, stride=4), :] for tile in range(VW // HEAD)]
        merge_in[number, pl.ds(me * 32, 32), :] = jnp.concatenate(picked, axis=1).astype(jnp.bfloat16)
    merge_gather[0]()
    weight_one[3]()
    weight_two[3]()
    load_merge.wait()
    merge_gather[1]()
    weight_one[4]()
    weight_two[4]()
    merge_gather[2]()
    text_swap[1].start()
    load_text.wait()
    first = start_ref[0] - seq * SECTION
    spot = lax.broadcasted_iota(jnp.int32, (SECTION, 256), 0) - first
    slot = lax.broadcasted_iota(jnp.int32, (SECTION, 256), 1)
    pick = ((spot == slot) & (slot < count_ref[0] // 4)).astype(jnp.float32).astype(jnp.bfloat16)
    merge_gather[3]()
    for c in text_swap:
        c.wait()
    spot = lax.broadcasted_iota(jnp.int32, (SECTION, 256), 0) - first
    inside = (spot >= 0) & (spot < count_ref[0] // 4)
    for number in range(4):
        if number == 2:
            weight_one[5]()
            weight_two[5]()
        columns = slice(256 * number, 256 * number + 256)
        token = rows_ref[6:7, columns]
        for part in range(4):
            token = token + jnp.dot(
                merge_in[part], merge_w[part * VW : part * VW + VW, columns], preferred_element_type=jnp.float32
            )
        placed = jnp.dot(pick, token.astype(jnp.bfloat16), preferred_element_type=jnp.float32)
        words = text[:, :, columns].reshape(SECTION, 256).astype(jnp.float32)
        hidden[me, number] = jnp.where(inside, placed, words).astype(jnp.bfloat16)
        hidden_gather[number][0]()
    squares[...] = jnp.zeros_like(squares)
    total[...] = jnp.zeros_like(total)

    def weigh(chunk):
        values = jnp.concatenate([hidden[chunk, n] for n in range(4)], axis=1).astype(jnp.float32)
        scaled = (values * rows_ref[pl.ds(8 + chunk, 1), :1024]).astype(jnp.bfloat16)
        folded = jnp.zeros((SECTION, HEAD), jnp.float32)
        for number in range(8):
            piece = values[:, number * HEAD : (number + 1) * HEAD]
            folded = folded + piece * piece
        w = weight[chunk // 2, pl.ds((chunk % 2) * 2, 2)].reshape(1024, 5 * HEAD)
        total[...] += jnp.dot(scaled, w, preferred_element_type=jnp.float32)
        squares[...] += folded

    for number in range(4):
        hidden_gather[number][1]()
    weight_one[6]()
    weight_two[6]()
    weigh(me)
    for number in range(4):
        hidden_gather[number][2]()
    weigh(order((y + 1) % 4, core))
    weigh(order((y + 3) % 4, core))
    for number in range(4):
        hidden_gather[number][3]()
    weigh(order((y + 2) % 4, core))

    def rest(number, carry):
        weigh(order((y + number) % 4, 1 - core))
        return carry

    lax.fori_loop(0, 4, rest, 0)
    scale = lax.rsqrt(jnp.sum(squares[...], axis=-1, keepdims=True) * (1.0 / 8192) + EPSILON)
    cosine, sine = turn_ref[:, :HEAD], turn_ref[:, HEAD:]
    for number in range(OWN_HEADS + 1):
        columns = slice(HEAD * number, HEAD * number + HEAD)
        head = total[:, columns] * scale + rows_ref[7:8, columns]
        swapped = pltpu.roll(head, HEAD // 2, 1)
        if number == OWN_HEADS:
            turned = jnp.where(img == 0, head * cosine + swapped * sine, head)
        else:
            turned = head * cosine + swapped * sine
        rows_out[:, columns] = turned.astype(jnp.bfloat16)


def encode(count, start, patches, rows, turn, qkv, proj, merge_weight, text, part):
    vmem = pl.BlockSpec(memory_space=pltpu.VMEM)
    hbm = pl.BlockSpec(memory_space=pl.ANY)
    smem = pl.BlockSpec(memory_space=pltpu.SMEM)
    bf16, f32 = jnp.bfloat16, jnp.float32
    return pl.pallas_call(
        vision_kernel,
        out_shape=jax.ShapeDtypeStruct((SECTION, 5 * HEAD), bf16),
        in_specs=[smem] * 2 + [vmem] * 5 + [hbm] * 3,
        out_specs=vmem,
        scratch_shapes=[
            pltpu.VMEM((VW, 6 * HEAD), bf16),
            pltpu.VMEM((PATCH_CAP, 6 * HEAD), bf16),
            pltpu.VMEM((2, HEAD, PATCH_CAP), bf16),
            pltpu.VMEM((PATCH_CAP, 2 * HEAD), bf16),
            pltpu.VMEM((8, 128, 2 * HEAD), bf16),
            pltpu.VMEM((8, 256, VW), bf16),
            pltpu.VMEM((4 * VW, 1024), bf16),
            pltpu.VMEM((VW // HEAD, 128, HEAD), f32),
            pltpu.VMEM((4, 256, VW), bf16),
            pltpu.VMEM((4, 4, 2, 256, 5 * HEAD), bf16),
            pltpu.VMEM((2, 256, 1024), bf16),
            pltpu.VMEM((8, 4, SECTION, 256), bf16),
            pltpu.VMEM((SECTION, 5 * HEAD), f32),
            pltpu.VMEM((SECTION, HEAD), f32),
            pltpu.SemaphoreType.DMA((98,)),
            pltpu.SemaphoreType.DMA((98,)),
            pltpu.SemaphoreType.DMA((7,)),
            pltpu.SemaphoreType.DMA((8,)),
            pltpu.SemaphoreType.DMA((4,)),
        ],
        compiler_params=pltpu.CompilerParams(
            collective_id=1, has_side_effects=True, vmem_limit_bytes=62 * 1024 * 1024
        ),
    )(count, start, patches, rows, turn, qkv, proj, merge_weight, text, part)


def on_device(
    patches, patch_counts, image_offsets, vision_gain, vision_shift, vision_qkv, vision_qkv_bias,
    vision_proj, vision_proj_bias, merge_gain, merge_shift, merge_weight, merge_bias, text_embed,
    norm_gain, qkv_weight, qkv_bias,
):
    img = lax.axis_index("img")
    wide_q = OWN_HEADS * HEAD
    f32 = jnp.float32

    def line(array):
        return jnp.pad(array.astype(f32), (0, VW - array.shape[0]))[None]

    first_bias = jnp.concatenate([qkv_bias[:wide_q], qkv_bias[2 * wide_q : 2 * wide_q + HEAD]])
    second_bias = jnp.concatenate([qkv_bias[wide_q : 2 * wide_q], qkv_bias[2 * wide_q + HEAD :]])
    own_bias = jnp.where(img == 0, first_bias, second_bias)
    singles = [
        vision_gain, vision_shift, vision_proj_bias, merge_gain, merge_shift, vision_qkv_bias, merge_bias, own_bias,
    ]
    gains = jnp.pad(norm_gain.astype(f32).reshape(8, 1024), ((0, 0), (0, VW - 1024)))
    lines = jnp.concatenate([line(array) for array in singles] + [gains], axis=0)
    positions = lax.axis_index("seq") * SECTION + jnp.arange(SECTION, dtype=jnp.int32)
    cosine, sine = rotation(positions)
    turn = jnp.concatenate([cosine, cosine, -sine, sine], axis=1)
    rows = encode(
        patch_counts, image_offsets, patches[0], lines, turn, vision_qkv, vision_proj, merge_weight, text_embed,
        qkv_weight,
    )
    return attend(rows)


def solution(mesh):
    placed = (
        P("seq", None, None),
        P("seq"),
        P("seq"),
        P(),
        P(),
        P(None, ("tp", "img")),
        P(("tp", "img")),
        P(("tp", "img"), None),
        P(),
        P(),
        P(),
        P(None, ("tp", "img")),
        P(("tp", "img")),
        P(("seq", "img"), "tp"),
        P(),
        P(("seq", "img"), "tp"),
        P("tp"),
    )
    return jax.shard_map(
        on_device, mesh=mesh, in_specs=placed, out_specs=P(("seq", "img"), "tp"), check_vma=False
    )
```

```python
import functools

import jax
import jax.numpy as jnp
from jax import lax
from jax.experimental import pallas as pl
from jax.experimental.pallas import tpu as pltpu
from jax.sharding import PartitionSpec as P

HEAD = 128
VW = 1280
PATCH_CAP = 1024
GROUP = 8
VHEAD = 80
SECTION = 512
HALF = 256
OWN_HEADS = 4

EPSILON = 1e-06
THETA = 1000000.0
MASKED = -1e30
LOG2E = 1.4426950408889634
MESH = pl.DeviceIdType.MESH


def rotation(positions):
    halfway = HEAD // 2
    frequency = jnp.power(jnp.float32(THETA), -(jnp.arange(halfway, dtype=jnp.float32) * 2.0) / HEAD)
    angles = positions.astype(jnp.float32)[:, None] * frequency[None, :]
    return jnp.cos(angles), jnp.sin(angles)


def grid_gather(copy, base, block, part, first, second, ahead, behind):
    before, after, far = (first + 3) % 4, (first + 1) % 4, (first + 2) % 4
    low, high = (second + 3) % 4, (second + 1) % 4

    def whole(number, a, way):
        return copy(block(a, second), block(a, second), base + number, way)

    def half(number, a, b, h, way):
        return copy(part(a, b, h), part(a, b, h), base + number, way)

    up, down = whole(0, first, ahead[0]), whole(1, first, behind[0])
    pass_up = half(2, before, second, 0, ahead[0])
    pass_down = half(3, after, second, 1, behind[0])
    columns = (first, before, after, far)
    over = [(whole(4 + 2 * n, a, ahead[1]), whole(5 + 2 * n, a, behind[1])) for n, a in enumerate(columns)]
    on = [
        (half(12 + 2 * n, a, low, 0, ahead[1]), half(13 + 2 * n, a, high, 1, behind[1]))
        for n, a in enumerate(columns)
    ]

    def spread(n):
        over[n][0].start()
        over[n][1].start()

    def relay(n):
        over[n][0].wait_recv()
        on[n][0].start()
        over[n][1].wait_recv()
        on[n][1].start()

    def begin():
        up.start()
        down.start()
        spread(0)

    def turn():
        up.wait_recv()
        pass_up.start()
        spread(1)
        down.wait_recv()
        pass_down.start()
        spread(2)

    def near():
        relay(0)

    def turned():
        pass_up.wait_recv()
        pass_down.wait_recv()
        spread(3)

    def middle():
        relay(1)
        relay(2)

    def last():
        relay(3)

    def done():
        for c in on:
            c[0].wait_recv()
            c[1].wait_recv()
        for c in [(up, down), (pass_up, pass_down)] + over + on:
            c[0].wait_send()
            c[1].wait_send()

    return begin, turn, near, turned, middle, last, done


def column_gather(copy, base, slot, part, y, core, device):
    before, after, far = (y + 3) % 4, (y + 1) % 4, (y + 2) % 4
    ahead, behind, sibling = device(after, core), device(before, core), device(y, 1 - core)
    own = slot(y, core)
    share = copy(own, own, base, sibling)
    send_up = copy(own, own, base + 1, ahead)
    send_down = copy(own, own, base + 2, behind)
    low, high = part(before, core, 0), part(after, core, 1)
    pass_up = copy(low, low, base + 3, ahead)
    pass_down = copy(high, high, base + 4, behind)
    left, right = slot(before, core), slot(after, core)
    give_left = copy(left, left, base + 5, sibling)
    give_right = copy(right, right, base + 6, sibling)
    far_low, far_high = part(far, core, 0), part(far, core, 1)
    give_low = copy(far_low, far_low, base + 7, sibling)
    give_high = copy(far_high, far_high, base + 8, sibling)

    def start():
        send_up.start()
        send_down.start()
        share.start()

    def turn():
        send_up.wait_recv()
        pass_up.start()
        give_left.start()
        send_down.wait_recv()
        pass_down.start()
        give_right.start()

    def last():
        pass_up.wait_recv()
        give_low.start()
        pass_down.wait_recv()
        give_high.start()

    def done():
        for c in (share, give_left, give_right, give_low, give_high):
            c.wait_recv()
        for c in (share, send_up, send_down, pass_up, pass_down, give_left, give_right, give_low, give_high):
            c.wait_send()

    return start, turn, last, done


def plane_spread(copy, base, give, slot, y, core, device):
    mate = y + 1 - 2 * (y % 2)
    straight = (y + 2) % 4
    across = straight + 1 - 2 * (straight % 2)
    own, sibling = slot(y, core), device(y, 1 - core)

    def send(src, number, peer):
        return copy(src, own, base + number, peer)

    share, near = send(own, 0, sibling), send(own, 1, device(mate, core))
    far, close = send(give, 2, device(straight, core)), send(give, 3, device(across, core))
    relays = [copy(slot(a, core), slot(a, core), base + 4 + n, sibling) for n, a in enumerate((mate, across, straight))]

    def start():
        near.start()
        close.start()
        far.start()
        share.start()

    def turn():
        for c, relay in zip((near, close, far), relays):
            c.wait_recv()
            relay.start()

    def done():
        for c in [share] + relays:
            c.wait_recv()
        for c in [share, near, far, close] + relays:
            c.wait_send()

    return start, turn, done


def vision_kernel(
    count_ref, start_ref, patches_ref, rows_ref, turn_ref, qkv_ref, proj_ref, merge_ref, text_ref, part_ref,
    out_ref,
    wide, mixed, flipped, ctx, ctx_in, proj_all, merge_w, lines, merge_in, weight, text_give, text, tok_give, tok,
    total, squares, sums, part_out, part_in, buf, guest, top, acc,
    send, recv, ctx_send, ctx_recv, local,
):
    seq = lax.axis_index("seq")
    tp = lax.axis_index("tp")
    img = lax.axis_index("img")
    x, z = seq // 4, seq % 4
    core, y = tp % 2, img * 2 + tp // 2
    me = tp * 2 + img
    gain, shift, proj_bias, merge_gain, merge_shift = [rows_ref[n : n + 1, :] for n in range(5)]

    def device(y_at, core_at):
        return {"tp": 2 * (y_at % 2) + core_at, "img": y_at // 2}

    def order(y_at, core_at):
        return (2 * (y_at % 2) + core_at) * 2 + y_at // 2

    def along_x(d):
        return {"seq": ((x + d) % 4) * 4 + z}

    def along_z(d):
        return {"seq": x * 4 + (z + d) % 4}

    def member(index):
        return {"tp": index // 2, "img": index % 2}

    peers = [member((me + d) % 8) for d in range(1, 8)]
    mirror = 15 - seq
    peers += [along_x(1), along_x(3), along_z(1), along_z(3), {"seq": mirror}, {"seq": mirror, "img": 1 - img}]
    barrier = pltpu.get_barrier_semaphore()
    for peer in peers:
        pl.semaphore_signal(barrier, inc=1, device_id=peer, device_id_type=MESH)
    load_merge = pltpu.make_async_copy(merge_ref, merge_w, local.at[0])
    load_merge.start()
    load_weight = pltpu.make_async_copy(part_ref, weight.at[x, z], local.at[1])
    load_weight.start()
    load_text = []
    for n in range(4):
        columns = pl.ds(256 * n, 256)
        for parity, target in ((1 - img, text_give.at[:, columns]), (img, text.at[tp, img, :, columns])):
            at = pl.ds(pl.multiple_of((2 * n + parity) * 256, 256), 256)
            load_text.append(pltpu.make_async_copy(text_ref.at[:, at], target, local.at[2 + len(load_text)]))
    for c in load_text:
        c.start()
    proj_all[:, 2 * VHEAD :, :] = jnp.zeros((8, 256 - 2 * VHEAD, VW), jnp.bfloat16)
    proj_all[me, : 2 * VHEAD, :] = proj_ref[...]
    pl.semaphore_wait(barrier, len(peers))

    def remote(src, dst, out, into, peer):
        return pltpu.make_async_remote_copy(
            src_ref=src,
            dst_ref=dst,
            send_sem=send.at[out],
            recv_sem=recv.at[into],
            device_id=peer,
            device_id_type=MESH,
        )

    def copy(src, dst, number, peer):
        return remote(src, dst, number, number, peer)

    proj_gather = column_gather(
        copy, 0,
        lambda a, b: proj_all.at[order(a, b), pl.ds(0, 160)],
        lambda a, b, h: proj_all.at[order(a, b), pl.ds(80 * h, 80)],
        y, core, device,
    )
    merge_gather = column_gather(
        copy, 9,
        lambda a, b: merge_in.at[:, pl.ds(order(a, b) * 32, 32)],
        lambda a, b, h: merge_in.at[pl.ds(2 * h, 2), pl.ds(order(a, b) * 32, 32)],
        y, core, device,
    )
    text_spread = [
        plane_spread(
            copy, 18 + 7 * n, text_give.at[pl.ds(128 * n, 128)],
            lambda a, b, n=n: text.at[2 * (a % 2) + b, a // 2, pl.ds(128 * n, 128)],
            y, core, device,
        )
        for n in range(2)
    ]
    token_spread = [
        plane_spread(copy, 32 + 7 * n, tok_give.at[n], lambda a, b, n=n: tok.at[order(a, b), n], y, core, device)
        for n in range(2)
    ]
    other = {"img": 1 - img}
    quarter, fifth = pl.ds(0, 4 * HEAD), pl.ds(4 * HEAD, HEAD)
    trade = [
        copy(sums.at[0], sums.at[1], 47, other),
        copy(part_out.at[:, fifth], part_in.at[:, fifth], 46, other),
        copy(part_out.at[:, quarter], part_in.at[:, quarter], 133, other),
    ]
    two = 2 * HEAD
    query = merge_w.at[pl.ds(0, 4 * SECTION), pl.ds(0, HEAD)]
    lent = merge_w.at[pl.ds(0, SECTION), pl.ds(HEAD, two)]
    away = merge_w.at[pl.ds(0, SECTION), pl.ds(HEAD + two, two)]
    home = merge_w.at[pl.ds(0, SECTION), pl.ds(HEAD + 2 * two, two)]
    ways = (along_x(1), along_z(1)), (along_x(3), along_z(3))
    weight_one = grid_gather(
        copy, 48,
        lambda a, b: weight.at[a, b, pl.ds(0, 128)],
        lambda a, b, h: weight.at[a, b, pl.ds(64 * h, 64)],
        x, z, ways[0], ways[1],
    )
    weight_two = grid_gather(
        copy, 68,
        lambda a, b: weight.at[b, a, pl.ds(128, 128)],
        lambda a, b, h: weight.at[b, a, pl.ds(128 + 64 * h, 64)],
        z, x, ways[0][::-1], ways[1][::-1],
    )

    proj_gather[0]()
    load_weight.wait()
    weight_one[0]()
    weight_two[0]()

    def norm(source, scaling, shifting):
        average = jnp.mean(source, axis=-1, keepdims=True)
        centred = source - average
        spread = jnp.mean(centred * centred, axis=-1, keepdims=True)
        return centred * lax.rsqrt(spread + EPSILON) * scaling + shifting

    old = lax.broadcasted_iota(jnp.int32, (6 * VHEAD, 6 * HEAD), 0)
    new = lax.broadcasted_iota(jnp.int32, (6 * VHEAD, 6 * HEAD), 1)
    place = ((old // VHEAD == new // HEAD) & (old % VHEAD == new % HEAD)).astype(jnp.float32).astype(jnp.bfloat16)
    wide[...] = jnp.dot(qkv_ref[...], place, preferred_element_type=jnp.float32).astype(jnp.bfloat16)
    bias = jnp.dot(
        rows_ref[5:6, : 6 * VHEAD].astype(jnp.bfloat16), place, preferred_element_type=jnp.float32
    )
    column = lax.broadcasted_iota(jnp.int32, (1, 6 * HEAD), 1)
    bias = bias + ((column % HEAD == VHEAD) & ((column // HEAD) % 3 == 2)).astype(jnp.float32)

    def mix(number, carry):
        rows = pl.ds(pl.multiple_of(number * 512, 512), 512)
        normed = norm(patches_ref[rows, :].astype(jnp.float32), gain, shift)
        product = jnp.dot(normed.astype(jnp.bfloat16), wide[...], preferred_element_type=jnp.float32) + bias
        mixed[rows, :] = product.astype(jnp.bfloat16)
        for head in range(2):
            keys = product[:, 384 * head + 128 : 384 * head + 256].T
            flipped[head, :, rows] = keys.astype(jnp.bfloat16)
        return carry

    lax.fori_loop(0, 2, mix, 0)
    for c in load_text:
        c.wait()
    valid = lax.broadcasted_iota(jnp.int32, (512, PATCH_CAP), 1) < count_ref[0]
    lane = lax.broadcasted_iota(jnp.int32, (512, HEAD), 1)

    def look(number):
        rows = pl.ds(pl.multiple_of(number * 512, 512), 512)
        parts = []
        for head in range(2):
            query = mixed[rows, 384 * head : 384 * head + 128]
            values = mixed[:, 384 * head + 256 : 384 * head + 384]
            scores = jnp.dot(query, flipped[head], preferred_element_type=jnp.float32)
            scores = jnp.where(valid, scores * (VHEAD ** (-0.5) * LOG2E), MASKED)
            best = jnp.max(scores, axis=-1, keepdims=True) + jnp.zeros((512, HEAD), jnp.float32)
            weights = [jnp.exp2(scores[:, n * HEAD : (n + 1) * HEAD] - best) for n in range(8)]
            weights = jnp.concatenate(weights, axis=1).astype(jnp.bfloat16)
            product = jnp.dot(weights, values, preferred_element_type=jnp.float32)
            parts.append(product / product[:, VHEAD : VHEAD + 1])
        turned = pltpu.roll(parts[1], VHEAD, 1)
        ctx[rows, :HEAD] = jnp.where(lane < VHEAD, parts[0], turned).astype(jnp.bfloat16)
        ctx[rows, HEAD:] = jnp.where(lane < 2 * VHEAD - HEAD, turned, 0.0).astype(jnp.bfloat16)

    def ctx_copy(number, target):
        return pltpu.make_async_remote_copy(
            src_ref=ctx.at[pl.ds(pl.multiple_of(target * 128, 128), 128)],
            dst_ref=ctx_in.at[me],
            send_sem=ctx_send.at[number],
            recv_sem=ctx_recv.at[me],
            device_id=member(target),
            device_id_type=MESH,
        )

    side = me // 4
    look(1 - side)
    for n in range(4):
        ctx_copy(n, (1 - side) * 4 + n).start()
    proj_gather[1]()
    look(side)
    for n in range(3):
        ctx_copy(4 + n, side * 4 + (me + 1 + n) % 4).start()
    ctx_in[me] = ctx[pl.ds(pl.multiple_of(me * 128, 128), 128), :]
    proj_gather[2]()
    weight_one[1]()
    weight_two[1]()
    weight_one[2]()
    weight_two[2]()

    def arrived(number, carry):
        source = (me + 1 + number) % 8
        pltpu.make_async_remote_copy(
            src_ref=ctx.at[pl.ds(0, 128)],
            dst_ref=ctx_in.at[source],
            send_sem=ctx_send.at[number],
            recv_sem=ctx_recv.at[source],
            device_id=member(source),
            device_id_type=MESH,
        ).wait()
        return carry

    lax.fori_loop(0, 7, arrived, 0)
    text_spread[0][0]()
    proj_gather[3]()
    weight_one[3]()
    weight_two[3]()
    resid = patches_ref[pl.ds(me * 128, 128), :].astype(jnp.float32) + proj_bias
    for number in range(8):
        resid = resid + jnp.dot(ctx_in[number], proj_all[number], preferred_element_type=jnp.float32)
    settled = norm(resid, merge_gain, merge_shift)
    for tile in range(VW // HEAD):
        lines[tile] = settled[:, tile * HEAD : (tile + 1) * HEAD]
    for number in range(4):
        picked = [lines[tile, pl.ds(number, 32, stride=4), :] for tile in range(VW // HEAD)]
        merge_in[number, pl.ds(me * 32, 32), :] = jnp.concatenate(picked, axis=1).astype(jnp.bfloat16)
    merge_gather[0]()
    load_merge.wait()
    merge_gather[1]()
    weight_one[4]()
    weight_two[4]()
    merge_gather[2]()
    text_spread[0][1]()
    text_spread[1][0]()
    first = start_ref[0] - seq * SECTION
    spot = lax.broadcasted_iota(jnp.int32, (SECTION, 256), 0) - first
    slot = lax.broadcasted_iota(jnp.int32, (SECTION, 256), 1)
    pick = ((spot == slot) & (slot < count_ref[0] // 4)).astype(jnp.float32).astype(jnp.bfloat16)
    merge_gather[3]()
    spot = lax.broadcasted_iota(jnp.int32, (SECTION, 512), 0) - first
    inside = (spot >= 0) & (spot < count_ref[0] // 4)

    def merge(number):
        columns = pl.ds(pl.multiple_of(number * 256, 256), 256)
        token = rows_ref[6:7, columns]
        for part in range(4):
            token = token + jnp.dot(
                merge_in[part], merge_w[pl.ds(part * VW, VW), columns], preferred_element_type=jnp.float32
            )
        return token.astype(jnp.bfloat16)

    for n in range(2):
        tok_give[n] = merge(2 * n + 1 - img)
        tok[me, n] = merge(2 * n + img)
        token_spread[n][0]()
    squares[...] = jnp.zeros_like(squares)
    total[...] = jnp.zeros_like(total)
    weight_one[5]()
    weight_two[5]()

    def weigh(chunk):
        token = jnp.concatenate([tok[chunk, 0], tok[chunk, 1]], axis=1)
        placed = jnp.dot(pick, token, preferred_element_type=jnp.float32)
        words = text[chunk // 2, :, :, pl.ds(pl.multiple_of((chunk % 2) * 512, 512), 512)]
        values = jnp.where(inside, placed, words.reshape(SECTION, 512).astype(jnp.float32))
        gains = [rows_ref[pl.ds(8 + chunk, 1), pl.ds(pl.multiple_of(512 * n + img * 256, 256), 256)] for n in range(2)]
        scaled = (values * jnp.concatenate(gains, axis=1)).astype(jnp.bfloat16)
        folded = jnp.zeros((SECTION, HEAD), jnp.float32)
        for number in range(4):
            piece = values[:, number * HEAD : (number + 1) * HEAD]
            folded = folded + piece * piece
        w = weight[chunk // 2, pl.ds((chunk % 2) * 2, 2)].reshape(512, 10 * HEAD)
        total[...] += jnp.dot(scaled, w, preferred_element_type=jnp.float32)
        squares[...] += folded

    text_spread[0][2]()
    text_spread[1][1]()
    token_spread[0][1]()
    token_spread[1][1]()
    text_spread[1][2]()
    weight_one[6]()
    weight_two[6]()

    def ours(number, carry):
        weigh(order((y + number) % 4, core))
        return carry

    def theirs(number, carry):
        weigh(order((y + number) % 4, 1 - core))
        return carry

    lax.fori_loop(0, 4, ours, 0)
    token_spread[0][2]()
    token_spread[1][2]()
    lax.fori_loop(0, 4, theirs, 0)

    def taken(side, size, start):
        return total[:, pl.ds(pl.multiple_of(start + side * size, HEAD), size)]

    part_out[:, : 4 * HEAD] = taken(1 - img, 4 * HEAD, 0).astype(jnp.bfloat16)
    part_out[:, 4 * HEAD :] = taken(1 - img, HEAD, 8 * HEAD).astype(jnp.bfloat16)
    sums[0] = jnp.sum(squares[...].T, axis=0, keepdims=True) + jnp.zeros((8, SECTION), jnp.float32)
    for c in trade:
        c.start()
    gather_one = grid_gather(
        copy, 90,
        lambda a, b: buf.at[img, a, b],
        lambda a, b, h: buf.at[img, a, b, pl.ds(HALF * h, HALF)],
        x, z, ways[0], ways[1],
    )
    gather_two = grid_gather(
        copy, 110,
        lambda a, b: buf.at[1 - img, b, a],
        lambda a, b, h: buf.at[1 - img, b, a, pl.ds(HALF * h, HALF)],
        z, x, ways[0][::-1], ways[1][::-1],
    )
    top[...] = jnp.full_like(top, MASKED)
    acc[...] = jnp.zeros_like(acc)
    trade[0].wait()
    mean = (sums[0, 0:1] + sums[1, 0:1]) * (1.0 / 8192)
    scale = (lax.rsqrt(mean + EPSILON) + jnp.zeros((HEAD, SECTION), jnp.float32)).T
    cosine, sine = turn_ref[:, :HEAD], turn_ref[:, HEAD:]

    def settle(mine, number):
        columns = slice(HEAD * number, HEAD * number + HEAD)
        head = (mine + part_in[:, columns].astype(jnp.float32)) * scale + rows_ref[7:8, columns]
        return head, head * cosine + pltpu.roll(head, HEAD // 2, 1) * sine

    trade[1].wait()
    plain, turned = settle(taken(img, HEAD, 8 * HEAD), OWN_HEADS)
    columns = [turned[n * HEAD : (n + 1) * HEAD].T for n in range(SECTION // HEAD)]
    buf[img, x, z] = jnp.where(img == 0, jnp.concatenate(columns, axis=0), plain).astype(jnp.bfloat16)
    swap = copy(buf.at[img, x, z], buf.at[img, x, z], 88, other)
    swap.start()
    gather_one[0]()
    trade[2].wait()
    heads = [settle(taken(img, 4 * HEAD, 0)[:, n * HEAD : n * HEAD + HEAD], n)[1].astype(jnp.bfloat16) for n in range(4)]
    for n in range(2):
        lent[:, n * HEAD : n * HEAD + HEAD] = heads[2 + n]
        query[pl.ds(n * SECTION, SECTION), :] = heads[n]
    lend = copy(lent, guest, 89, {"seq": mirror})
    lend.start()
    rows_all = 2 * SECTION
    ones = jnp.ones((SECTION, HEAD), jnp.bfloat16)
    tiles = SECTION // HEAD

    def block(group, number, masked):
        rows = pl.ds(pl.multiple_of(group * rows_all, rows_all), rows_all)
        a, b = number // 4, number % 4
        keys = jnp.concatenate([buf[0, a, b, n * HEAD : (n + 1) * HEAD] for n in range(tiles)], axis=1)
        values = jnp.concatenate([buf[1, a, b], ones], axis=1)
        scores = jnp.dot(query[rows, :], keys, preferred_element_type=jnp.float32)
        scores = scores * (HEAD ** (-0.5) * LOG2E)
        if masked:
            row = lax.broadcasted_iota(jnp.int32, (rows_all, SECTION), 0) % SECTION
            col = lax.broadcasted_iota(jnp.int32, (rows_all, SECTION), 1)
            scores = jnp.where(col <= row, scores, MASKED)
        old = top[rows, :]
        new = jnp.maximum(old, jnp.max(scores, axis=-1, keepdims=True))
        factor = jnp.exp2(old - new)
        weights = [jnp.exp2(scores[:, n * HEAD : (n + 1) * HEAD] - new) for n in range(tiles)]
        weights = jnp.concatenate(weights, axis=1).astype(jnp.bfloat16)
        product = jnp.dot(weights, values, preferred_element_type=jnp.float32)
        top[rows, :] = new
        acc[rows, :] = acc[rows, :] * jnp.concatenate([factor, factor], axis=1) + product

    def visit(group, dx, dz):
        number = ((x + dx) % 4) * 4 + (z + dz) % 4

        @pl.when(number < group * mirror + (1 - group) * seq)
        def _():
            block(group, number, False)

    def both(count, offset):
        def step(n, carry):
            visit(n % 2, *offset(n // 2))
            return carry

        lax.fori_loop(0, 2 * count, step, 0)

    def ending(group):
        def across(n, carry):
            visit(group, 2, n)
            return carry

        def along(n, carry):
            visit(group, n * (n + 1) // 2, 2)
            return carry

        lax.fori_loop(0, 4, across, 0)
        lax.fori_loop(0, 3, along, 0)

    def finish(group):
        parts = []
        for head in range(2):
            total = acc[pl.ds(group * rows_all + head * SECTION, SECTION), :]
            parts.append((total[:, :HEAD] / total[:, HEAD:]).astype(jnp.bfloat16))
        return jnp.concatenate(parts, axis=1)

    swap.wait()
    gather_two[0]()
    block(0, seq, True)
    gather_one[1]()
    gather_two[1]()
    gather_one[2]()
    gather_two[2]()
    lend.wait()
    for head in range(2):
        query[pl.ds(rows_all + head * SECTION, SECTION), :] = guest[:, head * HEAD : (head + 1) * HEAD]
    visit(1, 0, 0)
    both(2, lambda n: (1 + 2 * n, 0))
    gather_one[3]()
    gather_two[3]()
    both(2, lambda n: (0, 1 + 2 * n))
    gather_one[4]()
    gather_two[4]()
    block(1, mirror, True)
    gather_one[5]()
    gather_two[5]()
    both(4, lambda n: (1 + 2 * (n // 2), 1 + 2 * (n % 2)))
    gather_one[6]()
    gather_two[6]()
    ending(1)
    away[...] = finish(1)
    to_mirror = [
        remote(
            away.at[pl.ds(HALF * n, HALF)],
            out_ref.at[:, pl.ds(pl.multiple_of(img * 2 * two + two, two), two)],
            130 + n, 130 + img, {"seq": mirror, "img": n},
        )
        for n in range(2)
    ]
    for c in to_mirror:
        c.start()
    ending(0)
    home[...] = finish(0)
    columns = pl.ds(pl.multiple_of(img * 2 * two, two), two)
    back = copy(home.at[pl.ds(pl.multiple_of((1 - img) * HALF, HALF), HALF)], out_ref.at[:, columns], 132, other)
    back.start()
    out_ref[:, columns] = home[pl.ds(pl.multiple_of(img * HALF, HALF), HALF), :]
    for n in range(2):
        to_mirror[n].wait_send()
        remote(
            away.at[pl.ds(HALF * n, HALF)],
            out_ref.at[:, pl.ds(n * 2 * two + two, two)],
            130 + n, 130 + n, {"seq": mirror, "img": n},
        ).wait_recv()
    back.wait()


def encode(count, start, patches, rows, turn, qkv, proj, merge_weight, text, part):
    vmem = pl.BlockSpec(memory_space=pltpu.VMEM)
    hbm = pl.BlockSpec(memory_space=pl.ANY)
    smem = pl.BlockSpec(memory_space=pltpu.SMEM)
    bf16, f32 = jnp.bfloat16, jnp.float32
    return pl.pallas_call(
        vision_kernel,
        out_shape=jax.ShapeDtypeStruct((HALF, 2 * OWN_HEADS * HEAD), bf16),
        in_specs=[smem] * 2 + [vmem] * 5 + [hbm] * 3,
        out_specs=vmem,
        scratch_shapes=[
            pltpu.VMEM((VW, 6 * HEAD), bf16),
            pltpu.VMEM((PATCH_CAP, 6 * HEAD), bf16),
            pltpu.VMEM((2, HEAD, PATCH_CAP), bf16),
            pltpu.VMEM((PATCH_CAP, 2 * HEAD), bf16),
            pltpu.VMEM((8, 128, 2 * HEAD), bf16),
            pltpu.VMEM((8, 256, VW), bf16),
            pltpu.VMEM((4 * VW, 1024), bf16),
            pltpu.VMEM((VW // HEAD, 128, HEAD), f32),
            pltpu.VMEM((4, 256, VW), bf16),
            pltpu.VMEM((4, 4, 256, 10 * HEAD), bf16),
            pltpu.VMEM((256, 1024), bf16),
            pltpu.VMEM((4, 2, 256, 1024), bf16),
            pltpu.VMEM((2, 256, 256), bf16),
            pltpu.VMEM((8, 2, 256, 256), bf16),
            pltpu.VMEM((SECTION, 10 * HEAD), f32),
            pltpu.VMEM((SECTION, HEAD), f32),
            pltpu.VMEM((2, 8, SECTION), f32),
            pltpu.VMEM((SECTION, 5 * HEAD), bf16),
            pltpu.VMEM((SECTION, 5 * HEAD), bf16),
            pltpu.VMEM((2, 4, 4, SECTION, HEAD), bf16),
            pltpu.VMEM((SECTION, 2 * HEAD), bf16),
            pltpu.VMEM((4 * SECTION, HEAD), f32),
            pltpu.VMEM((4 * SECTION, 2 * HEAD), f32),
            pltpu.SemaphoreType.DMA((134,)),
            pltpu.SemaphoreType.DMA((134,)),
            pltpu.SemaphoreType.DMA((7,)),
            pltpu.SemaphoreType.DMA((8,)),
            pltpu.SemaphoreType.DMA((10,)),
        ],
        compiler_params=pltpu.CompilerParams(
            collective_id=1, has_side_effects=True, vmem_limit_bytes=62 * 1024 * 1024
        ),
    )(count, start, patches, rows, turn, qkv, proj, merge_weight, text, part)


def on_device(
    patches, patch_counts, image_offsets, vision_gain, vision_shift, vision_qkv, vision_qkv_bias,
    vision_proj, vision_proj_bias, merge_gain, merge_shift, merge_weight, merge_bias, text_embed,
    norm_gain, qkv_weight, qkv_bias,
):
    img = lax.axis_index("img")
    wide_q = OWN_HEADS * HEAD
    f32 = jnp.float32

    def line(array):
        return jnp.pad(array.astype(f32), (0, VW - array.shape[0]))[None]

    first_bias = jnp.concatenate([qkv_bias[:wide_q], qkv_bias[2 * wide_q : 2 * wide_q + HEAD]])
    second_bias = jnp.concatenate([qkv_bias[wide_q : 2 * wide_q], qkv_bias[2 * wide_q + HEAD :]])
    own_bias = jnp.where(img == 0, first_bias, second_bias)
    singles = [
        vision_gain, vision_shift, vision_proj_bias, merge_gain, merge_shift, vision_qkv_bias, merge_bias, own_bias,
    ]
    gains = jnp.pad(norm_gain.astype(f32).reshape(8, 1024), ((0, 0), (0, VW - 1024)))
    lines = jnp.concatenate([line(array) for array in singles] + [gains], axis=0)
    positions = lax.axis_index("seq") * SECTION + jnp.arange(SECTION, dtype=jnp.int32)
    cosine, sine = rotation(positions)
    turn = jnp.concatenate([cosine, cosine, -sine, sine], axis=1)
    return encode(
        patch_counts, image_offsets, patches[0], lines, turn, vision_qkv, vision_proj, merge_weight, text_embed,
        qkv_weight,
    )


def solution(mesh):
    placed = (
        P("seq", None, None),
        P("seq"),
        P("seq"),
        P(),
        P(),
        P(None, ("tp", "img")),
        P(("tp", "img")),
        P(("tp", "img"), None),
        P(),
        P(),
        P(),
        P(None, ("tp", "img")),
        P(("tp", "img")),
        P(("seq", "img"), "tp"),
        P(),
        P(("seq", "img"), "tp"),
        P("tp"),
    )
    return jax.shard_map(
        on_device, mesh=mesh, in_specs=placed, out_specs=P(("seq", "img"), "tp"), check_vma=False
    )
```

```python
import functools

import jax
import jax.numpy as jnp
from jax import lax
from jax.experimental import pallas as pl
from jax.experimental.pallas import tpu as pltpu
from jax.sharding import PartitionSpec as P

HEAD = 128
VW = 1280
PATCH_CAP = 1024
GROUP = 8
VHEAD = 80
SECTION = 512
HALF = 256
OWN_HEADS = 4

EPSILON = 1e-06
THETA = 1000000.0
MASKED = -1e30
LOG2E = 1.4426950408889634
MESH = pl.DeviceIdType.MESH


def rotation(positions):
    halfway = HEAD // 2
    frequency = jnp.power(jnp.float32(THETA), -(jnp.arange(halfway, dtype=jnp.float32) * 2.0) / HEAD)
    angles = positions.astype(jnp.float32)[:, None] * frequency[None, :]
    return jnp.cos(angles), jnp.sin(angles)


def grid_gather(copy, base, block, part, first, second, ahead, behind):
    before, after, far = (first + 3) % 4, (first + 1) % 4, (first + 2) % 4
    low, high = (second + 3) % 4, (second + 1) % 4

    def whole(number, a, way):
        return copy(block(a, second), block(a, second), base + number, way)

    def half(number, a, b, h, way):
        return copy(part(a, b, h), part(a, b, h), base + number, way)

    up, down = whole(0, first, ahead[0]), whole(1, first, behind[0])
    pass_up = half(2, before, second, 0, ahead[0])
    pass_down = half(3, after, second, 1, behind[0])
    columns = (first, before, after, far)
    over = [(whole(4 + 2 * n, a, ahead[1]), whole(5 + 2 * n, a, behind[1])) for n, a in enumerate(columns)]
    on = [
        (half(12 + 2 * n, a, low, 0, ahead[1]), half(13 + 2 * n, a, high, 1, behind[1]))
        for n, a in enumerate(columns)
    ]

    def spread(n):
        over[n][0].start()
        over[n][1].start()

    def relay(n):
        over[n][0].wait_recv()
        on[n][0].start()
        over[n][1].wait_recv()
        on[n][1].start()

    def begin():
        up.start()
        down.start()
        spread(0)

    def turn():
        up.wait_recv()
        pass_up.start()
        spread(1)
        down.wait_recv()
        pass_down.start()
        spread(2)

    def near():
        relay(0)

    def turned():
        pass_up.wait_recv()
        pass_down.wait_recv()
        spread(3)

    def middle():
        relay(1)
        relay(2)

    def last():
        relay(3)

    def done():
        for c in on:
            c[0].wait_recv()
            c[1].wait_recv()
        for c in [(up, down), (pass_up, pass_down)] + over + on:
            c[0].wait_send()
            c[1].wait_send()

    return begin, turn, near, turned, middle, last, done


def column_gather(copy, base, slot, part, y, core, device):
    before, after, far = (y + 3) % 4, (y + 1) % 4, (y + 2) % 4
    ahead, behind, sibling = device(after, core), device(before, core), device(y, 1 - core)
    own = slot(y, core)
    share = copy(own, own, base, sibling)
    send_up = copy(own, own, base + 1, ahead)
    send_down = copy(own, own, base + 2, behind)
    low, high = part(before, core, 0), part(after, core, 1)
    pass_up = copy(low, low, base + 3, ahead)
    pass_down = copy(high, high, base + 4, behind)
    left, right = slot(before, core), slot(after, core)
    give_left = copy(left, left, base + 5, sibling)
    give_right = copy(right, right, base + 6, sibling)
    far_low, far_high = part(far, core, 0), part(far, core, 1)
    give_low = copy(far_low, far_low, base + 7, sibling)
    give_high = copy(far_high, far_high, base + 8, sibling)

    def start():
        send_up.start()
        send_down.start()
        share.start()

    def turn():
        send_up.wait_recv()
        pass_up.start()
        give_left.start()
        send_down.wait_recv()
        pass_down.start()
        give_right.start()

    def last():
        pass_up.wait_recv()
        give_low.start()
        pass_down.wait_recv()
        give_high.start()

    def done():
        for c in (share, give_left, give_right, give_low, give_high):
            c.wait_recv()
        for c in (share, send_up, send_down, pass_up, pass_down, give_left, give_right, give_low, give_high):
            c.wait_send()

    return start, turn, last, done


def plane_spread(copy, base, give, slot, y, core, device):
    mate = y + 1 - 2 * (y % 2)
    straight = (y + 2) % 4
    across = straight + 1 - 2 * (straight % 2)
    own, sibling = slot(y, core), device(y, 1 - core)

    def send(src, number, peer):
        return copy(src, own, base + number, peer)

    share, near = send(own, 0, sibling), send(own, 1, device(mate, core))
    far, close = send(give, 2, device(straight, core)), send(give, 3, device(across, core))
    relays = [copy(slot(a, core), slot(a, core), base + 4 + n, sibling) for n, a in enumerate((mate, across, straight))]

    def start():
        near.start()
        close.start()
        far.start()
        share.start()

    def turn():
        for c, relay in zip((near, close, far), relays):
            c.wait_recv()
            relay.start()

    def done():
        for c in [share] + relays:
            c.wait_recv()
        for c in [share, near, far, close] + relays:
            c.wait_send()

    return start, turn, done


def vision_kernel(
    count_ref, start_ref, patches_ref, gain_ref, shift_ref, proj_bias_ref, merge_gain_ref, merge_shift_ref,
    qkv_bias_ref, merge_bias_ref, norm_ref, bias_ref, cos_ref, sin_ref, qkv_ref, proj_ref, merge_ref, text_ref,
    part_ref, out_ref,
    rows_ref, wide, mixed, flipped, ctx, ctx_in, proj_all, merge_w, lines, merge_in, weight, text_give, text, tok_give, tok,
    total, squares, sums, part_out, part_in, buf, guest, top, acc,
    send, recv, ctx_send, ctx_recv, local,
):
    seq = lax.axis_index("seq")
    tp = lax.axis_index("tp")
    img = lax.axis_index("img")
    x, z = seq // 4, seq % 4
    core, y = tp % 2, img * 2 + tp // 2
    me = tp * 2 + img
    singles = (gain_ref, shift_ref, proj_bias_ref, merge_gain_ref, merge_shift_ref, qkv_bias_ref, merge_bias_ref)
    for n, ref in enumerate(singles):
        rows_ref[n : n + 1, : ref.shape[0]] = ref[...].astype(jnp.float32)[None, :]
    bias_row = bias_ref[...].astype(jnp.float32)[None, :]
    q_bias = jnp.where(img == 0, bias_row[:, : 4 * HEAD], bias_row[:, 4 * HEAD : 8 * HEAD])
    kv_bias = jnp.where(img == 0, bias_row[:, 8 * HEAD : 9 * HEAD], bias_row[:, 9 * HEAD :])
    rows_ref[7:8, : 5 * HEAD] = jnp.concatenate([q_bias, kv_bias], axis=1)
    norm_row = norm_ref[...].astype(jnp.float32)[None, :]
    for n in range(8):
        rows_ref[8 + n : 9 + n, :1024] = norm_row[:, n * 1024 : (n + 1) * 1024]
    gain, shift, proj_bias, merge_gain, merge_shift = [rows_ref[n : n + 1, :] for n in range(5)]

    def device(y_at, core_at):
        return {"tp": 2 * (y_at % 2) + core_at, "img": y_at // 2}

    def order(y_at, core_at):
        return (2 * (y_at % 2) + core_at) * 2 + y_at // 2

    def along_x(d):
        return {"seq": ((x + d) % 4) * 4 + z}

    def along_z(d):
        return {"seq": x * 4 + (z + d) % 4}

    def member(index):
        return {"tp": index // 2, "img": index % 2}

    peers = [member((me + d) % 8) for d in range(1, 8)]
    mirror = 15 - seq
    peers += [along_x(1), along_x(3), along_z(1), along_z(3), {"seq": mirror}, {"seq": mirror, "img": 1 - img}]
    barrier = pltpu.get_barrier_semaphore()
    for peer in peers:
        pl.semaphore_signal(barrier, inc=1, device_id=peer, device_id_type=MESH)
    load_merge = pltpu.make_async_copy(merge_ref, merge_w, local.at[0])
    load_merge.start()
    load_weight = pltpu.make_async_copy(part_ref, weight.at[x, z], local.at[1])
    load_weight.start()
    load_text = []
    for n in range(4):
        columns = pl.ds(256 * n, 256)
        for parity, target in ((1 - img, text_give.at[:, columns]), (img, text.at[tp, img, :, columns])):
            at = pl.ds(pl.multiple_of((2 * n + parity) * 256, 256), 256)
            load_text.append(pltpu.make_async_copy(text_ref.at[:, at], target, local.at[2 + len(load_text)]))
    for c in load_text:
        c.start()
    proj_all[:, 2 * VHEAD :, :] = jnp.zeros((8, 256 - 2 * VHEAD, VW), jnp.bfloat16)
    proj_all[me, : 2 * VHEAD, :] = proj_ref[...]
    pl.semaphore_wait(barrier, len(peers))

    def remote(src, dst, out, into, peer):
        return pltpu.make_async_remote_copy(
            src_ref=src,
            dst_ref=dst,
            send_sem=send.at[out],
            recv_sem=recv.at[into],
            device_id=peer,
            device_id_type=MESH,
        )

    def copy(src, dst, number, peer):
        return remote(src, dst, number, number, peer)

    proj_gather = column_gather(
        copy, 0,
        lambda a, b: proj_all.at[order(a, b), pl.ds(0, 160)],
        lambda a, b, h: proj_all.at[order(a, b), pl.ds(80 * h, 80)],
        y, core, device,
    )
    merge_gather = column_gather(
        copy, 9,
        lambda a, b: merge_in.at[:, pl.ds(order(a, b) * 32, 32)],
        lambda a, b, h: merge_in.at[pl.ds(2 * h, 2), pl.ds(order(a, b) * 32, 32)],
        y, core, device,
    )
    text_spread = [
        plane_spread(
            copy, 18 + 7 * n, text_give.at[pl.ds(128 * n, 128)],
            lambda a, b, n=n: text.at[2 * (a % 2) + b, a // 2, pl.ds(128 * n, 128)],
            y, core, device,
        )
        for n in range(2)
    ]
    token_spread = [
        plane_spread(copy, 32 + 7 * n, tok_give.at[n], lambda a, b, n=n: tok.at[order(a, b), n], y, core, device)
        for n in range(2)
    ]
    other = {"img": 1 - img}
    quarter, fifth = pl.ds(0, 4 * HEAD), pl.ds(4 * HEAD, HEAD)
    trade = [
        copy(sums.at[0], sums.at[1], 47, other),
        copy(part_out.at[:, fifth], part_in.at[:, fifth], 46, other),
        copy(part_out.at[:, quarter], part_in.at[:, quarter], 133, other),
    ]
    two = 2 * HEAD
    query = merge_w.at[pl.ds(0, 4 * SECTION), pl.ds(0, HEAD)]
    lent = merge_w.at[pl.ds(0, SECTION), pl.ds(HEAD, two)]
    away = merge_w.at[pl.ds(0, SECTION), pl.ds(HEAD + two, two)]
    home = merge_w.at[pl.ds(0, SECTION), pl.ds(HEAD + 2 * two, two)]
    ways = (along_x(1), along_z(1)), (along_x(3), along_z(3))
    weight_one = grid_gather(
        copy, 48,
        lambda a, b: weight.at[a, b, pl.ds(0, 128)],
        lambda a, b, h: weight.at[a, b, pl.ds(64 * h, 64)],
        x, z, ways[0], ways[1],
    )
    weight_two = grid_gather(
        copy, 68,
        lambda a, b: weight.at[b, a, pl.ds(128, 128)],
        lambda a, b, h: weight.at[b, a, pl.ds(128 + 64 * h, 64)],
        z, x, ways[0][::-1], ways[1][::-1],
    )

    proj_gather[0]()
    load_weight.wait()
    weight_one[0]()
    weight_two[0]()

    def norm(source, scaling, shifting):
        average = jnp.mean(source, axis=-1, keepdims=True)
        centred = source - average
        spread = jnp.mean(centred * centred, axis=-1, keepdims=True)
        return centred * lax.rsqrt(spread + EPSILON) * scaling + shifting

    old = lax.broadcasted_iota(jnp.int32, (6 * VHEAD, 6 * HEAD), 0)
    new = lax.broadcasted_iota(jnp.int32, (6 * VHEAD, 6 * HEAD), 1)
    place = ((old // VHEAD == new // HEAD) & (old % VHEAD == new % HEAD)).astype(jnp.float32).astype(jnp.bfloat16)
    wide[...] = lax.dot_general(
        qkv_ref[...], place, (((0,), (0,)), ((), ())), preferred_element_type=jnp.float32
    ).astype(jnp.bfloat16)
    bias = jnp.dot(
        rows_ref[5:6, : 6 * VHEAD].astype(jnp.bfloat16), place, preferred_element_type=jnp.float32
    )
    column = lax.broadcasted_iota(jnp.int32, (1, 6 * HEAD), 1)
    bias = bias + ((column % HEAD == VHEAD) & ((column // HEAD) % 3 == 2)).astype(jnp.float32)

    def mix(number, carry):
        rows = pl.ds(pl.multiple_of(number * 512, 512), 512)
        normed = norm(patches_ref[rows, :].astype(jnp.float32), gain, shift)
        product = jnp.dot(normed.astype(jnp.bfloat16), wide[...], preferred_element_type=jnp.float32) + bias
        mixed[rows, :] = product.astype(jnp.bfloat16)
        for head in range(2):
            keys = product[:, 384 * head + 128 : 384 * head + 256].T
            flipped[head, :, rows] = keys.astype(jnp.bfloat16)
        return carry

    lax.fori_loop(0, 2, mix, 0)
    for c in load_text:
        c.wait()
    valid = lax.broadcasted_iota(jnp.int32, (512, PATCH_CAP), 1) < count_ref[0]
    lane = lax.broadcasted_iota(jnp.int32, (512, HEAD), 1)

    def look(number):
        rows = pl.ds(pl.multiple_of(number * 512, 512), 512)
        parts = []
        for head in range(2):
            query = mixed[rows, 384 * head : 384 * head + 128]
            values = mixed[:, 384 * head + 256 : 384 * head + 384]
            scores = jnp.dot(query, flipped[head], preferred_element_type=jnp.float32)
            scores = jnp.where(valid, scores * (VHEAD ** (-0.5) * LOG2E), MASKED)
            best = jnp.max(scores, axis=-1, keepdims=True) + jnp.zeros((512, HEAD), jnp.float32)
            weights = [jnp.exp2(scores[:, n * HEAD : (n + 1) * HEAD] - best) for n in range(8)]
            weights = jnp.concatenate(weights, axis=1).astype(jnp.bfloat16)
            product = jnp.dot(weights, values, preferred_element_type=jnp.float32)
            parts.append(product / product[:, VHEAD : VHEAD + 1])
        turned = pltpu.roll(parts[1], VHEAD, 1)
        ctx[rows, :HEAD] = jnp.where(lane < VHEAD, parts[0], turned).astype(jnp.bfloat16)
        ctx[rows, HEAD:] = jnp.where(lane < 2 * VHEAD - HEAD, turned, 0.0).astype(jnp.bfloat16)

    def ctx_copy(number, target):
        return pltpu.make_async_remote_copy(
            src_ref=ctx.at[pl.ds(pl.multiple_of(target * 128, 128), 128)],
            dst_ref=ctx_in.at[me],
            send_sem=ctx_send.at[number],
            recv_sem=ctx_recv.at[me],
            device_id=member(target),
            device_id_type=MESH,
        )

    side = me // 4
    look(1 - side)
    for n in range(4):
        ctx_copy(n, (1 - side) * 4 + n).start()
    proj_gather[1]()
    look(side)
    for n in range(3):
        ctx_copy(4 + n, side * 4 + (me + 1 + n) % 4).start()
    ctx_in[me] = ctx[pl.ds(pl.multiple_of(me * 128, 128), 128), :]
    proj_gather[2]()
    weight_one[1]()
    weight_two[1]()
    weight_one[2]()
    weight_two[2]()

    def arrived(number, carry):
        source = (me + 1 + number) % 8
        pltpu.make_async_remote_copy(
            src_ref=ctx.at[pl.ds(0, 128)],
            dst_ref=ctx_in.at[source],
            send_sem=ctx_send.at[number],
            recv_sem=ctx_recv.at[source],
            device_id=member(source),
            device_id_type=MESH,
        ).wait()
        return carry

    lax.fori_loop(0, 7, arrived, 0)
    text_spread[0][0]()
    proj_gather[3]()
    weight_one[3]()
    weight_two[3]()
    resid = patches_ref[pl.ds(me * 128, 128), :].astype(jnp.float32) + proj_bias
    for number in range(8):
        resid = resid + jnp.dot(ctx_in[number], proj_all[number], preferred_element_type=jnp.float32)
    settled = norm(resid, merge_gain, merge_shift)
    for tile in range(VW // HEAD):
        lines[tile] = settled[:, tile * HEAD : (tile + 1) * HEAD]
    for number in range(4):
        picked = [lines[tile, pl.ds(number, 32, stride=4), :] for tile in range(VW // HEAD)]
        merge_in[number, pl.ds(me * 32, 32), :] = jnp.concatenate(picked, axis=1).astype(jnp.bfloat16)
    merge_gather[0]()
    load_merge.wait()
    merge_gather[1]()
    weight_one[4]()
    weight_two[4]()
    merge_gather[2]()
    text_spread[0][1]()
    text_spread[1][0]()
    first = start_ref[0] - seq * SECTION
    spot = lax.broadcasted_iota(jnp.int32, (SECTION, 256), 0) - first
    slot = lax.broadcasted_iota(jnp.int32, (SECTION, 256), 1)
    pick = ((spot == slot) & (slot < count_ref[0] // 4)).astype(jnp.float32).astype(jnp.bfloat16)
    merge_gather[3]()
    spot = lax.broadcasted_iota(jnp.int32, (SECTION, 512), 0) - first
    inside = (spot >= 0) & (spot < count_ref[0] // 4)

    def merge(number):
        columns = pl.ds(pl.multiple_of(number * 256, 256), 256)
        token = rows_ref[6:7, columns]
        for part in range(4):
            token = token + jnp.dot(
                merge_in[part], merge_w[pl.ds(part * VW, VW), columns], preferred_element_type=jnp.float32
            )
        return token.astype(jnp.bfloat16)

    for n in range(2):
        tok_give[n] = merge(2 * n + 1 - img)
        tok[me, n] = merge(2 * n + img)
        token_spread[n][0]()
    squares[...] = jnp.zeros_like(squares)
    total[...] = jnp.zeros_like(total)
    weight_one[5]()
    weight_two[5]()

    def weigh(chunk):
        token = jnp.concatenate([tok[chunk, 0], tok[chunk, 1]], axis=1)
        placed = jnp.dot(pick, token, preferred_element_type=jnp.float32)
        words = text[chunk // 2, :, :, pl.ds(pl.multiple_of((chunk % 2) * 512, 512), 512)]
        values = jnp.where(inside, placed, words.reshape(SECTION, 512).astype(jnp.float32))
        gains = [rows_ref[pl.ds(8 + chunk, 1), pl.ds(pl.multiple_of(512 * n + img * 256, 256), 256)] for n in range(2)]
        scaled = (values * jnp.concatenate(gains, axis=1)).astype(jnp.bfloat16)
        folded = jnp.zeros((SECTION, HEAD), jnp.float32)
        for number in range(4):
            piece = values[:, number * HEAD : (number + 1) * HEAD]
            folded = folded + piece * piece
        w = weight[chunk // 2, pl.ds((chunk % 2) * 2, 2)].reshape(512, 10 * HEAD)
        total[...] += jnp.dot(scaled, w, preferred_element_type=jnp.float32)
        squares[...] += folded

    text_spread[0][2]()
    text_spread[1][1]()
    token_spread[0][1]()
    token_spread[1][1]()
    text_spread[1][2]()
    weight_one[6]()
    weight_two[6]()

    def ours(number, carry):
        weigh(order((y + number) % 4, core))
        return carry

    def theirs(number, carry):
        weigh(order((y + number) % 4, 1 - core))
        return carry

    lax.fori_loop(0, 4, ours, 0)
    token_spread[0][2]()
    token_spread[1][2]()
    lax.fori_loop(0, 4, theirs, 0)

    def taken(side, size, start):
        return total[:, pl.ds(pl.multiple_of(start + side * size, HEAD), size)]

    part_out[:, : 4 * HEAD] = taken(1 - img, 4 * HEAD, 0).astype(jnp.bfloat16)
    part_out[:, 4 * HEAD :] = taken(1 - img, HEAD, 8 * HEAD).astype(jnp.bfloat16)
    sums[0] = jnp.sum(squares[...].T, axis=0, keepdims=True) + jnp.zeros((8, SECTION), jnp.float32)
    for c in trade:
        c.start()
    gather_one = grid_gather(
        copy, 90,
        lambda a, b: buf.at[img, a, b],
        lambda a, b, h: buf.at[img, a, b, pl.ds(HALF * h, HALF)],
        x, z, ways[0], ways[1],
    )
    gather_two = grid_gather(
        copy, 110,
        lambda a, b: buf.at[1 - img, b, a],
        lambda a, b, h: buf.at[1 - img, b, a, pl.ds(HALF * h, HALF)],
        z, x, ways[0][::-1], ways[1][::-1],
    )
    top[...] = jnp.full_like(top, MASKED)
    acc[...] = jnp.zeros_like(acc)
    trade[0].wait()
    mean = (sums[0, 0:1] + sums[1, 0:1]) * (1.0 / 8192)
    scale = (lax.rsqrt(mean + EPSILON) + jnp.zeros((HEAD, SECTION), jnp.float32)).T
    cosine = jnp.concatenate([cos_ref[...], cos_ref[...]], axis=1)
    sine = jnp.concatenate([-sin_ref[...], sin_ref[...]], axis=1)

    def settle(mine, number):
        columns = slice(HEAD * number, HEAD * number + HEAD)
        head = (mine + part_in[:, columns].astype(jnp.float32)) * scale + rows_ref[7:8, columns]
        return head, head * cosine + pltpu.roll(head, HEAD // 2, 1) * sine

    trade[1].wait()
    plain, turned = settle(taken(img, HEAD, 8 * HEAD), OWN_HEADS)
    columns = [turned[n * HEAD : (n + 1) * HEAD].T for n in range(SECTION // HEAD)]
    buf[img, x, z] = jnp.where(img == 0, jnp.concatenate(columns, axis=0), plain).astype(jnp.bfloat16)
    swap = copy(buf.at[img, x, z], buf.at[img, x, z], 88, other)
    swap.start()
    gather_one[0]()
    trade[2].wait()
    heads = [settle(taken(img, 4 * HEAD, 0)[:, n * HEAD : n * HEAD + HEAD], n)[1].astype(jnp.bfloat16) for n in range(4)]
    for n in range(2):
        lent[:, n * HEAD : n * HEAD + HEAD] = heads[2 + n]
        query[pl.ds(n * SECTION, SECTION), :] = heads[n]
    lend = copy(lent, guest, 89, {"seq": mirror})
    lend.start()
    rows_all = 2 * SECTION
    ones = jnp.ones((SECTION, HEAD), jnp.bfloat16)
    tiles = SECTION // HEAD

    def block(group, number, masked):
        rows = pl.ds(pl.multiple_of(group * rows_all, rows_all), rows_all)
        a, b = number // 4, number % 4
        keys = jnp.concatenate([buf[0, a, b, n * HEAD : (n + 1) * HEAD] for n in range(tiles)], axis=1)
        values = jnp.concatenate([buf[1, a, b], ones], axis=1)
        scores = jnp.dot(query[rows, :], keys, preferred_element_type=jnp.float32)
        scores = scores * (HEAD ** (-0.5) * LOG2E)
        if masked:
            row = lax.broadcasted_iota(jnp.int32, (rows_all, SECTION), 0) % SECTION
            col = lax.broadcasted_iota(jnp.int32, (rows_all, SECTION), 1)
            scores = jnp.where(col <= row, scores, MASKED)
        old = top[rows, :]
        new = jnp.maximum(old, jnp.max(scores, axis=-1, keepdims=True))
        factor = jnp.exp2(old - new)
        weights = [jnp.exp2(scores[:, n * HEAD : (n + 1) * HEAD] - new) for n in range(tiles)]
        weights = jnp.concatenate(weights, axis=1).astype(jnp.bfloat16)
        product = jnp.dot(weights, values, preferred_element_type=jnp.float32)
        top[rows, :] = new
        acc[rows, :] = acc[rows, :] * jnp.concatenate([factor, factor], axis=1) + product

    def visit(group, dx, dz):
        number = ((x + dx) % 4) * 4 + (z + dz) % 4

        @pl.when(number < group * mirror + (1 - group) * seq)
        def _():
            block(group, number, False)

    def both(count, offset):
        def step(n, carry):
            visit(n % 2, *offset(n // 2))
            return carry

        lax.fori_loop(0, 2 * count, step, 0)

    def ending(group):
        def across(n, carry):
            visit(group, 2, n)
            return carry

        def along(n, carry):
            visit(group, n * (n + 1) // 2, 2)
            return carry

        lax.fori_loop(0, 4, across, 0)
        lax.fori_loop(0, 3, along, 0)

    def finish(group):
        parts = []
        for head in range(2):
            total = acc[pl.ds(group * rows_all + head * SECTION, SECTION), :]
            parts.append((total[:, :HEAD] / total[:, HEAD:]).astype(jnp.bfloat16))
        return jnp.concatenate(parts, axis=1)

    swap.wait()
    gather_two[0]()
    block(0, seq, True)
    gather_one[1]()
    gather_two[1]()
    gather_one[2]()
    gather_two[2]()
    lend.wait()
    for head in range(2):
        query[pl.ds(rows_all + head * SECTION, SECTION), :] = guest[:, head * HEAD : (head + 1) * HEAD]
    visit(1, 0, 0)
    both(2, lambda n: (1 + 2 * n, 0))
    gather_one[3]()
    gather_two[3]()
    both(2, lambda n: (0, 1 + 2 * n))
    gather_one[4]()
    gather_two[4]()
    block(1, mirror, True)
    gather_one[5]()
    gather_two[5]()
    both(4, lambda n: (1 + 2 * (n // 2), 1 + 2 * (n % 2)))
    gather_one[6]()
    gather_two[6]()
    ending(1)
    away[...] = finish(1)
    to_mirror = [
        remote(
            away.at[pl.ds(HALF * n, HALF)],
            out_ref.at[:, pl.ds(pl.multiple_of(img * 2 * two + two, two), two)],
            130 + n, 130 + img, {"seq": mirror, "img": n},
        )
        for n in range(2)
    ]
    for c in to_mirror:
        c.start()
    ending(0)
    home[...] = finish(0)
    columns = pl.ds(pl.multiple_of(img * 2 * two, two), two)
    back = copy(home.at[pl.ds(pl.multiple_of((1 - img) * HALF, HALF), HALF)], out_ref.at[:, columns], 132, other)
    back.start()
    out_ref[:, columns] = home[pl.ds(pl.multiple_of(img * HALF, HALF), HALF), :]
    for n in range(2):
        to_mirror[n].wait_send()
        remote(
            away.at[pl.ds(HALF * n, HALF)],
            out_ref.at[:, pl.ds(n * 2 * two + two, two)],
            130 + n, 130 + n, {"seq": mirror, "img": n},
        ).wait_recv()
    back.wait()


def encode(*operands):
    vmem = pl.BlockSpec(memory_space=pltpu.VMEM)
    hbm = pl.BlockSpec(memory_space=pl.ANY)
    smem = pl.BlockSpec(memory_space=pltpu.SMEM)
    bf16, f32 = jnp.bfloat16, jnp.float32
    return pl.pallas_call(
        vision_kernel,
        out_shape=jax.ShapeDtypeStruct((HALF, 2 * OWN_HEADS * HEAD), bf16),
        in_specs=[smem] * 2 + [vmem] * 14 + [hbm] * 3,
        out_specs=vmem,
        scratch_shapes=[
            pltpu.VMEM((16, VW), f32),
            pltpu.VMEM((VW, 6 * HEAD), bf16),
            pltpu.VMEM((PATCH_CAP, 6 * HEAD), bf16),
            pltpu.VMEM((2, HEAD, PATCH_CAP), bf16),
            pltpu.VMEM((PATCH_CAP, 2 * HEAD), bf16),
            pltpu.VMEM((8, 128, 2 * HEAD), bf16),
            pltpu.VMEM((8, 256, VW), bf16),
            pltpu.VMEM((4 * VW, 1024), bf16),
            pltpu.VMEM((VW // HEAD, 128, HEAD), f32),
            pltpu.VMEM((4, 256, VW), bf16),
            pltpu.VMEM((4, 4, 256, 10 * HEAD), bf16),
            pltpu.VMEM((256, 1024), bf16),
            pltpu.VMEM((4, 2, 256, 1024), bf16),
            pltpu.VMEM((2, 256, 256), bf16),
            pltpu.VMEM((8, 2, 256, 256), bf16),
            pltpu.VMEM((SECTION, 10 * HEAD), f32),
            pltpu.VMEM((SECTION, HEAD), f32),
            pltpu.VMEM((2, 8, SECTION), f32),
            pltpu.VMEM((SECTION, 5 * HEAD), bf16),
            pltpu.VMEM((SECTION, 5 * HEAD), bf16),
            pltpu.VMEM((2, 4, 4, SECTION, HEAD), bf16),
            pltpu.VMEM((SECTION, 2 * HEAD), bf16),
            pltpu.VMEM((4 * SECTION, HEAD), f32),
            pltpu.VMEM((4 * SECTION, 2 * HEAD), f32),
            pltpu.SemaphoreType.DMA((134,)),
            pltpu.SemaphoreType.DMA((134,)),
            pltpu.SemaphoreType.DMA((7,)),
            pltpu.SemaphoreType.DMA((8,)),
            pltpu.SemaphoreType.DMA((10,)),
        ],
        compiler_params=pltpu.CompilerParams(
            collective_id=1, has_side_effects=True, vmem_limit_bytes=62 * 1024 * 1024
        ),
    )(*operands)


def on_device(
    patches, patch_counts, image_offsets, vision_gain, vision_shift, vision_qkv, vision_qkv_bias,
    vision_proj, vision_proj_bias, merge_gain, merge_shift, merge_weight, merge_bias, text_embed,
    norm_gain, qkv_weight, qkv_bias,
):
    positions = lax.axis_index("seq") * SECTION + jnp.arange(SECTION, dtype=jnp.int32)
    cosine, sine = rotation(positions)
    return encode(
        patch_counts, image_offsets, patches[0], vision_gain, vision_shift, vision_proj_bias, merge_gain, merge_shift,
        vision_qkv_bias, merge_bias, norm_gain, qkv_bias, cosine, sine, vision_qkv.T, vision_proj, merge_weight,
        text_embed, qkv_weight,
    )


def solution(mesh):
    placed = (
        P("seq", None, None),
        P("seq"),
        P("seq"),
        P(),
        P(),
        P(None, ("tp", "img")),
        P(("tp", "img")),
        P(("tp", "img"), None),
        P(),
        P(),
        P(),
        P(None, ("tp", "img")),
        P(("tp", "img")),
        P(("seq", "img"), "tp"),
        P(),
        P(("seq", "img"), "tp"),
        P("tp"),
    )
    return jax.shard_map(
        on_device, mesh=mesh, in_specs=placed, out_specs=P(("seq", "img"), "tp"), check_vma=False
    )
```

```python
import functools

import jax
import jax.numpy as jnp
from jax import lax
from jax.experimental import pallas as pl
from jax.experimental.pallas import tpu as pltpu
from jax.sharding import PartitionSpec as P

HEAD = 128
VW = 1280
PATCH_CAP = 1024
GROUP = 8
VHEAD = 80
SECTION = 512
HALF = 256
OWN_HEADS = 4

EPSILON = 1e-06
THETA = 1000000.0
MASKED = -1e30
LOG2E = 1.4426950408889634
MESH = pl.DeviceIdType.MESH


def rotation(positions):
    halfway = HEAD // 2
    frequency = jnp.power(jnp.float32(THETA), -(jnp.arange(halfway, dtype=jnp.float32) * 2.0) / HEAD)
    angles = positions.astype(jnp.float32)[:, None] * frequency[None, :]
    return jnp.cos(angles), jnp.sin(angles)


def grid_gather(copy, base, block, part, first, second, ahead, behind):
    before, after, far = (first + 3) % 4, (first + 1) % 4, (first + 2) % 4
    low, high = (second + 3) % 4, (second + 1) % 4

    def whole(number, a, way):
        return copy(block(a, second), block(a, second), base + number, way)

    def half(number, a, b, h, way):
        return copy(part(a, b, h), part(a, b, h), base + number, way)

    up, down = whole(0, first, ahead[0]), whole(1, first, behind[0])
    pass_up = half(2, before, second, 0, ahead[0])
    pass_down = half(3, after, second, 1, behind[0])
    columns = (first, before, after, far)
    over = [(whole(4 + 2 * n, a, ahead[1]), whole(5 + 2 * n, a, behind[1])) for n, a in enumerate(columns)]
    on = [
        (half(12 + 2 * n, a, low, 0, ahead[1]), half(13 + 2 * n, a, high, 1, behind[1]))
        for n, a in enumerate(columns)
    ]

    def spread(n):
        over[n][0].start()
        over[n][1].start()

    def relay(n):
        over[n][0].wait_recv()
        on[n][0].start()
        over[n][1].wait_recv()
        on[n][1].start()

    def begin():
        up.start()
        down.start()
        spread(0)

    def turn():
        up.wait_recv()
        pass_up.start()
        spread(1)
        down.wait_recv()
        pass_down.start()
        spread(2)

    def near():
        relay(0)

    def turned():
        pass_up.wait_recv()
        pass_down.wait_recv()
        spread(3)

    def middle():
        relay(1)
        relay(2)

    def last():
        relay(3)

    def done():
        for c in on:
            c[0].wait_recv()
            c[1].wait_recv()
        for c in [(up, down), (pass_up, pass_down)] + over + on:
            c[0].wait_send()
            c[1].wait_send()

    return begin, turn, near, turned, middle, last, done


def column_gather(copy, base, slot, part, y, core, device):
    before, after, far = (y + 3) % 4, (y + 1) % 4, (y + 2) % 4
    ahead, behind, sibling = device(after, core), device(before, core), device(y, 1 - core)
    own = slot(y, core)
    share = copy(own, own, base, sibling)
    send_up = copy(own, own, base + 1, ahead)
    send_down = copy(own, own, base + 2, behind)
    low, high = part(before, core, 0), part(after, core, 1)
    pass_up = copy(low, low, base + 3, ahead)
    pass_down = copy(high, high, base + 4, behind)
    left, right = slot(before, core), slot(after, core)
    give_left = copy(left, left, base + 5, sibling)
    give_right = copy(right, right, base + 6, sibling)
    far_low, far_high = part(far, core, 0), part(far, core, 1)
    give_low = copy(far_low, far_low, base + 7, sibling)
    give_high = copy(far_high, far_high, base + 8, sibling)

    def start():
        send_up.start()
        send_down.start()
        share.start()

    def turn():
        send_up.wait_recv()
        pass_up.start()
        give_left.start()
        send_down.wait_recv()
        pass_down.start()
        give_right.start()

    def last():
        pass_up.wait_recv()
        give_low.start()
        pass_down.wait_recv()
        give_high.start()

    def done():
        for c in (share, give_left, give_right, give_low, give_high):
            c.wait_recv()
        for c in (share, send_up, send_down, pass_up, pass_down, give_left, give_right, give_low, give_high):
            c.wait_send()

    return start, turn, last, done


def plane_spread(copy, base, give, slot, y, core, device):
    mate = y + 1 - 2 * (y % 2)
    straight = (y + 2) % 4
    across = straight + 1 - 2 * (straight % 2)
    own, sibling = slot(y, core), device(y, 1 - core)

    def send(src, number, peer):
        return copy(src, own, base + number, peer)

    share, near = send(own, 0, sibling), send(own, 1, device(mate, core))
    far, close = send(give, 2, device(straight, core)), send(give, 3, device(across, core))
    relays = [copy(slot(a, core), slot(a, core), base + 4 + n, sibling) for n, a in enumerate((mate, across, straight))]

    def start():
        near.start()
        close.start()
        far.start()
        share.start()

    def turn():
        for c, relay in zip((near, close, far), relays):
            c.wait_recv()
            relay.start()

    def done():
        for c in [share] + relays:
            c.wait_recv()
        for c in [share, near, far, close] + relays:
            c.wait_send()

    return start, turn, done


def vision_kernel(
    count_ref, start_ref, patches_ref, gain_ref, shift_ref, proj_bias_ref, merge_gain_ref, merge_shift_ref,
    qkv_bias_ref, merge_bias_ref, norm_ref, bias_ref, cos_ref, sin_ref, qkv_ref, proj_ref, merge_ref, text_ref,
    part_ref, out_ref,
    rows_ref, wide, mixed, flipped, ctx, ctx_in, proj_all, merge_w, lines, merge_in, weight, text_give, text, tok_give, tok,
    total, squares, sums, part_out, part_in, buf, guest, top, acc,
    send, recv, ctx_send, ctx_recv, local,
):
    seq = lax.axis_index("seq")
    tp = lax.axis_index("tp")
    img = lax.axis_index("img")
    x, z = seq // 4, seq % 4
    core, y = tp % 2, img * 2 + tp // 2
    me = tp * 2 + img
    singles = (gain_ref, shift_ref, proj_bias_ref, merge_gain_ref, merge_shift_ref, qkv_bias_ref, merge_bias_ref)
    for n, ref in enumerate(singles):
        rows_ref[n : n + 1, : ref.shape[0]] = ref[...].astype(jnp.float32)[None, :]
    bias_row = bias_ref[...].astype(jnp.float32)[None, :]
    q_bias = jnp.where(img == 0, bias_row[:, : 4 * HEAD], bias_row[:, 4 * HEAD : 8 * HEAD])
    kv_bias = jnp.where(img == 0, bias_row[:, 8 * HEAD : 9 * HEAD], bias_row[:, 9 * HEAD :])
    rows_ref[7:8, : 5 * HEAD] = jnp.concatenate([q_bias, kv_bias], axis=1)
    norm_row = norm_ref[...].astype(jnp.float32)[None, :]
    for n in range(8):
        rows_ref[8 + n : 9 + n, :1024] = norm_row[:, n * 1024 : (n + 1) * 1024]
    gain, shift, proj_bias, merge_gain, merge_shift = [rows_ref[n : n + 1, :] for n in range(5)]

    def device(y_at, core_at):
        return {"tp": 2 * (y_at % 2) + core_at, "img": y_at // 2}

    def order(y_at, core_at):
        return (2 * (y_at % 2) + core_at) * 2 + y_at // 2

    def along_x(d):
        return {"seq": ((x + d) % 4) * 4 + z}

    def along_z(d):
        return {"seq": x * 4 + (z + d) % 4}

    def member(index):
        return {"tp": index // 2, "img": index % 2}

    peers = [member((me + d) % 8) for d in range(1, 8)]
    mirror = 15 - seq
    peers += [along_x(1), along_x(3), along_z(1), along_z(3), {"seq": mirror}, {"seq": mirror, "img": 1 - img}]
    barrier = pltpu.get_barrier_semaphore()
    for peer in peers:
        pl.semaphore_signal(barrier, inc=1, device_id=peer, device_id_type=MESH)
    load_merge = pltpu.make_async_copy(merge_ref, merge_w, local.at[0])
    load_merge.start()
    load_weight = pltpu.make_async_copy(part_ref, weight.at[x, z], local.at[1])
    load_weight.start()
    load_text = []
    for n in range(4):
        columns = pl.ds(256 * n, 256)
        for parity, target in ((1 - img, text_give.at[:, columns]), (img, text.at[tp, img, :, columns])):
            at = pl.ds(pl.multiple_of((2 * n + parity) * 256, 256), 256)
            load_text.append(pltpu.make_async_copy(text_ref.at[:, at], target, local.at[2 + len(load_text)]))
    for c in load_text:
        c.start()
    proj_all[:, 2 * VHEAD :, :] = jnp.zeros((8, 256 - 2 * VHEAD, VW), jnp.bfloat16)
    proj_all[me, : 2 * VHEAD, :] = proj_ref[...]
    pl.semaphore_wait(barrier, len(peers))

    def remote(src, dst, out, into, peer):
        return pltpu.make_async_remote_copy(
            src_ref=src,
            dst_ref=dst,
            send_sem=send.at[out],
            recv_sem=recv.at[into],
            device_id=peer,
            device_id_type=MESH,
        )

    def copy(src, dst, number, peer):
        return remote(src, dst, number, number, peer)

    proj_gather = column_gather(
        copy, 0,
        lambda a, b: proj_all.at[order(a, b), pl.ds(0, 160)],
        lambda a, b, h: proj_all.at[order(a, b), pl.ds(80 * h, 80)],
        y, core, device,
    )
    merge_gather = column_gather(
        copy, 9,
        lambda a, b: merge_in.at[:, pl.ds(order(a, b) * 32, 32)],
        lambda a, b, h: merge_in.at[pl.ds(2 * h, 2), pl.ds(order(a, b) * 32, 32)],
        y, core, device,
    )
    text_spread = [
        plane_spread(
            copy, 18 + 7 * n, text_give.at[pl.ds(128 * n, 128)],
            lambda a, b, n=n: text.at[2 * (a % 2) + b, a // 2, pl.ds(128 * n, 128)],
            y, core, device,
        )
        for n in range(2)
    ]
    token_spread = [
        plane_spread(copy, 32 + 7 * n, tok_give.at[n], lambda a, b, n=n: tok.at[order(a, b), n], y, core, device)
        for n in range(2)
    ]
    other = {"img": 1 - img}
    quarter, fifth = pl.ds(0, 4 * HEAD), pl.ds(4 * HEAD, HEAD)
    trade = [
        copy(sums.at[0], sums.at[1], 47, other),
        copy(part_out.at[:, fifth], part_in.at[:, fifth], 46, other),
        copy(part_out.at[:, quarter], part_in.at[:, quarter], 133, other),
    ]
    two = 2 * HEAD
    query = merge_w.at[pl.ds(0, 4 * SECTION), pl.ds(0, HEAD)]
    lent = merge_w.at[pl.ds(0, SECTION), pl.ds(HEAD, two)]
    away = merge_w.at[pl.ds(0, SECTION), pl.ds(HEAD + two, two)]
    home = merge_w.at[pl.ds(0, SECTION), pl.ds(HEAD + 2 * two, two)]
    ways = (along_x(1), along_z(1)), (along_x(3), along_z(3))
    weight_one = grid_gather(
        copy, 48,
        lambda a, b: weight.at[a, b, pl.ds(0, 128)],
        lambda a, b, h: weight.at[a, b, pl.ds(64 * h, 64)],
        x, z, ways[0], ways[1],
    )
    weight_two = grid_gather(
        copy, 68,
        lambda a, b: weight.at[b, a, pl.ds(128, 128)],
        lambda a, b, h: weight.at[b, a, pl.ds(128 + 64 * h, 64)],
        z, x, ways[0][::-1], ways[1][::-1],
    )

    proj_gather[0]()
    load_weight.wait()
    weight_one[0]()
    weight_two[0]()

    def norm(source, scaling, shifting):
        average = jnp.mean(source, axis=-1, keepdims=True)
        centred = source - average
        spread = jnp.mean(centred * centred, axis=-1, keepdims=True)
        return centred * lax.rsqrt(spread + EPSILON) * scaling + shifting

    old = lax.broadcasted_iota(jnp.int32, (6 * VHEAD, 6 * HEAD), 0)
    new = lax.broadcasted_iota(jnp.int32, (6 * VHEAD, 6 * HEAD), 1)
    place = ((old // VHEAD == new // HEAD) & (old % VHEAD == new % HEAD)).astype(jnp.float32).astype(jnp.bfloat16)
    wide[...] = lax.dot_general(
        qkv_ref[...], place, (((0,), (0,)), ((), ())), preferred_element_type=jnp.float32
    ).astype(jnp.bfloat16)
    bias = jnp.dot(
        rows_ref[5:6, : 6 * VHEAD].astype(jnp.bfloat16), place, preferred_element_type=jnp.float32
    )
    column = lax.broadcasted_iota(jnp.int32, (1, 6 * HEAD), 1)
    bias = bias + ((column % HEAD == VHEAD) & ((column // HEAD) % 3 == 2)).astype(jnp.float32)

    def mix(number, carry):
        rows = pl.ds(pl.multiple_of(number * 512, 512), 512)
        normed = norm(patches_ref[rows, :].astype(jnp.float32), gain, shift)
        product = jnp.dot(normed.astype(jnp.bfloat16), wide[...], preferred_element_type=jnp.float32) + bias
        mixed[rows, :] = product.astype(jnp.bfloat16)
        for head in range(2):
            keys = product[:, 384 * head + 128 : 384 * head + 256].T
            flipped[head, :, rows] = keys.astype(jnp.bfloat16)
        return carry

    lax.fori_loop(0, 2, mix, 0)
    for c in load_text:
        c.wait()
    valid = lax.broadcasted_iota(jnp.int32, (512, PATCH_CAP), 1) < count_ref[0]
    lane = lax.broadcasted_iota(jnp.int32, (512, HEAD), 1)

    def look(number):
        rows = pl.ds(pl.multiple_of(number * 512, 512), 512)
        parts = []
        for head in range(2):
            query = mixed[rows, 384 * head : 384 * head + 128]
            values = mixed[:, 384 * head + 256 : 384 * head + 384]
            scores = jnp.dot(query, flipped[head], preferred_element_type=jnp.float32)
            scores = jnp.where(valid, scores * (VHEAD ** (-0.5) * LOG2E), MASKED)
            best = jnp.max(scores, axis=-1, keepdims=True) + jnp.zeros((512, HEAD), jnp.float32)
            weights = [jnp.exp2(scores[:, n * HEAD : (n + 1) * HEAD] - best) for n in range(8)]
            weights = jnp.concatenate(weights, axis=1).astype(jnp.bfloat16)
            product = jnp.dot(weights, values, preferred_element_type=jnp.float32)
            parts.append(product / product[:, VHEAD : VHEAD + 1])
        turned = pltpu.roll(parts[1], VHEAD, 1)
        ctx[rows, :HEAD] = jnp.where(lane < VHEAD, parts[0], turned).astype(jnp.bfloat16)
        ctx[rows, HEAD:] = jnp.where(lane < 2 * VHEAD - HEAD, turned, 0.0).astype(jnp.bfloat16)

    def ctx_copy(number, target):
        return pltpu.make_async_remote_copy(
            src_ref=ctx.at[pl.ds(pl.multiple_of(target * 128, 128), 128)],
            dst_ref=ctx_in.at[me],
            send_sem=ctx_send.at[number],
            recv_sem=ctx_recv.at[me],
            device_id=member(target),
            device_id_type=MESH,
        )

    side = me // 4
    look(1 - side)
    for n in range(4):
        ctx_copy(n, (1 - side) * 4 + n).start()
    proj_gather[1]()
    look(side)
    for n in range(3):
        ctx_copy(4 + n, side * 4 + (me + 1 + n) % 4).start()
    ctx_in[me] = ctx[pl.ds(pl.multiple_of(me * 128, 128), 128), :]
    proj_gather[2]()
    weight_one[1]()
    weight_two[1]()
    weight_one[2]()
    weight_two[2]()

    def arrived(number, carry):
        source = (me + 1 + number) % 8
        pltpu.make_async_remote_copy(
            src_ref=ctx.at[pl.ds(0, 128)],
            dst_ref=ctx_in.at[source],
            send_sem=ctx_send.at[number],
            recv_sem=ctx_recv.at[source],
            device_id=member(source),
            device_id_type=MESH,
        ).wait()
        return carry

    lax.fori_loop(0, 7, arrived, 0)
    text_spread[0][0]()
    proj_gather[3]()
    weight_one[3]()
    weight_two[3]()
    resid = patches_ref[pl.ds(me * 128, 128), :].astype(jnp.float32) + proj_bias
    for number in range(8):
        resid = resid + jnp.dot(ctx_in[number], proj_all[number], preferred_element_type=jnp.float32)
    settled = norm(resid, merge_gain, merge_shift)
    for tile in range(VW // HEAD):
        lines[tile] = settled[:, tile * HEAD : (tile + 1) * HEAD]
    for number in range(4):
        picked = [lines[tile, pl.ds(number, 32, stride=4), :] for tile in range(VW // HEAD)]
        merge_in[number, pl.ds(me * 32, 32), :] = jnp.concatenate(picked, axis=1).astype(jnp.bfloat16)
    merge_gather[0]()
    load_merge.wait()
    merge_gather[1]()
    weight_one[4]()
    weight_two[4]()
    merge_gather[2]()
    text_spread[0][1]()
    text_spread[1][0]()
    first = start_ref[0] - seq * SECTION
    spot = lax.broadcasted_iota(jnp.int32, (SECTION, 256), 0) - first
    slot = lax.broadcasted_iota(jnp.int32, (SECTION, 256), 1)
    pick = ((spot == slot) & (slot < count_ref[0] // 4)).astype(jnp.float32).astype(jnp.bfloat16)
    merge_gather[3]()
    spot = lax.broadcasted_iota(jnp.int32, (SECTION, 512), 0) - first
    inside = (spot >= 0) & (spot < count_ref[0] // 4)

    def merge(number):
        columns = pl.ds(pl.multiple_of(number * 256, 256), 256)
        token = rows_ref[6:7, columns]
        for part in range(4):
            token = token + jnp.dot(
                merge_in[part], merge_w[pl.ds(part * VW, VW), columns], preferred_element_type=jnp.float32
            )
        return token.astype(jnp.bfloat16)

    for n in range(2):
        tok_give[n] = merge(2 * n + 1 - img)
        tok[me, n] = merge(2 * n + img)
        token_spread[n][0]()
    squares[...] = jnp.zeros_like(squares)
    total[...] = jnp.zeros_like(total)
    weight_one[5]()
    weight_two[5]()

    def weigh(chunk):
        token = jnp.concatenate([tok[chunk, 0], tok[chunk, 1]], axis=1)
        placed = jnp.dot(pick, token, preferred_element_type=jnp.float32)
        words = text[chunk // 2, :, :, pl.ds(pl.multiple_of((chunk % 2) * 512, 512), 512)]
        values = jnp.where(inside, placed, words.reshape(SECTION, 512).astype(jnp.float32))
        gains = [rows_ref[pl.ds(8 + chunk, 1), pl.ds(pl.multiple_of(512 * n + img * 256, 256), 256)] for n in range(2)]
        scaled = (values * jnp.concatenate(gains, axis=1)).astype(jnp.bfloat16)
        folded = jnp.zeros((SECTION, HEAD), jnp.float32)
        for number in range(4):
            piece = values[:, number * HEAD : (number + 1) * HEAD]
            folded = folded + piece * piece
        w = weight[chunk // 2, pl.ds((chunk % 2) * 2, 2)].reshape(512, 10 * HEAD)
        total[...] += jnp.dot(scaled, w, preferred_element_type=jnp.float32)
        squares[...] += folded

    text_spread[0][2]()
    text_spread[1][1]()
    token_spread[0][1]()
    token_spread[1][1]()
    text_spread[1][2]()
    weight_one[6]()
    weight_two[6]()

    def ours(number, carry):
        weigh(order((y + number) % 4, core))
        return carry

    def theirs(number, carry):
        weigh(order((y + number) % 4, 1 - core))
        return carry

    lax.fori_loop(0, 4, ours, 0)
    token_spread[0][2]()
    token_spread[1][2]()
    lax.fori_loop(0, 4, theirs, 0)

    def taken(side, size, start):
        return total[:, pl.ds(pl.multiple_of(start + side * size, HEAD), size)]

    part_out[:, : 4 * HEAD] = taken(1 - img, 4 * HEAD, 0).astype(jnp.bfloat16)
    part_out[:, 4 * HEAD :] = taken(1 - img, HEAD, 8 * HEAD).astype(jnp.bfloat16)
    sums[0] = jnp.sum(squares[...].T, axis=0, keepdims=True) + jnp.zeros((8, SECTION), jnp.float32)
    trade[0].start()
    trade[1].start()
    gather_one = grid_gather(
        copy, 90,
        lambda a, b: buf.at[img, a, b],
        lambda a, b, h: buf.at[img, a, b, pl.ds(HALF * h, HALF)],
        x, z, ways[0], ways[1],
    )
    gather_two = grid_gather(
        copy, 110,
        lambda a, b: buf.at[1 - img, b, a],
        lambda a, b, h: buf.at[1 - img, b, a, pl.ds(HALF * h, HALF)],
        z, x, ways[0][::-1], ways[1][::-1],
    )
    top[...] = jnp.full_like(top, MASKED)
    acc[...] = jnp.zeros_like(acc)
    trade[0].wait()
    mean = (sums[0, 0:1] + sums[1, 0:1]) * (1.0 / 8192)
    scale = (lax.rsqrt(mean + EPSILON) + jnp.zeros((HEAD, SECTION), jnp.float32)).T
    cosine = jnp.concatenate([cos_ref[...], cos_ref[...]], axis=1)
    sine = jnp.concatenate([-sin_ref[...], sin_ref[...]], axis=1)

    def settle(mine, number):
        columns = slice(HEAD * number, HEAD * number + HEAD)
        head = (mine + part_in[:, columns].astype(jnp.float32)) * scale + rows_ref[7:8, columns]
        return head, head * cosine + pltpu.roll(head, HEAD // 2, 1) * sine

    trade[1].wait()
    plain, turned = settle(taken(img, HEAD, 8 * HEAD), OWN_HEADS)
    columns = [turned[n * HEAD : (n + 1) * HEAD].T for n in range(SECTION // HEAD)]
    buf[img, x, z] = jnp.where(img == 0, jnp.concatenate(columns, axis=0), plain).astype(jnp.bfloat16)
    swap = copy(buf.at[img, x, z], buf.at[img, x, z], 88, other)
    swap.start()
    gather_one[0]()
    rows_all = 2 * SECTION
    ones = jnp.ones((SECTION, HEAD), jnp.bfloat16)
    tiles = SECTION // HEAD

    def block(group, number, masked):
        rows = pl.ds(pl.multiple_of(group * rows_all, rows_all), rows_all)
        a, b = number // 4, number % 4
        keys = jnp.concatenate([buf[0, a, b, n * HEAD : (n + 1) * HEAD] for n in range(tiles)], axis=1)
        values = jnp.concatenate([buf[1, a, b], ones], axis=1)
        scores = jnp.dot(query[rows, :], keys, preferred_element_type=jnp.float32)
        scores = scores * (HEAD ** (-0.5) * LOG2E)
        if masked:
            row = lax.broadcasted_iota(jnp.int32, (rows_all, SECTION), 0) % SECTION
            col = lax.broadcasted_iota(jnp.int32, (rows_all, SECTION), 1)
            scores = jnp.where(col <= row, scores, MASKED)
        old = top[rows, :]
        new = jnp.maximum(old, jnp.max(scores, axis=-1, keepdims=True))
        factor = jnp.exp2(old - new)
        weights = [jnp.exp2(scores[:, n * HEAD : (n + 1) * HEAD] - new) for n in range(tiles)]
        weights = jnp.concatenate(weights, axis=1).astype(jnp.bfloat16)
        product = jnp.dot(weights, values, preferred_element_type=jnp.float32)
        top[rows, :] = new
        acc[rows, :] = acc[rows, :] * jnp.concatenate([factor, factor], axis=1) + product

    def visit(group, dx, dz):
        number = ((x + dx) % 4) * 4 + (z + dz) % 4

        @pl.when(number < group * mirror + (1 - group) * seq)
        def _():
            block(group, number, False)

    def both(count, offset):
        def step(n, carry):
            visit(n % 2, *offset(n // 2))
            return carry

        lax.fori_loop(0, 2 * count, step, 0)

    def ending(group):
        def across(n, carry):
            visit(group, 2, n)
            return carry

        def along(n, carry):
            visit(group, n * (n + 1) // 2, 2)
            return carry

        lax.fori_loop(0, 4, across, 0)
        lax.fori_loop(0, 3, along, 0)

    def finish(group):
        parts = []
        for head in range(2):
            total = acc[pl.ds(group * rows_all + head * SECTION, SECTION), :]
            parts.append((total[:, :HEAD] / total[:, HEAD:]).astype(jnp.bfloat16))
        return jnp.concatenate(parts, axis=1)

    swap.wait()
    gather_two[0]()
    trade[2].start()
    gather_one[1]()
    gather_two[1]()
    gather_one[2]()
    gather_two[2]()
    trade[2].wait()
    heads = [settle(taken(img, 4 * HEAD, 0)[:, n * HEAD : n * HEAD + HEAD], n)[1].astype(jnp.bfloat16) for n in range(4)]
    for n in range(2):
        lent[:, n * HEAD : n * HEAD + HEAD] = heads[2 + n]
        query[pl.ds(n * SECTION, SECTION), :] = heads[n]
    lend = copy(lent, guest, 89, {"seq": mirror})
    lend.start()
    block(0, seq, True)
    gather_one[3]()
    gather_two[3]()
    gather_one[4]()
    gather_two[4]()
    lend.wait()
    for head in range(2):
        query[pl.ds(rows_all + head * SECTION, SECTION), :] = guest[:, head * HEAD : (head + 1) * HEAD]
    visit(1, 0, 0)
    both(2, lambda n: (1 + 2 * n, 0))
    gather_one[5]()
    gather_two[5]()
    block(1, mirror, True)
    both(2, lambda n: (0, 1 + 2 * n))
    both(4, lambda n: (1 + 2 * (n // 2), 1 + 2 * (n % 2)))
    gather_one[6]()
    gather_two[6]()
    ending(1)
    away[...] = finish(1)
    to_mirror = [
        remote(
            away.at[pl.ds(HALF * n, HALF)],
            out_ref.at[:, pl.ds(pl.multiple_of(img * 2 * two + two, two), two)],
            130 + n, 130 + img, {"seq": mirror, "img": n},
        )
        for n in range(2)
    ]
    for c in to_mirror:
        c.start()
    ending(0)
    home[...] = finish(0)
    columns = pl.ds(pl.multiple_of(img * 2 * two, two), two)
    back = copy(home.at[pl.ds(pl.multiple_of((1 - img) * HALF, HALF), HALF)], out_ref.at[:, columns], 132, other)
    back.start()
    out_ref[:, columns] = home[pl.ds(pl.multiple_of(img * HALF, HALF), HALF), :]
    for n in range(2):
        to_mirror[n].wait_send()
        remote(
            away.at[pl.ds(HALF * n, HALF)],
            out_ref.at[:, pl.ds(n * 2 * two + two, two)],
            130 + n, 130 + n, {"seq": mirror, "img": n},
        ).wait_recv()
    back.wait()


def encode(*operands):
    vmem = pl.BlockSpec(memory_space=pltpu.VMEM)
    hbm = pl.BlockSpec(memory_space=pl.ANY)
    smem = pl.BlockSpec(memory_space=pltpu.SMEM)
    bf16, f32 = jnp.bfloat16, jnp.float32
    return pl.pallas_call(
        vision_kernel,
        out_shape=jax.ShapeDtypeStruct((HALF, 2 * OWN_HEADS * HEAD), bf16),
        in_specs=[smem] * 2 + [vmem] * 14 + [hbm] * 3,
        out_specs=vmem,
        scratch_shapes=[
            pltpu.VMEM((16, VW), f32),
            pltpu.VMEM((VW, 6 * HEAD), bf16),
            pltpu.VMEM((PATCH_CAP, 6 * HEAD), bf16),
            pltpu.VMEM((2, HEAD, PATCH_CAP), bf16),
            pltpu.VMEM((PATCH_CAP, 2 * HEAD), bf16),
            pltpu.VMEM((8, 128, 2 * HEAD), bf16),
            pltpu.VMEM((8, 256, VW), bf16),
            pltpu.VMEM((4 * VW, 1024), bf16),
            pltpu.VMEM((VW // HEAD, 128, HEAD), f32),
            pltpu.VMEM((4, 256, VW), bf16),
            pltpu.VMEM((4, 4, 256, 10 * HEAD), bf16),
            pltpu.VMEM((256, 1024), bf16),
            pltpu.VMEM((4, 2, 256, 1024), bf16),
            pltpu.VMEM((2, 256, 256), bf16),
            pltpu.VMEM((8, 2, 256, 256), bf16),
            pltpu.VMEM((SECTION, 10 * HEAD), f32),
            pltpu.VMEM((SECTION, HEAD), f32),
            pltpu.VMEM((2, 8, SECTION), f32),
            pltpu.VMEM((SECTION, 5 * HEAD), bf16),
            pltpu.VMEM((SECTION, 5 * HEAD), bf16),
            pltpu.VMEM((2, 4, 4, SECTION, HEAD), bf16),
            pltpu.VMEM((SECTION, 2 * HEAD), bf16),
            pltpu.VMEM((4 * SECTION, HEAD), f32),
            pltpu.VMEM((4 * SECTION, 2 * HEAD), f32),
            pltpu.SemaphoreType.DMA((134,)),
            pltpu.SemaphoreType.DMA((134,)),
            pltpu.SemaphoreType.DMA((7,)),
            pltpu.SemaphoreType.DMA((8,)),
            pltpu.SemaphoreType.DMA((10,)),
        ],
        compiler_params=pltpu.CompilerParams(
            collective_id=1, has_side_effects=True, vmem_limit_bytes=62 * 1024 * 1024
        ),
    )(*operands)


def on_device(
    patches, patch_counts, image_offsets, vision_gain, vision_shift, vision_qkv, vision_qkv_bias,
    vision_proj, vision_proj_bias, merge_gain, merge_shift, merge_weight, merge_bias, text_embed,
    norm_gain, qkv_weight, qkv_bias,
):
    positions = lax.axis_index("seq") * SECTION + jnp.arange(SECTION, dtype=jnp.int32)
    cosine, sine = rotation(positions)
    return encode(
        patch_counts, image_offsets, patches[0], vision_gain, vision_shift, vision_proj_bias, merge_gain, merge_shift,
        vision_qkv_bias, merge_bias, norm_gain, qkv_bias, cosine, sine, vision_qkv.T, vision_proj, merge_weight,
        text_embed, qkv_weight,
    )


def solution(mesh):
    placed = (
        P("seq", None, None),
        P("seq"),
        P("seq"),
        P(),
        P(),
        P(None, ("tp", "img")),
        P(("tp", "img")),
        P(("tp", "img"), None),
        P(),
        P(),
        P(),
        P(None, ("tp", "img")),
        P(("tp", "img")),
        P(("seq", "img"), "tp"),
        P(),
        P(("seq", "img"), "tp"),
        P("tp"),
    )
    return jax.shard_map(
        on_device, mesh=mesh, in_specs=placed, out_specs=P(("seq", "img"), "tp"), check_vma=False
    )
```

```python
import functools

import jax
import jax.numpy as jnp
from jax import lax
from jax.experimental import pallas as pl
from jax.experimental.pallas import tpu as pltpu
from jax.sharding import PartitionSpec as P

HEAD = 128
VW = 1280
PATCH_CAP = 1024
GROUP = 8
VHEAD = 80
SECTION = 512
HALF = 256
OWN_HEADS = 4

EPSILON = 1e-06
THETA = 1000000.0
MASKED = -1e30
LOG2E = 1.4426950408889634
MESH = pl.DeviceIdType.MESH


def rotation(positions):
    halfway = HEAD // 2
    frequency = jnp.power(jnp.float32(THETA), -(jnp.arange(halfway, dtype=jnp.float32) * 2.0) / HEAD)
    angles = positions.astype(jnp.float32)[:, None] * frequency[None, :]
    return jnp.cos(angles), jnp.sin(angles)


def grid_gather(copy, base, block, part, first, second, ahead, behind):
    before, after, far = (first + 3) % 4, (first + 1) % 4, (first + 2) % 4
    low, high = (second + 3) % 4, (second + 1) % 4

    def whole(number, a, way):
        return copy(block(a, second), block(a, second), base + number, way)

    def half(number, a, b, h, way):
        return copy(part(a, b, h), part(a, b, h), base + number, way)

    up, down = whole(0, first, ahead[0]), whole(1, first, behind[0])
    pass_up = half(2, before, second, 0, ahead[0])
    pass_down = half(3, after, second, 1, behind[0])
    columns = (first, before, after, far)
    over = [(whole(4 + 2 * n, a, ahead[1]), whole(5 + 2 * n, a, behind[1])) for n, a in enumerate(columns)]
    on = [
        (half(12 + 2 * n, a, low, 0, ahead[1]), half(13 + 2 * n, a, high, 1, behind[1]))
        for n, a in enumerate(columns)
    ]

    def spread(n):
        over[n][0].start()
        over[n][1].start()

    def relay(n):
        over[n][0].wait_recv()
        on[n][0].start()
        over[n][1].wait_recv()
        on[n][1].start()

    def begin():
        up.start()
        down.start()
        spread(0)

    def turn():
        up.wait_recv()
        pass_up.start()
        spread(1)
        down.wait_recv()
        pass_down.start()
        spread(2)

    def near():
        relay(0)

    def turned():
        pass_up.wait_recv()
        pass_down.wait_recv()
        spread(3)

    def middle():
        relay(1)
        relay(2)

    def last():
        relay(3)

    def done():
        for c in on:
            c[0].wait_recv()
            c[1].wait_recv()
        for c in [(up, down), (pass_up, pass_down)] + over + on:
            c[0].wait_send()
            c[1].wait_send()

    return begin, turn, near, turned, middle, last, done


def column_gather(copy, base, slot, part, y, core, device):
    before, after, far = (y + 3) % 4, (y + 1) % 4, (y + 2) % 4
    ahead, behind, sibling = device(after, core), device(before, core), device(y, 1 - core)
    own = slot(y, core)
    share = copy(own, own, base, sibling)
    send_up = copy(own, own, base + 1, ahead)
    send_down = copy(own, own, base + 2, behind)
    low, high = part(before, core, 0), part(after, core, 1)
    pass_up = copy(low, low, base + 3, ahead)
    pass_down = copy(high, high, base + 4, behind)
    left, right = slot(before, core), slot(after, core)
    give_left = copy(left, left, base + 5, sibling)
    give_right = copy(right, right, base + 6, sibling)
    far_low, far_high = part(far, core, 0), part(far, core, 1)
    give_low = copy(far_low, far_low, base + 7, sibling)
    give_high = copy(far_high, far_high, base + 8, sibling)

    def start():
        send_up.start()
        send_down.start()
        share.start()

    def turn():
        send_up.wait_recv()
        pass_up.start()
        give_left.start()
        send_down.wait_recv()
        pass_down.start()
        give_right.start()

    def last():
        pass_up.wait_recv()
        give_low.start()
        pass_down.wait_recv()
        give_high.start()

    def done():
        for c in (share, give_left, give_right, give_low, give_high):
            c.wait_recv()
        for c in (share, send_up, send_down, pass_up, pass_down, give_left, give_right, give_low, give_high):
            c.wait_send()

    return start, turn, last, done


def plane_spread(copy, base, give, slot, y, core, device):
    mate = y + 1 - 2 * (y % 2)
    straight = (y + 2) % 4
    across = straight + 1 - 2 * (straight % 2)
    own, sibling = slot(y, core), device(y, 1 - core)

    def send(src, number, peer):
        return copy(src, own, base + number, peer)

    share, near = send(own, 0, sibling), send(own, 1, device(mate, core))
    far, close = send(give, 2, device(straight, core)), send(give, 3, device(across, core))
    relays = [copy(slot(a, core), slot(a, core), base + 4 + n, sibling) for n, a in enumerate((mate, across, straight))]

    def start():
        near.start()
        close.start()
        far.start()
        share.start()

    def turn():
        for c, relay in zip((near, close, far), relays):
            c.wait_recv()
            relay.start()

    def done():
        for c in [share] + relays:
            c.wait_recv()
        for c in [share, near, far, close] + relays:
            c.wait_send()

    return start, turn, done


def vision_kernel(
    count_ref, start_ref, patches_ref, gain_ref, shift_ref, proj_bias_ref, merge_gain_ref, merge_shift_ref,
    qkv_bias_ref, merge_bias_ref, norm_ref, bias_ref, cos_ref, sin_ref, qkv_ref, proj_ref, merge_ref, text_ref,
    part_ref, out_ref,
    rows_ref, wide, mixed, flipped, ctx, ctx_in, proj_all, merge_w, lines, merge_in, weight, text_give, text, tok_give, tok,
    total, squares, sums, part_out, part_in, buf, guest, top, acc,
    send, recv, ctx_send, ctx_recv, local,
):
    seq = lax.axis_index("seq")
    tp = lax.axis_index("tp")
    img = lax.axis_index("img")
    x, z = seq // 4, seq % 4
    core, y = tp % 2, img * 2 + tp // 2
    me = tp * 2 + img
    singles = (gain_ref, shift_ref, proj_bias_ref, merge_gain_ref, merge_shift_ref, qkv_bias_ref, merge_bias_ref)
    for n, ref in enumerate(singles):
        rows_ref[n : n + 1, : ref.shape[0]] = ref[...].astype(jnp.float32)[None, :]
    bias_row = bias_ref[...].astype(jnp.float32)[None, :]
    q_bias = jnp.where(img == 0, bias_row[:, : 4 * HEAD], bias_row[:, 4 * HEAD : 8 * HEAD])
    rows_ref[7:8, : 6 * HEAD] = jnp.concatenate([q_bias, bias_row[:, 8 * HEAD :]], axis=1)
    norm_row = norm_ref[...].astype(jnp.float32)[None, :]
    for n in range(8):
        rows_ref[8 + n : 9 + n, :1024] = norm_row[:, n * 1024 : (n + 1) * 1024]
    gain, shift, proj_bias, merge_gain, merge_shift = [rows_ref[n : n + 1, :] for n in range(5)]

    def device(y_at, core_at):
        return {"tp": 2 * (y_at % 2) + core_at, "img": y_at // 2}

    def order(y_at, core_at):
        return (2 * (y_at % 2) + core_at) * 2 + y_at // 2

    def along_x(d):
        return {"seq": ((x + d) % 4) * 4 + z}

    def along_z(d):
        return {"seq": x * 4 + (z + d) % 4}

    def member(index):
        return {"tp": index // 2, "img": index % 2}

    peers = [member((me + d) % 8) for d in range(1, 8)]
    mirror = 15 - seq
    peers += [along_x(1), along_x(3), along_z(1), along_z(3), {"seq": mirror}, {"seq": mirror, "img": 1 - img}]
    barrier = pltpu.get_barrier_semaphore()
    for peer in peers:
        pl.semaphore_signal(barrier, inc=1, device_id=peer, device_id_type=MESH)
    load_merge = pltpu.make_async_copy(merge_ref, merge_w, local.at[0])
    load_merge.start()
    load_weight = pltpu.make_async_copy(part_ref, weight.at[x, z], local.at[1])
    load_weight.start()
    load_text = []
    for n in range(4):
        columns = pl.ds(256 * n, 256)
        for parity, target in ((1 - img, text_give.at[:, columns]), (img, text.at[tp, img, :, columns])):
            at = pl.ds(pl.multiple_of((2 * n + parity) * 256, 256), 256)
            load_text.append(pltpu.make_async_copy(text_ref.at[:, at], target, local.at[2 + len(load_text)]))
    for c in load_text:
        c.start()
    proj_all[:, 2 * VHEAD :, :] = jnp.zeros((8, 256 - 2 * VHEAD, VW), jnp.bfloat16)
    proj_all[me, : 2 * VHEAD, :] = proj_ref[...]
    pl.semaphore_wait(barrier, len(peers))

    def remote(src, dst, out, into, peer):
        return pltpu.make_async_remote_copy(
            src_ref=src,
            dst_ref=dst,
            send_sem=send.at[out],
            recv_sem=recv.at[into],
            device_id=peer,
            device_id_type=MESH,
        )

    def copy(src, dst, number, peer):
        return remote(src, dst, number, number, peer)

    proj_gather = column_gather(
        copy, 0,
        lambda a, b: proj_all.at[order(a, b), pl.ds(0, 160)],
        lambda a, b, h: proj_all.at[order(a, b), pl.ds(80 * h, 80)],
        y, core, device,
    )
    merge_gather = column_gather(
        copy, 9,
        lambda a, b: merge_in.at[:, pl.ds(order(a, b) * 32, 32)],
        lambda a, b, h: merge_in.at[pl.ds(2 * h, 2), pl.ds(order(a, b) * 32, 32)],
        y, core, device,
    )
    text_spread = [
        plane_spread(
            copy, 18 + 7 * n, text_give.at[pl.ds(128 * n, 128)],
            lambda a, b, n=n: text.at[2 * (a % 2) + b, a // 2, pl.ds(128 * n, 128)],
            y, core, device,
        )
        for n in range(2)
    ]
    token_spread = [
        plane_spread(copy, 32 + 7 * n, tok_give.at[n], lambda a, b, n=n: tok.at[order(a, b), n], y, core, device)
        for n in range(2)
    ]
    other = {"img": 1 - img}
    quarter, fifth = pl.ds(0, 4 * HEAD), pl.ds(4 * HEAD, 2 * HEAD)
    trade = [
        copy(sums.at[0], sums.at[1], 47, other),
        copy(part_out.at[:, fifth], part_in.at[:, fifth], 46, other),
        copy(part_out.at[:, quarter], part_in.at[:, quarter], 133, other),
    ]
    two = 2 * HEAD
    query = merge_w.at[pl.ds(0, 4 * SECTION), pl.ds(0, HEAD)]
    lent = merge_w.at[pl.ds(0, SECTION), pl.ds(HEAD, two)]
    away = merge_w.at[pl.ds(0, SECTION), pl.ds(HEAD + two, two)]
    home = merge_w.at[pl.ds(0, SECTION), pl.ds(HEAD + 2 * two, two)]
    ways = (along_x(1), along_z(1)), (along_x(3), along_z(3))
    weight_one = grid_gather(
        copy, 48,
        lambda a, b: weight.at[a, b, pl.ds(0, 128)],
        lambda a, b, h: weight.at[a, b, pl.ds(64 * h, 64)],
        x, z, ways[0], ways[1],
    )
    weight_two = grid_gather(
        copy, 68,
        lambda a, b: weight.at[b, a, pl.ds(128, 128)],
        lambda a, b, h: weight.at[b, a, pl.ds(128 + 64 * h, 64)],
        z, x, ways[0][::-1], ways[1][::-1],
    )

    proj_gather[0]()
    load_weight.wait()
    weight_one[0]()
    weight_two[0]()

    def norm(source, scaling, shifting):
        average = jnp.mean(source, axis=-1, keepdims=True)
        centred = source - average
        spread = jnp.mean(centred * centred, axis=-1, keepdims=True)
        return centred * lax.rsqrt(spread + EPSILON) * scaling + shifting

    old = lax.broadcasted_iota(jnp.int32, (6 * VHEAD, 6 * HEAD), 0)
    new = lax.broadcasted_iota(jnp.int32, (6 * VHEAD, 6 * HEAD), 1)
    place = ((old // VHEAD == new // HEAD) & (old % VHEAD == new % HEAD)).astype(jnp.float32).astype(jnp.bfloat16)
    wide[...] = lax.dot_general(
        qkv_ref[...], place, (((0,), (0,)), ((), ())), preferred_element_type=jnp.float32
    ).astype(jnp.bfloat16)
    bias = jnp.dot(
        rows_ref[5:6, : 6 * VHEAD].astype(jnp.bfloat16), place, preferred_element_type=jnp.float32
    )
    column = lax.broadcasted_iota(jnp.int32, (1, 6 * HEAD), 1)
    bias = bias + ((column % HEAD == VHEAD) & ((column // HEAD) % 3 == 2)).astype(jnp.float32)

    def mix(number, carry):
        rows = pl.ds(pl.multiple_of(number * 512, 512), 512)
        normed = norm(patches_ref[rows, :].astype(jnp.float32), gain, shift)
        product = jnp.dot(normed.astype(jnp.bfloat16), wide[...], preferred_element_type=jnp.float32) + bias
        mixed[rows, :] = product.astype(jnp.bfloat16)
        for head in range(2):
            keys = product[:, 384 * head + 128 : 384 * head + 256].T
            flipped[head, :, rows] = keys.astype(jnp.bfloat16)
        return carry

    lax.fori_loop(0, 2, mix, 0)
    for c in load_text:
        c.wait()
    valid = lax.broadcasted_iota(jnp.int32, (512, PATCH_CAP), 1) < count_ref[0]
    lane = lax.broadcasted_iota(jnp.int32, (512, HEAD), 1)

    def look(number):
        rows = pl.ds(pl.multiple_of(number * 512, 512), 512)
        parts = []
        for head in range(2):
            query = mixed[rows, 384 * head : 384 * head + 128]
            values = mixed[:, 384 * head + 256 : 384 * head + 384]
            scores = jnp.dot(query, flipped[head], preferred_element_type=jnp.float32)
            scores = jnp.where(valid, scores * (VHEAD ** (-0.5) * LOG2E), MASKED)
            best = jnp.max(scores, axis=-1, keepdims=True) + jnp.zeros((512, HEAD), jnp.float32)
            weights = [jnp.exp2(scores[:, n * HEAD : (n + 1) * HEAD] - best) for n in range(8)]
            weights = jnp.concatenate(weights, axis=1).astype(jnp.bfloat16)
            product = jnp.dot(weights, values, preferred_element_type=jnp.float32)
            parts.append(product / product[:, VHEAD : VHEAD + 1])
        turned = pltpu.roll(parts[1], VHEAD, 1)
        ctx[rows, :HEAD] = jnp.where(lane < VHEAD, parts[0], turned).astype(jnp.bfloat16)
        ctx[rows, HEAD:] = jnp.where(lane < 2 * VHEAD - HEAD, turned, 0.0).astype(jnp.bfloat16)

    def ctx_copy(number, target):
        return pltpu.make_async_remote_copy(
            src_ref=ctx.at[pl.ds(pl.multiple_of(target * 128, 128), 128)],
            dst_ref=ctx_in.at[me],
            send_sem=ctx_send.at[number],
            recv_sem=ctx_recv.at[me],
            device_id=member(target),
            device_id_type=MESH,
        )

    side = me // 4
    look(1 - side)
    for n in range(4):
        ctx_copy(n, (1 - side) * 4 + n).start()
    proj_gather[1]()
    look(side)
    for n in range(3):
        ctx_copy(4 + n, side * 4 + (me + 1 + n) % 4).start()
    ctx_in[me] = ctx[pl.ds(pl.multiple_of(me * 128, 128), 128), :]
    proj_gather[2]()
    weight_one[1]()
    weight_two[1]()
    weight_one[2]()
    weight_two[2]()

    def arrived(number, carry):
        source = (me + 1 + number) % 8
        pltpu.make_async_remote_copy(
            src_ref=ctx.at[pl.ds(0, 128)],
            dst_ref=ctx_in.at[source],
            send_sem=ctx_send.at[number],
            recv_sem=ctx_recv.at[source],
            device_id=member(source),
            device_id_type=MESH,
        ).wait()
        return carry

    lax.fori_loop(0, 7, arrived, 0)
    text_spread[0][0]()
    proj_gather[3]()
    weight_one[3]()
    weight_two[3]()
    resid = patches_ref[pl.ds(me * 128, 128), :].astype(jnp.float32) + proj_bias
    for number in range(8):
        resid = resid + jnp.dot(ctx_in[number], proj_all[number], preferred_element_type=jnp.float32)
    settled = norm(resid, merge_gain, merge_shift)
    for tile in range(VW // HEAD):
        lines[tile] = settled[:, tile * HEAD : (tile + 1) * HEAD]
    for number in range(4):
        picked = [lines[tile, pl.ds(number, 32, stride=4), :] for tile in range(VW // HEAD)]
        merge_in[number, pl.ds(me * 32, 32), :] = jnp.concatenate(picked, axis=1).astype(jnp.bfloat16)
    merge_gather[0]()
    load_merge.wait()
    merge_gather[1]()
    weight_one[4]()
    weight_two[4]()
    merge_gather[2]()
    text_spread[0][1]()
    text_spread[1][0]()
    first = start_ref[0] - seq * SECTION
    spot = lax.broadcasted_iota(jnp.int32, (SECTION, 256), 0) - first
    slot = lax.broadcasted_iota(jnp.int32, (SECTION, 256), 1)
    pick = ((spot == slot) & (slot < count_ref[0] // 4)).astype(jnp.float32).astype(jnp.bfloat16)
    merge_gather[3]()
    spot = lax.broadcasted_iota(jnp.int32, (SECTION, 512), 0) - first
    inside = (spot >= 0) & (spot < count_ref[0] // 4)

    def merge(number):
        columns = pl.ds(pl.multiple_of(number * 256, 256), 256)
        token = rows_ref[6:7, columns]
        for part in range(4):
            token = token + jnp.dot(
                merge_in[part], merge_w[pl.ds(part * VW, VW), columns], preferred_element_type=jnp.float32
            )
        return token.astype(jnp.bfloat16)

    for n in range(2):
        tok_give[n] = merge(2 * n + 1 - img)
        tok[me, n] = merge(2 * n + img)
        token_spread[n][0]()
    squares[...] = jnp.zeros_like(squares)
    total[...] = jnp.zeros_like(total)
    weight_one[5]()
    weight_two[5]()

    def weigh(chunk):
        token = jnp.concatenate([tok[chunk, 0], tok[chunk, 1]], axis=1)
        placed = jnp.dot(pick, token, preferred_element_type=jnp.float32)
        words = text[chunk // 2, :, :, pl.ds(pl.multiple_of((chunk % 2) * 512, 512), 512)]
        values = jnp.where(inside, placed, words.reshape(SECTION, 512).astype(jnp.float32))
        gains = [rows_ref[pl.ds(8 + chunk, 1), pl.ds(pl.multiple_of(512 * n + img * 256, 256), 256)] for n in range(2)]
        scaled = (values * jnp.concatenate(gains, axis=1)).astype(jnp.bfloat16)
        folded = jnp.zeros((SECTION, HEAD), jnp.float32)
        for number in range(4):
            piece = values[:, number * HEAD : (number + 1) * HEAD]
            folded = folded + piece * piece
        w = weight[chunk // 2, pl.ds((chunk % 2) * 2, 2)].reshape(512, 10 * HEAD)
        total[...] += jnp.dot(scaled, w, preferred_element_type=jnp.float32)
        squares[...] += folded

    text_spread[0][2]()
    text_spread[1][1]()
    token_spread[0][1]()
    token_spread[1][1]()
    text_spread[1][2]()
    weight_one[6]()
    weight_two[6]()

    def ours(number, carry):
        weigh(order((y + number) % 4, core))
        return carry

    def theirs(number, carry):
        weigh(order((y + number) % 4, 1 - core))
        return carry

    lax.fori_loop(0, 4, ours, 0)
    token_spread[0][2]()
    token_spread[1][2]()
    lax.fori_loop(0, 4, theirs, 0)

    def taken(side, size, start):
        return total[:, pl.ds(pl.multiple_of(start + side * size, HEAD), size)]

    part_out[:, : 4 * HEAD] = taken(1 - img, 4 * HEAD, 0).astype(jnp.bfloat16)
    part_out[:, 4 * HEAD :] = total[:, 8 * HEAD :].astype(jnp.bfloat16)
    sums[0] = jnp.sum(squares[...].T, axis=0, keepdims=True) + jnp.zeros((8, SECTION), jnp.float32)
    trade[0].start()
    trade[1].start()
    gather_one = grid_gather(
        copy, 90,
        lambda a, b: buf.at[img, a, b],
        lambda a, b, h: buf.at[img, a, b, pl.ds(HALF * h, HALF)],
        x, z, ways[0], ways[1],
    )
    gather_two = grid_gather(
        copy, 110,
        lambda a, b: buf.at[1 - img, b, a],
        lambda a, b, h: buf.at[1 - img, b, a, pl.ds(HALF * h, HALF)],
        z, x, ways[0][::-1], ways[1][::-1],
    )
    top[...] = jnp.full_like(top, MASKED)
    acc[...] = jnp.zeros_like(acc)
    trade[0].wait()
    mean = (sums[0, 0:1] + sums[1, 0:1]) * (1.0 / 8192)
    scale = (lax.rsqrt(mean + EPSILON) + jnp.zeros((HEAD, SECTION), jnp.float32)).T
    cosine = jnp.concatenate([cos_ref[...], cos_ref[...]], axis=1)
    sine = jnp.concatenate([-sin_ref[...], sin_ref[...]], axis=1)

    def settle(mine, number):
        columns = slice(HEAD * number, HEAD * number + HEAD)
        head = (mine + part_in[:, columns].astype(jnp.float32)) * scale + rows_ref[7:8, columns]
        return head, head * cosine + pltpu.roll(head, HEAD // 2, 1) * sine

    trade[1].wait()
    turned = settle(total[:, 8 * HEAD : 9 * HEAD], OWN_HEADS)[1]
    columns = [turned[n * HEAD : (n + 1) * HEAD].T for n in range(SECTION // HEAD)]
    buf[0, x, z] = jnp.concatenate(columns, axis=0).astype(jnp.bfloat16)
    buf[1, x, z] = settle(total[:, 9 * HEAD :], OWN_HEADS + 1)[0].astype(jnp.bfloat16)
    gather_one[0]()
    rows_all = 2 * SECTION
    ones = jnp.ones((SECTION, HEAD), jnp.bfloat16)
    tiles = SECTION // HEAD

    def block(group, number, masked):
        rows = pl.ds(pl.multiple_of(group * rows_all, rows_all), rows_all)
        a, b = number // 4, number % 4
        keys = jnp.concatenate([buf[0, a, b, n * HEAD : (n + 1) * HEAD] for n in range(tiles)], axis=1)
        values = jnp.concatenate([buf[1, a, b], ones], axis=1)
        scores = jnp.dot(query[rows, :], keys, preferred_element_type=jnp.float32)
        scores = scores * (HEAD ** (-0.5) * LOG2E)
        if masked:
            row = lax.broadcasted_iota(jnp.int32, (rows_all, SECTION), 0) % SECTION
            col = lax.broadcasted_iota(jnp.int32, (rows_all, SECTION), 1)
            scores = jnp.where(col <= row, scores, MASKED)
        old = top[rows, :]
        new = jnp.maximum(old, jnp.max(scores, axis=-1, keepdims=True))
        factor = jnp.exp2(old - new)
        weights = [jnp.exp2(scores[:, n * HEAD : (n + 1) * HEAD] - new) for n in range(tiles)]
        weights = jnp.concatenate(weights, axis=1).astype(jnp.bfloat16)
        product = jnp.dot(weights, values, preferred_element_type=jnp.float32)
        top[rows, :] = new
        acc[rows, :] = acc[rows, :] * jnp.concatenate([factor, factor], axis=1) + product

    def visit(group, dx, dz):
        number = ((x + dx) % 4) * 4 + (z + dz) % 4

        @pl.when(number < group * mirror + (1 - group) * seq)
        def _():
            block(group, number, False)

    def both(count, offset):
        def step(n, carry):
            visit(n % 2, *offset(n // 2))
            return carry

        lax.fori_loop(0, 2 * count, step, 0)

    def ending(group):
        def across(n, carry):
            visit(group, 2, n)
            return carry

        def along(n, carry):
            visit(group, n * (n + 1) // 2, 2)
            return carry

        lax.fori_loop(0, 4, across, 0)
        lax.fori_loop(0, 3, along, 0)

    def finish(group):
        parts = []
        for head in range(2):
            total = acc[pl.ds(group * rows_all + head * SECTION, SECTION), :]
            parts.append((total[:, :HEAD] / total[:, HEAD:]).astype(jnp.bfloat16))
        return jnp.concatenate(parts, axis=1)

    gather_two[0]()
    trade[2].start()
    gather_one[1]()
    gather_two[1]()
    gather_one[2]()
    gather_two[2]()
    trade[2].wait()
    heads = [settle(taken(img, 4 * HEAD, 0)[:, n * HEAD : n * HEAD + HEAD], n)[1].astype(jnp.bfloat16) for n in range(4)]
    for n in range(2):
        lent[:, n * HEAD : n * HEAD + HEAD] = heads[2 + n]
        query[pl.ds(n * SECTION, SECTION), :] = heads[n]
    lend = copy(lent, guest, 89, {"seq": mirror})
    lend.start()
    block(0, seq, True)
    gather_one[3]()
    gather_two[3]()
    gather_one[4]()
    gather_two[4]()
    lend.wait()
    for head in range(2):
        query[pl.ds(rows_all + head * SECTION, SECTION), :] = guest[:, head * HEAD : (head + 1) * HEAD]
    visit(1, 0, 0)
    both(2, lambda n: (1 + 2 * n, 0))
    gather_one[5]()
    gather_two[5]()
    block(1, mirror, True)
    both(2, lambda n: (0, 1 + 2 * n))
    both(4, lambda n: (1 + 2 * (n // 2), 1 + 2 * (n % 2)))
    gather_one[6]()
    gather_two[6]()
    ending(1)
    away[...] = finish(1)
    to_mirror = [
        remote(
            away.at[pl.ds(HALF * n, HALF)],
            out_ref.at[:, pl.ds(pl.multiple_of(img * 2 * two + two, two), two)],
            130 + n, 130 + img, {"seq": mirror, "img": n},
        )
        for n in range(2)
    ]
    for c in to_mirror:
        c.start()
    ending(0)
    home[...] = finish(0)
    columns = pl.ds(pl.multiple_of(img * 2 * two, two), two)
    back = copy(home.at[pl.ds(pl.multiple_of((1 - img) * HALF, HALF), HALF)], out_ref.at[:, columns], 132, other)
    back.start()
    out_ref[:, columns] = home[pl.ds(pl.multiple_of(img * HALF, HALF), HALF), :]
    for n in range(2):
        to_mirror[n].wait_send()
        remote(
            away.at[pl.ds(HALF * n, HALF)],
            out_ref.at[:, pl.ds(n * 2 * two + two, two)],
            130 + n, 130 + n, {"seq": mirror, "img": n},
        ).wait_recv()
    back.wait()


def encode(*operands):
    vmem = pl.BlockSpec(memory_space=pltpu.VMEM)
    hbm = pl.BlockSpec(memory_space=pl.ANY)
    smem = pl.BlockSpec(memory_space=pltpu.SMEM)
    bf16, f32 = jnp.bfloat16, jnp.float32
    return pl.pallas_call(
        vision_kernel,
        out_shape=jax.ShapeDtypeStruct((HALF, 2 * OWN_HEADS * HEAD), bf16),
        in_specs=[smem] * 2 + [vmem] * 14 + [hbm] * 3,
        out_specs=vmem,
        scratch_shapes=[
            pltpu.VMEM((16, VW), f32),
            pltpu.VMEM((VW, 6 * HEAD), bf16),
            pltpu.VMEM((PATCH_CAP, 6 * HEAD), bf16),
            pltpu.VMEM((2, HEAD, PATCH_CAP), bf16),
            pltpu.VMEM((PATCH_CAP, 2 * HEAD), bf16),
            pltpu.VMEM((8, 128, 2 * HEAD), bf16),
            pltpu.VMEM((8, 256, VW), bf16),
            pltpu.VMEM((4 * VW, 1024), bf16),
            pltpu.VMEM((VW // HEAD, 128, HEAD), f32),
            pltpu.VMEM((4, 256, VW), bf16),
            pltpu.VMEM((4, 4, 256, 10 * HEAD), bf16),
            pltpu.VMEM((256, 1024), bf16),
            pltpu.VMEM((4, 2, 256, 1024), bf16),
            pltpu.VMEM((2, 256, 256), bf16),
            pltpu.VMEM((8, 2, 256, 256), bf16),
            pltpu.VMEM((SECTION, 10 * HEAD), f32),
            pltpu.VMEM((SECTION, HEAD), f32),
            pltpu.VMEM((2, 8, SECTION), f32),
            pltpu.VMEM((SECTION, 6 * HEAD), bf16),
            pltpu.VMEM((SECTION, 6 * HEAD), bf16),
            pltpu.VMEM((2, 4, 4, SECTION, HEAD), bf16),
            pltpu.VMEM((SECTION, 2 * HEAD), bf16),
            pltpu.VMEM((4 * SECTION, HEAD), f32),
            pltpu.VMEM((4 * SECTION, 2 * HEAD), f32),
            pltpu.SemaphoreType.DMA((134,)),
            pltpu.SemaphoreType.DMA((134,)),
            pltpu.SemaphoreType.DMA((7,)),
            pltpu.SemaphoreType.DMA((8,)),
            pltpu.SemaphoreType.DMA((10,)),
        ],
        compiler_params=pltpu.CompilerParams(
            collective_id=1, has_side_effects=True, vmem_limit_bytes=62 * 1024 * 1024
        ),
    )(*operands)


def on_device(
    patches, patch_counts, image_offsets, vision_gain, vision_shift, vision_qkv, vision_qkv_bias,
    vision_proj, vision_proj_bias, merge_gain, merge_shift, merge_weight, merge_bias, text_embed,
    norm_gain, qkv_weight, qkv_bias,
):
    positions = lax.axis_index("seq") * SECTION + jnp.arange(SECTION, dtype=jnp.int32)
    cosine, sine = rotation(positions)
    return encode(
        patch_counts, image_offsets, patches[0], vision_gain, vision_shift, vision_proj_bias, merge_gain, merge_shift,
        vision_qkv_bias, merge_bias, norm_gain, qkv_bias, cosine, sine, vision_qkv.T, vision_proj, merge_weight,
        text_embed, qkv_weight,
    )


def solution(mesh):
    placed = (
        P("seq", None, None),
        P("seq"),
        P("seq"),
        P(),
        P(),
        P(None, ("tp", "img")),
        P(("tp", "img")),
        P(("tp", "img"), None),
        P(),
        P(),
        P(),
        P(None, ("tp", "img")),
        P(("tp", "img")),
        P(("seq", "img"), "tp"),
        P(),
        P(("seq", "img"), "tp"),
        P("tp"),
    )
    return jax.shard_map(
        on_device, mesh=mesh, in_specs=placed, out_specs=P(("seq", "img"), "tp"), check_vma=False
    )
```
